256 devices in a mesh: segment: 8 (over x, core), adapter: 32 (over y, z).
Axes of the slice: x: 4, y: 4, z: 8, core: 2. Of those that a mesh axis runs over, the one named last changes fastest.
Arguments:
- tokens: bfloat16 [2, 64, 8192], P(None, 'adapter'), may hold values from -6 to 6
- adapter_ids: int32 [2, 64, 1], P(None, 'adapter'), may hold values from 0 to 63
- ranks: int32 [64], P('adapter'), may hold values from 16 to 64, as said below
- gain: float32 [8, 8192], P('segment'), may hold values from 0.1 to 1.9
- base_weight: bfloat16 [8, 8192, 8192], P('segment', None, 'adapter'), may hold values from -0.0625 to 0.0625
- shrink_weight: bfloat16 [8, 64, 8192, 64], P('segment', 'adapter'), may hold values from -0.0625 to 0.0625
- expand_weight: bfloat16 [8, 64, 64, 8192], P('segment', None, None, 'adapter'), may hold values from -0.75 to 0.75
Outputs:
- layer_states: bfloat16 [8, 2, 64, 8192], P('segment', None, None, 'adapter')
The draws below stay inside these ranges and needn't reach their ends.
Inputs may be any that keep to these rules, and one draw needn't show every extreme that they name: `adapter_ids`: adapter a of a request is held on adapter index a // 2. `ranks`: each rank is a multiple of 16.
All inputs are finite; a program needn't handle non-finite values.
Results may differ from the reference program's by a relative error of at most 0.02.
Values may be sent and summed in bfloat16 or wider, within the bound.
No kernel may reach another device: no remote copies, remote signals or barrier semaphores. Data moves between devices by JAX's collectives and lax.ppermute only.
A program may use at most 64 MiB of HBM per device.

```python
import jax
import jax.numpy as jnp
from jax import lax

D = 8192
RMAX = 64
MICRO = 2
LAYERS = 8
ADAPTERS = 64
REQS = 64


def draw_ranks(key, part):
    key = jax.random.fold_in(key, 7)
    first_key, second_key = jax.random.split(key)
    levels = jax.random.randint(first_key, (ADAPTERS,), 1, 5)
    chosen = jax.random.permutation(second_key, ADAPTERS)
    levels = levels.at[chosen[0]].set(4)
    levels = levels.at[chosen[1]].set(1)
    return (levels * (RMAX // 4)).astype(jnp.int32)


def block_scale(rng, dims, pieces, smallest, high):
    level, own = 1.0, jax.random.fold_in(rng, 6)
    for dim, blocks in pieces:
        steps = jnp.exp(jax.random.uniform(jax.random.fold_in(own, dim), (blocks,), jnp.float32, smallest / len(pieces), high / len(pieces)))
        level = level * jnp.repeat(steps, dims[dim] // blocks).reshape([-1 if axis == dim else 1 for axis in range(len(dims))])
    return level


def choose_distinct(own_key, rows, number_of, top, lift):
    ranking = jax.random.permutation(jax.random.fold_in(own_key, 1), number_of)
    favour = ranking
    for power in range(3):
        favour = favour * favour // number_of
    favour = favour * lift // number_of
    tickets = jax.random.randint(jax.random.fold_in(own_key, 2), (rows, number_of), 0, 4096) + favour
    sure = jax.random.permutation(jax.random.fold_in(own_key, 3), rows)[jnp.arange(number_of) % rows]
    tickets = jnp.where(jnp.arange(rows)[:, None] == sure[None, :], 1 << 14, tickets)
    priority = tickets * number_of + jnp.arange(number_of)
    return lax.top_k(priority.astype(jnp.int32), top)[1].astype(jnp.int32)


def normal_values(own_key, extent, spread, reach, cuts=(), kind=jnp.bfloat16):
    drawn = spread * jax.random.normal(own_key, extent, jnp.float32)
    if cuts:
        drawn = drawn * block_scale(own_key, extent, cuts, -0.22, 0.18)
    return jnp.clip(drawn, -reach, reach).astype(kind)


def setup_inputs(seed: int = 0) -> dict:
    key_list = jax.random.split(jax.random.key(seed), 8)
    tokens = normal_values(key_list[0], (MICRO, REQS, D), 1.0, 6.0, ((1, 32),))
    adapter_ids = choose_distinct(key_list[1], MICRO * REQS, ADAPTERS, 1, 256).reshape((MICRO, REQS, 1))
    ranks = draw_ranks(jax.random.fold_in(key_list[7], 71), 0)
    gain = jnp.clip(1.0 + 0.18 * jax.random.normal(key_list[3], (LAYERS, D), jnp.float32), 0.1, 1.9)
    base_weight = normal_values(key_list[4], (LAYERS, D, D), D ** -0.5, 0.0625, ((0, 8), (2, 32)))
    shrink_weight = normal_values(key_list[5], (LAYERS, ADAPTERS, D, RMAX), D ** -0.5, 0.0625, ((0, 8), (1, 32)))
    expand_weight = normal_values(key_list[6], (LAYERS, ADAPTERS, RMAX, D), RMAX ** -0.5, 0.75, ((0, 8), (3, 32)))
    return {"tokens": tokens, "adapter_ids": adapter_ids, "ranks": ranks, "gain": gain, "base_weight": base_weight, "shrink_weight": shrink_weight, "expand_weight": expand_weight}


def rms_normed(hidden, gain_row):
    as_float = hidden.astype(jnp.float32)
    mean_square = lax.optimization_barrier(jnp.mean(as_float * as_float, axis=-1, keepdims=True))
    return (as_float * lax.rsqrt(mean_square + 1e-05) * gain_row).astype(jnp.bfloat16)

def reference(tokens, adapter_ids, ranks, gain, base_weight, shrink_weight, expand_weight):
    rank_float = ranks.astype(jnp.float32)
    column_keep = (jnp.arange(RMAX)[None, :] < ranks[:, None]).astype(jnp.float32)
    factor_table = column_keep * (32.0 / rank_float)[:, None]
    states = []
    for layer_index in range(LAYERS):
        states.append([])
    for micro_index in range(MICRO):
        hidden = tokens[micro_index]
        adapters_per_row = adapter_ids[micro_index, :, 0].astype(jnp.int32)
        for layer_index in range(LAYERS):
            normalized_hidden = rms_normed(hidden, gain[layer_index])
            base_contribution = jnp.dot(normalized_hidden, base_weight[layer_index], preferred_element_type=jnp.float32)
            shrink_layer = shrink_weight[layer_index]
            expand_layer = expand_weight[layer_index]

            def row_adapter_delta(adapter_pairing):
                normed_row, adapter = adapter_pairing
                low_float = jnp.dot(normed_row[None, :], shrink_layer[adapter], preferred_element_type=jnp.float32)[0]
                low_rank = (low_float * factor_table[adapter]).astype(jnp.bfloat16)
                return jnp.dot(low_rank[None, :], expand_layer[adapter], preferred_element_type=jnp.float32)[0]
            adapter_contribution = lax.map(row_adapter_delta, (normalized_hidden, adapters_per_row))
            hidden_update = (base_contribution + adapter_contribution).astype(jnp.bfloat16)
            hidden = (hidden.astype(jnp.float32) + hidden_update.astype(jnp.float32)).astype(jnp.bfloat16)
            states[layer_index].append(hidden)
    return jnp.stack([jnp.stack(layer_list, axis=0) for layer_list in states], axis=0)
```

```python
import jax
import jax.numpy as jnp
from jax import lax
from jax.experimental import pallas as pl
from jax.experimental.pallas import tpu as pltpu
from jax.sharding import PartitionSpec as P

GROUP = 4


def lane_group(shape, rank_most):
    return lax.broadcasted_iota(jnp.int32, shape, len(shape) - 1) // rank_most


def spread(value, rank_most):
    step = rank_most
    while step < value.shape[-1]:
        value = value + pltpu.roll(value, step, 1)
        step *= 2
    return value


def before_kernel(rank_most, h_ref, ids_ref, shrink_ref, out_ref):
    rows, cols = h_ref.shape
    packed = rows // GROUP
    h = h_ref[...]
    groups = lane_group((rows, cols), rank_most)
    wanted = ids_ref[...] - groups
    total = jnp.zeros((rows, cols), jnp.float32)
    for j in range(shrink_ref.shape[0] // cols):
        part = lax.dot_general(
            h,
            shrink_ref[j * cols : (j + 1) * cols, :],
            (((1,), (1,)), ((), ())),
            preferred_element_type=jnp.float32,
        )
        total = total + jnp.where(wanted == j * GROUP, part, 0.0)
    total = spread(total, rank_most)
    folded = jnp.zeros((packed, cols), jnp.float32)
    for g in range(GROUP):
        mine = groups[:packed] == g
        folded = jnp.where(mine, total[g * packed : (g + 1) * packed], folded)
    folded = folded.astype(jnp.bfloat16)
    for d in range(out_ref.shape[0]):
        out_ref[d, :rows, :] = h
        out_ref[d, rows:, :] = folded


def after_kernel(rank_most, h_ref, got_ref, ids_ref, rank_ref, base_ref, expand_ref, out_ref):
    rows, cols = h_ref.shape
    packed = rows // GROUP
    sources = got_ref.shape[0]
    groups = lane_group((rows, cols), rank_most)
    base = jnp.zeros((rows, cols), jnp.float32)
    squares = jnp.zeros((rows, cols), jnp.float32)
    partial = jnp.zeros((packed, cols), jnp.float32)
    for j in range(sources):
        block = got_ref[j, :rows, :]
        base = base + jnp.dot(
            block, base_ref[j * cols : (j + 1) * cols, :], preferred_element_type=jnp.float32
        )
        wide = block.astype(jnp.float32)
        squares = squares + wide * wide
        partial = partial + got_ref[j, rows:, :].astype(jnp.float32)
    mean_square = jnp.sum(squares, axis=-1, keepdims=True) / (sources * cols)
    inverse = lax.rsqrt(mean_square + 1e-05)
    low = jnp.concatenate(
        [
            spread(jnp.where(groups[:packed] == g, partial, 0.0), rank_most)
            for g in range(GROUP)
        ],
        axis=0,
    )
    rank = rank_ref[...]
    place = lax.broadcasted_iota(jnp.int32, (rows, cols), 1) - groups * rank_most
    factor = jnp.where(place.astype(jnp.float32) < rank, 32.0 / rank, 0.0)
    low = low * inverse * factor
    wanted = ids_ref[...] - groups
    added = jnp.zeros((rows, cols), jnp.float32)
    for j in range(expand_ref.shape[0] // cols):
        picked = jnp.where(wanted == j * GROUP, low, 0.0).astype(jnp.bfloat16)
        added = added + jnp.dot(
            picked, expand_ref[j * cols : (j + 1) * cols, :], preferred_element_type=jnp.float32
        )
    update = (base * inverse + added).astype(jnp.bfloat16)
    out_ref[...] = (h_ref[...].astype(jnp.float32) + update.astype(jnp.float32)).astype(
        jnp.bfloat16
    )


def in_vmem(count):
    return [pl.BlockSpec(memory_space=pltpu.VMEM)] * count


def on_device(tokens, adapter_ids, ranks, gain, base_weight, shrink_weight, expand_weight):
    micro_count, own_rows, model_width = tokens.shape
    cols = base_weight.shape[2]
    ad_count, _, rank_most = shrink_weight.shape[1:]
    total_adapters = expand_weight.shape[1]
    devices = lax.axis_size("adapter")
    segments = lax.axis_size("segment")
    planes = segments // 2
    segment = lax.axis_index("segment")
    owner = lax.axis_index("adapter")
    plane, core = segment // 2, segment % 2
    rows = own_rows * devices
    params = pltpu.CompilerParams(vmem_limit_bytes=40 * 1024 * 1024)

    by_dest = tokens.reshape(micro_count * own_rows, devices, cols).transpose(1, 0, 2)
    small = jnp.concatenate([adapter_ids.reshape(-1), ranks]).astype(jnp.bfloat16)
    small = jnp.pad(small, (0, cols - small.shape[0]))
    small = jnp.broadcast_to(small, (devices, micro_count * own_rows, cols))
    first = lax.all_to_all(
        jnp.concatenate([by_dest, small], axis=1), "adapter", 0, 0, tiled=True
    )
    count = micro_count * own_rows
    token_cols = (
        first[:, :count]
        .reshape(devices, micro_count, own_rows, cols)
        .transpose(1, 0, 2, 3)
        .reshape(micro_count, rows, cols)
    )
    all_ids = (
        first[:, count, :count]
        .reshape(devices, micro_count, own_rows)
        .transpose(1, 0, 2)
        .reshape(micro_count, rows)
        .astype(jnp.int32)
    )
    all_ranks = first[:, count, count : count + ad_count].reshape(-1).astype(jnp.float32)
    onehot = all_ids[:, :, None] == jnp.arange(total_adapters, dtype=jnp.int32)
    row_ranks = jnp.sum(jnp.where(onehot, all_ranks, 0.0), axis=-1, keepdims=True)

    shrink = shrink_weight[0].reshape(ad_count, devices, cols, rank_most).transpose(1, 0, 3, 2)
    shrink = lax.all_to_all(
        shrink.reshape(devices, ad_count * rank_most, cols), "adapter", 0, 0, tiled=True
    ).reshape(total_adapters * rank_most, cols)
    own_gain = lax.dynamic_slice_in_dim(gain[0], owner * cols, cols, 0)
    shrink = (shrink.astype(jnp.float32) * own_gain[None, :]).astype(jnp.bfloat16)
    base = (base_weight[0].astype(jnp.float32) * gain[0][:, None]).astype(jnp.bfloat16)
    expand = expand_weight[0].reshape(total_adapters * rank_most, cols)

    block_rows = rows + rows // GROUP

    def work(h, ids, rank):
        sent = pl.pallas_call(
            lambda *refs: before_kernel(rank_most, *refs),
            out_shape=jax.ShapeDtypeStruct((devices, block_rows, cols), jnp.bfloat16),
            in_specs=in_vmem(3),
            out_specs=in_vmem(1)[0],
            compiler_params=params,
        )(h, ids, shrink)
        got = lax.all_to_all(sent, "adapter", 0, 0, tiled=True)
        return pl.pallas_call(
            lambda *refs: after_kernel(rank_most, *refs),
            out_shape=jax.ShapeDtypeStruct((rows, cols), jnp.bfloat16),
            in_specs=in_vmem(6),
            out_specs=in_vmem(1)[0],
            compiler_params=params,
        )(h, got, ids, rank, base, expand)

    to_core = [(2 * p, 2 * p + 1) for p in range(planes)]
    to_plane = [(2 * p + 1, 2 * p + 2) for p in range(planes - 1)]

    def super_tick(k, carry):
        h, out = carry
        micro = k - plane
        valid = (micro >= 0) & (micro < micro_count)
        micro = jnp.clip(micro, 0, micro_count - 1)
        h = jnp.where(segment == 0, token_cols[micro], h)
        ids, rank = all_ids[micro][:, None], row_ranks[micro]
        for turn in range(2):
            active = valid & (core == turn)
            h = lax.cond(active, work, lambda h, ids, rank: h, h, ids, rank)
            out = jnp.where(active, lax.dynamic_update_index_in_dim(out, h, micro, 0), out)
            h = lax.ppermute(h, "segment", to_plane if turn else to_core)
        return h, out

    start = (
        jnp.zeros((rows, cols), jnp.bfloat16),
        jnp.zeros((micro_count, rows, cols), jnp.bfloat16),
    )
    return lax.fori_loop(0, planes + micro_count - 1, super_tick, start)[1][None]


def solution(mesh):
    in_specs = (
        P(None, "adapter", None),
        P(None, "adapter", None),
        P("adapter"),
        P("segment", None),
        P("segment", None, "adapter"),
        P("segment", "adapter", None, None),
        P("segment", None, None, "adapter"),
    )
    out_specs = P("segment", None, None, "adapter")
    return jax.shard_map(
        on_device, mesh=mesh, in_specs=in_specs, out_specs=out_specs, check_vma=False
    )
```

```python
import jax
import jax.numpy as jnp
from jax import lax
from jax.experimental import pallas as pl
from jax.experimental.pallas import tpu as pltpu
from jax.sharding import PartitionSpec as P

GROUP = 4


def lane_group(shape, rank_most):
    return lax.broadcasted_iota(jnp.int32, shape, len(shape) - 1) // rank_most


def spread(value, rank_most):
    step = rank_most
    while step < value.shape[-1]:
        value = value + pltpu.roll(value, step, 1)
        step *= 2
    return value


def before_kernel(rank_most, h_ref, ids_ref, shrink_ref, out_ref):
    rows, cols = h_ref.shape
    packed = rows // GROUP
    h = h_ref[...]
    groups = lane_group((rows, cols), rank_most)
    wanted = ids_ref[...] - groups
    total = jnp.zeros((rows, cols), jnp.float32)
    for j in range(shrink_ref.shape[0] // cols):
        part = lax.dot_general(
            h,
            shrink_ref[j * cols : (j + 1) * cols, :],
            (((1,), (1,)), ((), ())),
            preferred_element_type=jnp.float32,
        )
        total = total + jnp.where(wanted == j * GROUP, part, 0.0)
    total = spread(total, rank_most)
    folded = jnp.zeros((packed, cols), jnp.float32)
    for g in range(GROUP):
        mine = groups[:packed] == g
        folded = jnp.where(mine, total[g * packed : (g + 1) * packed], folded)
    folded = folded.astype(jnp.bfloat16)
    for d in range(out_ref.shape[0]):
        out_ref[d, :rows, :] = h
        out_ref[d, rows:, :] = folded


def finish(rank_most, h_ref, base, low, ids_ref, expand_ref, out_ref):
    rows, cols = h_ref.shape
    wanted = ids_ref[...] - lane_group((rows, cols), rank_most)
    added = jnp.zeros((rows, cols), jnp.float32)
    for j in range(expand_ref.shape[0] // cols):
        picked = jnp.where(wanted == j * GROUP, low, 0.0).astype(jnp.bfloat16)
        added = added + jnp.dot(
            picked, expand_ref[j * cols : (j + 1) * cols, :], preferred_element_type=jnp.float32
        )
    update = (base + added).astype(jnp.bfloat16)
    out_ref[...] = (h_ref[...].astype(jnp.float32) + update.astype(jnp.float32)).astype(
        jnp.bfloat16
    )


def unpacked(rank_most, partial, cols):
    groups = lane_group(partial.shape, rank_most)
    return jnp.concatenate(
        [spread(jnp.where(groups == g, partial, 0.0), rank_most) for g in range(GROUP)], axis=0
    )


def after_kernel(rank_most, h_ref, got_ref, ids_ref, rank_ref, base_ref, expand_ref, out_ref):
    rows, cols = h_ref.shape
    packed = rows // GROUP
    sources = got_ref.shape[0]
    base = jnp.zeros((rows, cols), jnp.float32)
    squares = jnp.zeros((rows, cols), jnp.float32)
    partial = jnp.zeros((packed, cols), jnp.float32)
    for j in range(sources):
        block = got_ref[j, :rows, :]
        base = base + jnp.dot(
            block, base_ref[j * cols : (j + 1) * cols, :], preferred_element_type=jnp.float32
        )
        wide = block.astype(jnp.float32)
        squares = squares + wide * wide
        partial = partial + got_ref[j, rows:, :].astype(jnp.float32)
    mean_square = jnp.sum(squares, axis=-1, keepdims=True) / (sources * cols)
    inverse = lax.rsqrt(mean_square + 1e-05)
    low = unpacked(rank_most, partial, cols)
    rank = rank_ref[...]
    place = lax.broadcasted_iota(jnp.int32, (rows, cols), 1) % rank_most
    factor = jnp.where(place.astype(jnp.float32) < rank, 32.0 / rank, 0.0)
    finish(rank_most, h_ref, base * inverse, low * inverse * factor, ids_ref, expand_ref, out_ref)


def first_after_kernel(rank_most, h_ref, got_ref, ids_ref, base_ref, expand_ref, out_ref):
    partial = jnp.zeros(got_ref.shape[1:], jnp.float32)
    for j in range(got_ref.shape[0]):
        partial = partial + got_ref[j].astype(jnp.float32)
    low = unpacked(rank_most, partial, h_ref.shape[1])
    finish(rank_most, h_ref, base_ref[...], low, ids_ref, expand_ref, out_ref)


def in_vmem(count):
    return [pl.BlockSpec(memory_space=pltpu.VMEM)] * count


def on_device(tokens, adapter_ids, ranks, gain, base_weight, shrink_weight, expand_weight):
    micro_count, own_rows, model_width = tokens.shape
    cols = base_weight.shape[2]
    ad_count, _, rank_most = shrink_weight.shape[1:]
    total_adapters = expand_weight.shape[1]
    devices = lax.axis_size("adapter")
    segments = lax.axis_size("segment")
    segment = lax.axis_index("segment")
    owner = lax.axis_index("adapter")
    rows = own_rows * devices
    packed = rows // GROUP
    count = micro_count * own_rows
    params = pltpu.CompilerParams(vmem_limit_bytes=40 * 1024 * 1024)
    gain_row = gain[0]
    expand = expand_weight[0].reshape(total_adapters * rank_most, cols)

    def call(kernel, shape, *operands):
        return pl.pallas_call(
            lambda *refs: kernel(rank_most, *refs),
            out_shape=jax.ShapeDtypeStruct(shape, jnp.bfloat16),
            in_specs=in_vmem(len(operands)),
            out_specs=in_vmem(1)[0],
            compiler_params=params,
        )(*operands)

    def exchange(blocks):
        return lax.all_to_all(blocks, "adapter", 0, 0, tiled=True)

    def tables(small):
        ids = small[:, :count].reshape(devices, micro_count, own_rows).transpose(1, 0, 2)
        ids = ids.reshape(micro_count, rows).astype(jnp.int32)
        all_ranks = small[:, count : count + ad_count].reshape(-1).astype(jnp.float32)
        onehot = ids[:, :, None] == jnp.arange(total_adapters, dtype=jnp.int32)
        row_ranks = jnp.sum(jnp.where(onehot, all_ranks, 0.0), axis=-1, keepdims=True)
        return ids[:, :, None], row_ranks

    def first_layer(hidden, ids, rank):
        wide = hidden.astype(jnp.float32)
        mean_square = jnp.mean(wide * wide, axis=-1, keepdims=True)
        normed = (wide * lax.rsqrt(mean_square + 1e-05) * gain_row).astype(jnp.bfloat16)
        maps = shrink_weight[0].transpose(0, 2, 1).reshape(ad_count * rank_most, model_width)
        shrunk = lax.dot_general(
            normed, maps, (((1,), (1,)), ((), ())), preferred_element_type=jnp.float32
        ).reshape(rows, ad_count, rank_most)
        mine = (ids - owner * ad_count == jnp.arange(ad_count)).astype(jnp.float32)
        keep = jnp.arange(rank_most, dtype=jnp.float32)[None, :] < rank
        low = jnp.sum(shrunk * mine[:, :, None], axis=1) * jnp.where(keep, 32.0 / rank, 0.0)
        low = low.astype(jnp.bfloat16).reshape(GROUP, packed, rank_most)
        low = low.transpose(1, 0, 2).reshape(packed, cols)
        got = exchange(jnp.broadcast_to(low, (devices, packed, cols)))
        base = jnp.dot(normed, base_weight[0], preferred_element_type=jnp.float32)
        held = lax.dynamic_slice_in_dim(hidden, owner * cols, cols, 1)
        return call(first_after_kernel, (rows, cols), held, got, ids, base, expand)

    small = jnp.concatenate([adapter_ids.reshape(-1), ranks]).astype(jnp.bfloat16)

    def open_first():
        extra = jnp.pad(small, (0, 128 - small.shape[0]))
        extra = jnp.broadcast_to(extra, (own_rows, 128))
        block = jnp.concatenate([tokens[0], extra], axis=1)
        got = exchange(jnp.broadcast_to(block, (devices,) + block.shape))
        ids, row_ranks = tables(got[:, 0, model_width:])
        hidden = got[:, :, :model_width].reshape(rows, model_width)
        h = first_layer(hidden, ids[0], row_ranks[0])
        shrink = jnp.zeros((total_adapters * rank_most, cols), jnp.bfloat16)
        base = jnp.zeros((model_width, cols), jnp.bfloat16)
        return h, ids, row_ranks, shrink, base

    def open_other():
        maps = shrink_weight[0].reshape(ad_count, devices, cols, rank_most).transpose(1, 0, 3, 2)
        maps = maps.reshape(devices, ad_count * rank_most, cols)
        extra = jnp.broadcast_to(jnp.pad(small, (0, cols - small.shape[0])), (devices, 16, cols))
        got = exchange(jnp.concatenate([maps, extra], axis=1))
        ids, row_ranks = tables(got[:, ad_count * rank_most])
        shrink = got[:, : ad_count * rank_most].reshape(total_adapters * rank_most, cols)
        own_gain = lax.dynamic_slice_in_dim(gain_row, owner * cols, cols, 0)
        shrink = (shrink.astype(jnp.float32) * own_gain[None, :]).astype(jnp.bfloat16)
        base = (base_weight[0].astype(jnp.float32) * gain_row[:, None]).astype(jnp.bfloat16)
        h = jnp.zeros((rows, cols), jnp.bfloat16)
        return h, ids, row_ranks, shrink, base

    def work(h, ids, rank, shrink, base):
        sent = call(before_kernel, (devices, rows + packed, cols), h, ids, shrink)
        return call(after_kernel, (rows, cols), h, exchange(sent), ids, rank, base, expand)

    def next_first(h, ids, rank, shrink, base):
        block = tokens[1]
        got = exchange(jnp.broadcast_to(block, (devices,) + block.shape))
        return first_layer(got.reshape(rows, model_width), ids, rank)

    def idle(h, ids, rank, shrink, base):
        return jnp.zeros((rows, cols), jnp.bfloat16)

    h, ids, row_ranks, shrink, base = lax.cond(segment == 0, open_first, open_other)
    outs = [h, h]
    for stage in range(1, segments + 1):
        pairs = [(s, s + 1) for s in (stage - 1, stage - 2) if 0 <= s < segments - 1]
        h = lax.ppermute(h, "segment", pairs)
        leads, trails = segment == stage, segment == stage - 1
        operands = (
            h,
            jnp.where(leads, ids[0], ids[1]),
            jnp.where(leads, row_ranks[0], row_ranks[1]),
            shrink,
            base,
        )
        if stage == 1:
            branch = jnp.where(trails, 2, jnp.where(leads, 1, 0))
            h = lax.switch(branch, (idle, work, next_first), *operands)
        else:
            h = lax.cond(leads | trails, work, idle, *operands)
        outs = [jnp.where(leads, h, outs[0]), jnp.where(trails, h, outs[1])]
    return jnp.stack(outs)[None]


def solution(mesh):
    in_specs = (
        P(None, "adapter", None),
        P(None, "adapter", None),
        P("adapter"),
        P("segment", None),
        P("segment", None, "adapter"),
        P("segment", "adapter", None, None),
        P("segment", None, None, "adapter"),
    )
    out_specs = P("segment", None, None, "adapter")
    return jax.shard_map(
        on_device, mesh=mesh, in_specs=in_specs, out_specs=out_specs, check_vma=False
    )
```

```python
import jax
import jax.numpy as jnp
from jax import lax
from jax.experimental import pallas as pl
from jax.experimental.pallas import tpu as pltpu
from jax.sharding import PartitionSpec as P

GROUP = 4


def lane_group(shape, rank_most):
    return lax.broadcasted_iota(jnp.int32, shape, len(shape) - 1) // rank_most


def spread(value, rank_most):
    step = rank_most
    while step < value.shape[-1]:
        value = value + pltpu.roll(value, step, 1)
        step *= 2
    return value


def before_kernel(rank_most, h_ref, ids_ref, shrink_ref, out_ref):
    rows, cols = h_ref.shape
    packed = rows // GROUP
    h = h_ref[...]
    groups = lane_group((rows, cols), rank_most)
    wanted = ids_ref[...] - groups
    total = jnp.zeros((rows, cols), jnp.float32)
    for j in range(shrink_ref.shape[0] // cols):
        part = lax.dot_general(
            h,
            shrink_ref[j * cols : (j + 1) * cols, :],
            (((1,), (1,)), ((), ())),
            preferred_element_type=jnp.float32,
        )
        total = total + jnp.where(wanted == j * GROUP, part, 0.0)
    total = spread(total, rank_most)
    folded = jnp.zeros((packed, cols), jnp.float32)
    for g in range(GROUP):
        mine = groups[:packed] == g
        folded = jnp.where(mine, total[g * packed : (g + 1) * packed], folded)
    folded = folded.astype(jnp.bfloat16)
    for d in range(out_ref.shape[0]):
        out_ref[d, :rows, :] = h
        out_ref[d, rows:, :] = folded


def finish(rank_most, h_ref, base, low, ids_ref, expand_ref, out_ref):
    rows, cols = h_ref.shape
    wanted = ids_ref[...] - lane_group((rows, cols), rank_most)
    added = jnp.zeros((rows, cols), jnp.float32)
    for j in range(expand_ref.shape[0] // cols):
        picked = jnp.where(wanted == j * GROUP, low, 0.0).astype(jnp.bfloat16)
        added = added + jnp.dot(
            picked, expand_ref[j * cols : (j + 1) * cols, :], preferred_element_type=jnp.float32
        )
    update = (base + added).astype(jnp.bfloat16)
    out_ref[...] = (h_ref[...].astype(jnp.float32) + update.astype(jnp.float32)).astype(
        jnp.bfloat16
    )


def unpacked(rank_most, partial, cols):
    groups = lane_group(partial.shape, rank_most)
    return jnp.concatenate(
        [spread(jnp.where(groups == g, partial, 0.0), rank_most) for g in range(GROUP)], axis=0
    )


def after_kernel(rank_most, h_ref, got_ref, ids_ref, rank_ref, base_ref, expand_ref, out_ref):
    rows, cols = h_ref.shape
    packed = rows // GROUP
    sources = got_ref.shape[0]
    base = jnp.zeros((rows, cols), jnp.float32)
    squares = jnp.zeros((rows, cols), jnp.float32)
    partial = jnp.zeros((packed, cols), jnp.float32)
    for j in range(sources):
        block = got_ref[j, :rows, :]
        base = base + jnp.dot(
            block, base_ref[j * cols : (j + 1) * cols, :], preferred_element_type=jnp.float32
        )
        wide = block.astype(jnp.float32)
        squares = squares + wide * wide
        partial = partial + got_ref[j, rows:, :].astype(jnp.float32)
    mean_square = jnp.sum(squares, axis=-1, keepdims=True) / (sources * cols)
    inverse = lax.rsqrt(mean_square + 1e-05)
    low = unpacked(rank_most, partial, cols)
    rank = rank_ref[...]
    place = lax.broadcasted_iota(jnp.int32, (rows, cols), 1) % rank_most
    factor = jnp.where(place.astype(jnp.float32) < rank, 32.0 / rank, 0.0)
    finish(rank_most, h_ref, base * inverse, low * inverse * factor, ids_ref, expand_ref, out_ref)


def first_kernel(rank_most, hidden_ref, base_ref, maps_ref, gain_ref, wanted_ref, rank_ref, base_out, sent_out):
    rows, width = hidden_ref.shape
    cols, held = base_ref.shape[1], maps_ref.shape[0]
    packed = rows // GROUP
    base = jnp.zeros((rows, cols), jnp.float32)
    shrunk = jnp.zeros((rows, held), jnp.float32)
    squares = jnp.zeros((rows, cols), jnp.float32)
    for j in range(width // cols):
        part = slice(j * cols, (j + 1) * cols)
        wide = hidden_ref[:, part].astype(jnp.float32)
        squares = squares + wide * wide
        scaled = (wide * gain_ref[:, part]).astype(jnp.bfloat16)
        base = base + jnp.dot(scaled, base_ref[part, :], preferred_element_type=jnp.float32)
        shrunk = shrunk + lax.dot_general(
            scaled, maps_ref[:, part], (((1,), (1,)), ((), ())), preferred_element_type=jnp.float32
        )
    inverse = lax.rsqrt(jnp.sum(squares, axis=-1, keepdims=True) / width + 1e-05)
    base_out[...] = base * inverse
    groups = lane_group((rows, held), rank_most)
    place = lax.broadcasted_iota(jnp.int32, (rows, held), 1) % rank_most
    rank = rank_ref[...]
    factor = jnp.where(place.astype(jnp.float32) < rank, 32.0 / rank, 0.0)
    low = jnp.where(wanted_ref[...] == groups, shrunk * inverse * factor, 0.0)
    low = spread(low, rank_most)
    low = jnp.concatenate([low] * (cols // held), axis=1)
    groups = lane_group((packed, cols), rank_most)
    folded = jnp.zeros((packed, cols), jnp.float32)
    for g in range(GROUP):
        folded = jnp.where(groups == g, low[g * packed : (g + 1) * packed], folded)
    folded = folded.astype(jnp.bfloat16)
    for d in range(sent_out.shape[0]):
        sent_out[d] = folded


def first_after_kernel(rank_most, h_ref, got_ref, ids_ref, base_ref, expand_ref, out_ref):
    partial = jnp.zeros(got_ref.shape[1:], jnp.float32)
    for j in range(got_ref.shape[0]):
        partial = partial + got_ref[j].astype(jnp.float32)
    low = unpacked(rank_most, partial, h_ref.shape[1])
    finish(rank_most, h_ref, base_ref[...], low, ids_ref, expand_ref, out_ref)


def unused_kernel(rank_most, *refs):
    for ref in refs:
        ref[:16, :] = jnp.zeros((16, ref.shape[1]), ref.dtype)


def in_vmem(count):
    return [pl.BlockSpec(memory_space=pltpu.VMEM)] * count


def on_device(tokens, adapter_ids, ranks, gain, base_weight, shrink_weight, expand_weight):
    micro_count, own_rows, model_width = tokens.shape
    cols = base_weight.shape[2]
    ad_count, _, rank_most = shrink_weight.shape[1:]
    total_adapters = expand_weight.shape[1]
    devices = lax.axis_size("adapter")
    segments = lax.axis_size("segment")
    segment = lax.axis_index("segment")
    owner = lax.axis_index("adapter")
    rows = own_rows * devices
    packed = rows // GROUP
    count = micro_count * own_rows
    params = pltpu.CompilerParams(vmem_limit_bytes=14 * 1024 * 1024)
    gain_row = gain[0]
    expand = expand_weight[0].reshape(total_adapters * rank_most, cols)

    def call(kernel, shapes, *operands):
        return pl.pallas_call(
            lambda *refs: kernel(rank_most, *refs),
            out_shape=[jax.ShapeDtypeStruct(*shape) for shape in shapes],
            in_specs=in_vmem(len(operands)),
            out_specs=in_vmem(len(shapes)),
            compiler_params=params,
        )(*operands)

    state = ((rows, cols), jnp.bfloat16)

    def exchange(blocks):
        return lax.all_to_all(blocks, "adapter", 0, 0, tiled=True)

    def tables(small):
        ids = small[:, :count].reshape(devices, micro_count, own_rows).transpose(1, 0, 2)
        ids = ids.reshape(micro_count, rows).astype(jnp.int32)
        all_ranks = small[:, count : count + ad_count].reshape(-1).astype(jnp.float32)
        onehot = ids[:, :, None] == jnp.arange(total_adapters, dtype=jnp.int32)
        row_ranks = jnp.sum(jnp.where(onehot, all_ranks, 0.0), axis=-1, keepdims=True)
        return ids[:, :, None], row_ranks

    small = jnp.concatenate([adapter_ids.reshape(-1), ranks]).astype(jnp.bfloat16)

    def gather_rows(micro):
        extra = jnp.broadcast_to(jnp.pad(small, (0, 128 - small.shape[0])), (own_rows, 128))
        block = jnp.concatenate([tokens[micro], extra], axis=1)
        return exchange(jnp.broadcast_to(block, (devices,) + block.shape))

    def first_layer(got, ids, rank):
        hidden = got[:, :, :model_width].reshape(rows, model_width)
        maps = shrink_weight[0].transpose(0, 2, 1).reshape(ad_count * rank_most, model_width)
        base, sent = call(
            first_kernel,
            [((rows, cols), jnp.float32), ((devices, packed, cols), jnp.bfloat16)],
            hidden,
            base_weight[0],
            maps,
            gain,
            ids - owner * ad_count,
            rank,
        )
        held = lax.dynamic_slice_in_dim(hidden, owner * cols, cols, 1)
        return call(first_after_kernel, [state], held, exchange(sent), ids, base, expand)[0]

    def open_first(got):
        ids, row_ranks = tables(got[:, 0, model_width:])
        h = first_layer(got, ids[0], row_ranks[0])
        shrink, base = call(
            unused_kernel,
            [
                ((total_adapters * rank_most, cols), jnp.bfloat16),
                ((model_width, cols), jnp.bfloat16),
            ],
        )
        return h, ids, row_ranks, shrink, base

    def open_other(got):
        maps = shrink_weight[0].reshape(ad_count, devices, cols, rank_most).transpose(1, 0, 3, 2)
        maps = maps.reshape(devices, ad_count * rank_most, cols)
        extra = jnp.broadcast_to(jnp.pad(small, (0, cols - small.shape[0])), (devices, 16, cols))
        got = exchange(jnp.concatenate([maps, extra], axis=1))
        ids, row_ranks = tables(got[:, ad_count * rank_most])
        shrink = got[:, : ad_count * rank_most].reshape(total_adapters * rank_most, cols)
        own_gain = lax.dynamic_slice_in_dim(gain_row, owner * cols, cols, 0)
        shrink = (shrink.astype(jnp.float32) * own_gain[None, :]).astype(jnp.bfloat16)
        base = (base_weight[0].astype(jnp.float32) * gain_row[:, None]).astype(jnp.bfloat16)
        h = jnp.zeros((rows, cols), jnp.bfloat16)
        return h, ids, row_ranks, shrink, base

    def work(h, ids, rank, shrink, base, later):
        blocks = ((devices, rows + packed, cols), jnp.bfloat16)
        (sent,) = call(before_kernel, [blocks], h, ids, shrink)
        return call(after_kernel, [state], h, exchange(sent), ids, rank, base, expand)[0]

    def next_first(h, ids, rank, shrink, base, later):
        return first_layer(later, ids, rank)

    def idle(h, ids, rank, shrink, base, later):
        return jnp.zeros((rows, cols), jnp.bfloat16)

    got = lax.cond(
        segment == 0,
        lambda: gather_rows(0),
        lambda: lax.cond(
            segment == 2,
            lambda: gather_rows(1),
            lambda: jnp.zeros((devices, own_rows, model_width + 128), jnp.bfloat16),
        ),
    )
    later = lax.ppermute(got, "segment", [(2, 0)])
    h, ids, row_ranks, shrink, base = lax.cond(segment == 0, open_first, open_other, got)
    outs = [h, h]
    for stage in range(1, segments + 1):
        pairs = [(s, s + 1) for s in (stage - 1, stage - 2) if 0 <= s < segments - 1]
        h = lax.ppermute(h, "segment", pairs)
        leads, trails = segment == stage, segment == stage - 1
        operands = (
            h,
            jnp.where(leads, ids[0], ids[1]),
            jnp.where(leads, row_ranks[0], row_ranks[1]),
            shrink,
            base,
            later,
        )
        if stage == 1:
            branch = jnp.where(trails, 2, jnp.where(leads, 1, 0))
            h = lax.switch(branch, (idle, work, next_first), *operands)
        else:
            h = lax.cond(leads | trails, work, idle, *operands)
        outs = [jnp.where(leads, h, outs[0]), jnp.where(trails, h, outs[1])]
    return jnp.stack(outs)[None]


def solution(mesh):
    in_specs = (
        P(None, "adapter", None),
        P(None, "adapter", None),
        P("adapter"),
        P("segment", None),
        P("segment", None, "adapter"),
        P("segment", "adapter", None, None),
        P("segment", None, None, "adapter"),
    )
    out_specs = P("segment", None, None, "adapter")
    return jax.shard_map(
        on_device, mesh=mesh, in_specs=in_specs, out_specs=out_specs, check_vma=False
    )
```

```python
import jax
import jax.numpy as jnp
from jax import lax
from jax.experimental import pallas as pl
from jax.experimental.pallas import tpu as pltpu
from jax.sharding import PartitionSpec as P

GROUP = 4
CHUNKS = 8
LANES = 128


def lane_group(shape, rank_most):
    return lax.broadcasted_iota(jnp.int32, shape, len(shape) - 1) // rank_most


def spread(value, rank_most):
    step = rank_most
    while step < value.shape[-1]:
        value = value + pltpu.roll(value, step, 1)
        step *= 2
    return value


def fold(rank_most, wide, cols):
    packed = wide.shape[0] // GROUP
    groups = lane_group((packed, cols), rank_most)
    folded = jnp.zeros((packed, cols), jnp.float32)
    for g in range(GROUP):
        folded = jnp.where(groups == g, wide[g * packed : (g + 1) * packed], folded)
    return folded.astype(jnp.bfloat16)


def unfold(rank_most, folded):
    groups = lane_group(folded.shape, rank_most)
    return jnp.concatenate(
        [spread(jnp.where(groups == g, folded, 0.0), rank_most) for g in range(GROUP)], axis=0
    )


def scaling(rank_most, rank, shape):
    place = lax.broadcasted_iota(jnp.int32, shape, 1) % rank_most
    return jnp.where(place.astype(jnp.float32) < rank, 32.0 / rank, 0.0)


def fetches(source, target, sems, axis=0):
    size = source.shape[axis] // CHUNKS
    copies = []
    for c in range(CHUNKS):
        part = (slice(None),) * axis + (pl.ds(c * size, size),)
        copies.append(pltpu.make_async_copy(source.at[part], target.at[part], sems.at[c]))
    for copy in copies:
        copy.start()
    return copies


def inverse_rms(squares, width):
    return lax.rsqrt(jnp.sum(squares, axis=-1, keepdims=True) / width + 1e-05)


def table_kernel(rank_most, info_ref, first_ref, second_ref):
    info = info_ref[...].astype(jnp.float32)
    rows = info.shape[0]
    lane = lax.broadcasted_iota(jnp.int32, info.shape, 1)
    ranks = jnp.broadcast_to(info[:, 2:3], info.shape).astype(jnp.bfloat16)
    numbers = lax.broadcasted_iota(jnp.int32, (rows, rows), 1).astype(jnp.float32)
    for micro, ref in enumerate((first_ref, second_ref)):
        ids = info[:, micro : micro + 1]
        onehot = jnp.where(ids == numbers, 1.0, 0.0).astype(jnp.bfloat16)
        rank = jnp.dot(onehot, ranks, preferred_element_type=jnp.float32)
        ref[...] = jnp.where(lane == 0, ids, rank)


def pack_kernel(rank_most, maps_ref, info_ref, out_ref):
    held, cols = maps_ref.shape[0], out_ref.shape[2]
    for d in range(out_ref.shape[0]):
        out_ref[d, :held, :] = maps_ref[:, d * cols : (d + 1) * cols]
        out_ref[d, held:, :] = info_ref[...]


def first_kernel(
    rank_most, hidden_ref, base_hbm, maps_hbm, gain_ref, table_ref, owner_ref, order_hbm,
    base_out, sent_out, base_ref, maps_ref, base_sems, maps_sems,
):
    rows = hidden_ref.shape[0]
    width, cols = base_ref.shape
    held = maps_ref.shape[0]
    base_copies = fetches(base_hbm, base_ref, base_sems)
    maps_copies = fetches(maps_hbm, maps_ref, maps_sems, axis=1)
    base = jnp.zeros((rows, cols), jnp.float32)
    shrunk = jnp.zeros((rows, held), jnp.float32)
    squares = jnp.zeros((rows, cols), jnp.float32)
    steps = width // cols
    for j in range(steps):
        if j % (steps // CHUNKS) == 0:
            base_copies[j // (steps // CHUNKS)].wait()
            maps_copies[j // (steps // CHUNKS)].wait()
        part = slice(j * cols, (j + 1) * cols)
        wide = hidden_ref[:, part].astype(jnp.float32)
        squares = squares + wide * wide
        scaled = (wide * gain_ref[:, part]).astype(jnp.bfloat16)
        base = base + jnp.dot(scaled, base_ref[part, :], preferred_element_type=jnp.float32)
        shrunk = shrunk + lax.dot_general(
            scaled, maps_ref[:, part], (((1,), (1,)), ((), ())), preferred_element_type=jnp.float32
        )
    inverse = inverse_rms(squares, width)
    base_out[...] = base * inverse
    groups = lane_group((rows, held), rank_most)
    first = owner_ref[0] * (held // rank_most)
    wanted = table_ref[:, 0:1] == (first + groups).astype(jnp.float32)
    factor = scaling(rank_most, table_ref[:, 1:2], (rows, held))
    low = spread(jnp.where(wanted, shrunk * inverse * factor, 0.0), rank_most)
    folded = fold(rank_most, jnp.concatenate([low] * (cols // held), axis=1), cols)
    for d in range(sent_out.shape[0]):
        sent_out[d] = folded


def finish(rank_most, h_ref, base, low, table_ref, expand_ref, out_ref):
    rows, cols = h_ref.shape
    wanted = table_ref[:, 0:1] - lane_group((rows, cols), rank_most).astype(jnp.float32)
    added = jnp.zeros((rows, cols), jnp.float32)
    for j in range(expand_ref.shape[0] // cols):
        picked = jnp.where(wanted == j * GROUP, low, 0.0).astype(jnp.bfloat16)
        added = added + jnp.dot(
            picked, expand_ref[j * cols : (j + 1) * cols, :], preferred_element_type=jnp.float32
        )
    update = (base + added).astype(jnp.bfloat16)
    out_ref[...] = (h_ref[...].astype(jnp.float32) + update.astype(jnp.float32)).astype(
        jnp.bfloat16
    )


def first_after_kernel(rank_most, h_ref, got_ref, table_ref, base_ref, expand_ref, out_ref):
    partial = jnp.zeros(got_ref.shape[1:], jnp.float32)
    for j in range(got_ref.shape[0]):
        partial = partial + got_ref[j].astype(jnp.float32)
    low = unfold(rank_most, partial)
    finish(rank_most, h_ref, base_ref[...], low, table_ref, expand_ref, out_ref)


def before_kernel(rank_most, h_ref, table_ref, shrink_hbm, out_ref, shrink_ref, sems):
    rows, cols = h_ref.shape
    copies = fetches(shrink_hbm, shrink_ref, sems)
    h = h_ref[...]
    wanted = table_ref[:, 0:1] - lane_group((rows, cols), rank_most).astype(jnp.float32)
    total = jnp.zeros((rows, cols), jnp.float32)
    steps = shrink_ref.shape[0] // cols
    for j in range(steps):
        if j % (steps // CHUNKS) == 0:
            copies[j // (steps // CHUNKS)].wait()
        part = lax.dot_general(
            h,
            shrink_ref[j * cols : (j + 1) * cols, :],
            (((1,), (1,)), ((), ())),
            preferred_element_type=jnp.float32,
        )
        total = total + jnp.where(wanted == j * GROUP, part, 0.0)
    folded = fold(rank_most, spread(total, rank_most), cols)
    for d in range(out_ref.shape[0]):
        out_ref[d, :rows, :] = h
        out_ref[d, rows:, :] = folded


def after_kernel(
    rank_most, h_ref, got_ref, table_ref, base_hbm, expand_ref, out_ref, base_ref, sems
):
    rows, cols = h_ref.shape
    copies = fetches(base_hbm, base_ref, sems)
    sources = got_ref.shape[0]
    base = jnp.zeros((rows, cols), jnp.float32)
    squares = jnp.zeros((rows, cols), jnp.float32)
    partial = jnp.zeros((rows // GROUP, cols), jnp.float32)
    for j in range(sources):
        if j % (sources // CHUNKS) == 0:
            copies[j // (sources // CHUNKS)].wait()
        block = got_ref[j, :rows, :]
        base = base + jnp.dot(
            block, base_ref[j * cols : (j + 1) * cols, :], preferred_element_type=jnp.float32
        )
        wide = block.astype(jnp.float32)
        squares = squares + wide * wide
        partial = partial + got_ref[j, rows:, :].astype(jnp.float32)
    inverse = inverse_rms(squares, sources * cols)
    factor = scaling(rank_most, table_ref[:, 1:2], (rows, cols))
    low = unfold(rank_most, partial) * inverse * factor
    finish(rank_most, h_ref, base * inverse, low, table_ref, expand_ref, out_ref)


def unused_kernel(rank_most, *refs):
    for ref in refs:
        ref[:16, :] = jnp.zeros((16, ref.shape[1]), ref.dtype)


def on_device(tokens, adapter_ids, ranks, gain, base_weight, shrink_weight, expand_weight):
    micro_count, own_rows, model_width = tokens.shape
    cols = base_weight.shape[2]
    ad_count, _, rank_most = shrink_weight.shape[1:]
    total_adapters = expand_weight.shape[1]
    devices = lax.axis_size("adapter")
    segments = lax.axis_size("segment")
    segment = lax.axis_index("segment")
    owner = lax.axis_index("adapter")
    rows = own_rows * devices
    packed = rows // GROUP
    held = ad_count * rank_most
    all_held = total_adapters * rank_most
    gain_row = gain[0]
    expand = expand_weight[0].reshape(all_held, cols)
    maps = shrink_weight[0].transpose(0, 2, 1).reshape(held, model_width)

    half, full = jnp.bfloat16, jnp.float32
    state = ((rows, cols), half)
    vmem = pl.BlockSpec(memory_space=pltpu.VMEM)
    hbm = pl.BlockSpec(memory_space=pl.ANY)
    smem = pl.BlockSpec(memory_space=pltpu.SMEM)
    fetched = pltpu.SemaphoreType.DMA((CHUNKS,))

    def call(kernel, shapes, *operands, specs=None, scratch=()):
        return pl.pallas_call(
            lambda *refs: kernel(rank_most, *refs),
            out_shape=[jax.ShapeDtypeStruct(*shape) for shape in shapes],
            in_specs=specs or [vmem] * len(operands),
            out_specs=[vmem] * len(shapes),
            scratch_shapes=scratch,
            compiler_params=pltpu.CompilerParams(vmem_limit_bytes=14 * 1024 * 1024),
        )(*operands)

    def exchange(blocks):
        return lax.all_to_all(blocks, "adapter", 0, 0, tiled=True)

    info = jnp.concatenate([adapter_ids[0], adapter_ids[1], ranks[:, None]], axis=1)
    info = jnp.pad(info.astype(half), ((0, 0), (0, LANES - info.shape[1])))

    def tables(info):
        return call(table_kernel, [((rows, LANES), full)] * 2, info)

    def gather_rows(micro):
        block = jnp.concatenate([tokens[micro], info], axis=1)
        got = exchange(jnp.broadcast_to(block, (devices,) + block.shape))
        return got.reshape(rows, model_width + LANES)

    def first_layer(hidden, table, order):
        base, sent = call(
            first_kernel,
            [((rows, cols), full), ((devices, packed, cols), half)],
            hidden,
            base_weight[0],
            maps,
            gain,
            table,
            owner.astype(jnp.int32).reshape(1),
            order,
            specs=[vmem, hbm, hbm, vmem, vmem, smem, hbm],
            scratch=[
                pltpu.VMEM((model_width, cols), half),
                pltpu.VMEM((held, model_width), half),
                fetched,
                fetched,
            ],
        )
        own = lax.dynamic_slice_in_dim(hidden, owner * cols, cols, 1)
        return call(first_after_kernel, [state], own, exchange(sent), table, base, expand)[0]

    def open_first(hidden):
        table, next_table = tables(hidden[:, model_width:])
        h = first_layer(hidden, table, hidden)
        shrink, base = call(
            unused_kernel, [((all_held, cols), half), ((model_width, cols), half)]
        )
        return h, table, next_table, shrink, base

    def open_other(hidden):
        extra = jnp.pad(info, ((0, 16 - own_rows), (0, cols - LANES)))
        (sent,) = call(pack_kernel, [((devices, held + 16, cols), half)], maps, extra)
        got = exchange(sent)
        table, next_table = tables(got[:, held : held + own_rows, :LANES].reshape(rows, LANES))
        shrink = got[:, :held].reshape(all_held, cols)
        own_gain = lax.dynamic_slice_in_dim(gain_row, owner * cols, cols, 0)
        shrink = (shrink.astype(full) * own_gain[None, :]).astype(half)
        base = (base_weight[0].astype(full) * gain_row[:, None]).astype(half)
        return jnp.zeros((rows, cols), half), table, next_table, shrink, base

    block_shape = (devices, rows + packed, cols)

    def spread_out(h, table, shrink):
        (sent,) = call(
            before_kernel,
            [(block_shape, half)],
            h,
            table,
            shrink,
            specs=[vmem, vmem, hbm],
            scratch=[pltpu.VMEM((all_held, cols), half), fetched],
        )
        return exchange(sent)

    def project(h, got, table, base):
        return call(
            after_kernel,
            [state],
            h,
            got,
            table,
            base,
            expand,
            specs=[vmem, vmem, vmem, hbm, vmem],
            scratch=[pltpu.VMEM((model_width, cols), half), fetched],
        )[0]

    def nothing():
        return jnp.zeros((rows, cols), half)

    hidden = lax.cond(
        segment == 0,
        lambda: gather_rows(0),
        lambda: lax.cond(
            segment == 2,
            lambda: gather_rows(1),
            lambda: jnp.zeros((rows, model_width + LANES), half),
        ),
    )
    later = lax.ppermute(hidden, "segment", [(2, 0)])
    h, table, next_table, shrink, base = lax.cond(segment == 0, open_first, open_other, hidden)
    outs = [h, h]
    for stage in range(1, segments + 1):
        pairs = [(s, s + 1) for s in (stage - 1, stage - 2) if 0 <= s < segments - 1]
        h = lax.ppermute(h, "segment", pairs)
        leads, trails = segment == stage, segment == stage - 1
        now = jnp.where(leads, table, next_table)
        if stage == 1:
            got = lax.cond(
                leads,
                lambda: spread_out(h, now, shrink),
                lambda: jnp.zeros(block_shape, half),
            )
            over = lax.ppermute(got[0, :16, :LANES], "segment", [(1, 0)])
            branch = jnp.where(trails, 2, jnp.where(leads, 1, 0))
            h = lax.switch(
                branch,
                (nothing, lambda: project(h, got, now, base), lambda: first_layer(later, now, over)),
            )
        else:
            h = lax.cond(
                leads | trails,
                lambda: project(h, spread_out(h, now, shrink), now, base),
                nothing,
            )
        outs = [jnp.where(leads, h, outs[0]), jnp.where(trails, h, outs[1])]
    return jnp.stack(outs)[None]


def solution(mesh):
    in_specs = (
        P(None, "adapter", None),
        P(None, "adapter", None),
        P("adapter"),
        P("segment", None),
        P("segment", None, "adapter"),
        P("segment", "adapter", None, None),
        P("segment", None, None, "adapter"),
    )
    out_specs = P("segment", None, None, "adapter")
    return jax.shard_map(
        on_device, mesh=mesh, in_specs=in_specs, out_specs=out_specs, check_vma=False
    )
```

```python
import jax
import jax.numpy as jnp
from jax import lax
from jax.experimental import pallas as pl
from jax.experimental.pallas import tpu as pltpu
from jax.sharding import PartitionSpec as P

GROUP = 4
CHUNKS = 8
LANES = 128


def lane_group(shape, rank_most):
    return lax.broadcasted_iota(jnp.int32, shape, len(shape) - 1) // rank_most


def spread(value, rank_most):
    step = rank_most
    while step < value.shape[-1]:
        value = value + pltpu.roll(value, step, 1)
        step *= 2
    return value


def fold(rank_most, wide, cols):
    packed = wide.shape[0] // GROUP
    groups = lane_group((packed, cols), rank_most)
    folded = jnp.zeros((packed, cols), jnp.float32)
    for g in range(GROUP):
        folded = jnp.where(groups == g, wide[g * packed : (g + 1) * packed], folded)
    return folded.astype(jnp.bfloat16)


def unfold(rank_most, folded):
    groups = lane_group(folded.shape, rank_most)
    return jnp.concatenate(
        [spread(jnp.where(groups == g, folded, 0.0), rank_most) for g in range(GROUP)], axis=0
    )


def scaling(rank_most, rank, shape):
    place = lax.broadcasted_iota(jnp.int32, shape, 1) % rank_most
    return jnp.where(place.astype(jnp.float32) < rank, 32.0 / rank, 0.0)


def fetches(source, target, sems, axis=0):
    size = source.shape[axis] // CHUNKS
    copies = []
    for c in range(CHUNKS):
        part = (slice(None),) * axis + (pl.ds(c * size, size),)
        copies.append(pltpu.make_async_copy(source.at[part], target.at[part], sems.at[c]))
    for copy in copies:
        copy.start()
    return copies


def inverse_rms(squares, width):
    return lax.rsqrt(jnp.sum(squares, axis=-1, keepdims=True) / width + 1e-05)


def table_kernel(rank_most, info_ref, first_ref, second_ref):
    info = info_ref[...].astype(jnp.float32)
    rows = info.shape[0]
    lane = lax.broadcasted_iota(jnp.int32, info.shape, 1)
    ranks = jnp.broadcast_to(info[:, 2:3], info.shape).astype(jnp.bfloat16)
    numbers = lax.broadcasted_iota(jnp.int32, (rows, rows), 1).astype(jnp.float32)
    for micro, ref in enumerate((first_ref, second_ref)):
        ids = info[:, micro : micro + 1]
        onehot = jnp.where(ids == numbers, 1.0, 0.0).astype(jnp.bfloat16)
        rank = jnp.dot(onehot, ranks, preferred_element_type=jnp.float32)
        ref[...] = jnp.where(lane == 0, ids, rank)


def pack_kernel(rank_most, maps_ref, info_ref, out_ref):
    held, cols = maps_ref.shape[0], out_ref.shape[2]
    for d in range(out_ref.shape[0]):
        out_ref[d, :held, :] = maps_ref[:, d * cols : (d + 1) * cols]
        out_ref[d, held:, :] = info_ref[...]


def first_kernel(
    rank_most, hidden_ref, base_hbm, maps_hbm, gain_ref, table_ref, owner_ref,
    base_out, sent_out, base_ref, maps_ref, base_sems, maps_sems,
):
    rows = hidden_ref.shape[0]
    width, cols = base_ref.shape
    held = maps_ref.shape[0]
    base_copies = fetches(base_hbm, base_ref, base_sems)
    maps_copies = fetches(maps_hbm, maps_ref, maps_sems, axis=1)
    base = jnp.zeros((rows, cols), jnp.float32)
    shrunk = jnp.zeros((rows, held), jnp.float32)
    squares = jnp.zeros((rows, cols), jnp.float32)
    steps = width // cols
    for j in range(steps):
        if j % (steps // CHUNKS) == 0:
            base_copies[j // (steps // CHUNKS)].wait()
            maps_copies[j // (steps // CHUNKS)].wait()
        part = slice(j * cols, (j + 1) * cols)
        wide = hidden_ref[:, part].astype(jnp.float32)
        squares = squares + wide * wide
        scaled = (wide * gain_ref[:, part]).astype(jnp.bfloat16)
        base = base + jnp.dot(scaled, base_ref[part, :], preferred_element_type=jnp.float32)
        shrunk = shrunk + lax.dot_general(
            scaled, maps_ref[:, part], (((1,), (1,)), ((), ())), preferred_element_type=jnp.float32
        )
    inverse = inverse_rms(squares, width)
    base_out[...] = base * inverse
    groups = lane_group((rows, held), rank_most)
    first = owner_ref[0] * (held // rank_most)
    wanted = table_ref[:, 0:1] == (first + groups).astype(jnp.float32)
    factor = scaling(rank_most, table_ref[:, 1:2], (rows, held))
    low = spread(jnp.where(wanted, shrunk * inverse * factor, 0.0), rank_most)
    folded = fold(rank_most, jnp.concatenate([low] * (cols // held), axis=1), cols)
    for d in range(sent_out.shape[0]):
        sent_out[d] = folded


def finish(rank_most, h_ref, base, low, table_ref, expand_ref, out_ref):
    rows, cols = h_ref.shape
    wanted = table_ref[:, 0:1] - lane_group((rows, cols), rank_most).astype(jnp.float32)
    added = jnp.zeros((rows, cols), jnp.float32)
    for j in range(expand_ref.shape[0] // cols):
        picked = jnp.where(wanted == j * GROUP, low, 0.0).astype(jnp.bfloat16)
        added = added + jnp.dot(
            picked, expand_ref[j * cols : (j + 1) * cols, :], preferred_element_type=jnp.float32
        )
    update = (base + added).astype(jnp.bfloat16)
    out_ref[...] = (h_ref[...].astype(jnp.float32) + update.astype(jnp.float32)).astype(
        jnp.bfloat16
    )


def first_after_kernel(rank_most, h_ref, got_ref, table_ref, base_ref, expand_ref, out_ref):
    partial = jnp.zeros(got_ref.shape[1:], jnp.float32)
    for j in range(got_ref.shape[0]):
        partial = partial + got_ref[j].astype(jnp.float32)
    low = unfold(rank_most, partial)
    finish(rank_most, h_ref, base_ref[...], low, table_ref, expand_ref, out_ref)


def before_kernel(rank_most, h_ref, table_ref, gain_ref, shrink_hbm, out_ref, shrink_ref, sems):
    rows, cols = h_ref.shape
    copies = fetches(shrink_hbm, shrink_ref, sems)
    h = h_ref[...]
    scaled = (h.astype(jnp.float32) * gain_ref[...]).astype(jnp.bfloat16)
    wanted = table_ref[:, 0:1] - lane_group((rows, cols), rank_most).astype(jnp.float32)
    total = jnp.zeros((rows, cols), jnp.float32)
    steps = shrink_ref.shape[0] // cols
    for j in range(steps):
        if j % (steps // CHUNKS) == 0:
            copies[j // (steps // CHUNKS)].wait()
        part = lax.dot_general(
            scaled,
            shrink_ref[j * cols : (j + 1) * cols, :],
            (((1,), (1,)), ((), ())),
            preferred_element_type=jnp.float32,
        )
        total = total + jnp.where(wanted == j * GROUP, part, 0.0)
    folded = fold(rank_most, spread(total, rank_most), cols)
    for d in range(out_ref.shape[0]):
        out_ref[d, :rows, :] = h
        out_ref[d, rows:, :] = folded


def after_kernel(
    rank_most, h_ref, got_ref, table_ref, gain_ref, base_hbm, expand_ref, out_ref, base_ref, sems
):
    rows, cols = h_ref.shape
    copies = fetches(base_hbm, base_ref, sems)
    sources = got_ref.shape[0]
    base = jnp.zeros((rows, cols), jnp.float32)
    squares = jnp.zeros((rows, cols), jnp.float32)
    partial = jnp.zeros((rows // GROUP, cols), jnp.float32)
    for j in range(sources):
        if j % (sources // CHUNKS) == 0:
            copies[j // (sources // CHUNKS)].wait()
        part = slice(j * cols, (j + 1) * cols)
        wide = got_ref[j, :rows, :].astype(jnp.float32)
        squares = squares + wide * wide
        scaled = (wide * gain_ref[:, part]).astype(jnp.bfloat16)
        base = base + jnp.dot(scaled, base_ref[part, :], preferred_element_type=jnp.float32)
        partial = partial + got_ref[j, rows:, :].astype(jnp.float32)
    inverse = inverse_rms(squares, sources * cols)
    factor = scaling(rank_most, table_ref[:, 1:2], (rows, cols))
    low = unfold(rank_most, partial) * inverse * factor
    finish(rank_most, h_ref, base * inverse, low, table_ref, expand_ref, out_ref)


def unused_kernel(rank_most, ref):
    ref[:16, :] = jnp.zeros((16, ref.shape[1]), ref.dtype)


def on_device(tokens, adapter_ids, ranks, gain, base_weight, shrink_weight, expand_weight):
    micro_count, own_rows, model_width = tokens.shape
    cols = base_weight.shape[2]
    ad_count, _, rank_most = shrink_weight.shape[1:]
    total_adapters = expand_weight.shape[1]
    devices = lax.axis_size("adapter")
    segments = lax.axis_size("segment")
    planes = segments // 2
    segment = lax.axis_index("segment")
    owner = lax.axis_index("adapter")
    plane, core = segment // 2, segment % 2
    rows = own_rows * devices
    packed = rows // GROUP
    held = ad_count * rank_most
    all_held = total_adapters * rank_most
    base = base_weight[0]
    expand = expand_weight[0].reshape(all_held, cols)
    maps = shrink_weight[0].transpose(0, 2, 1).reshape(held, model_width)

    half, full = jnp.bfloat16, jnp.float32
    state = ((rows, cols), half)
    vmem = pl.BlockSpec(memory_space=pltpu.VMEM)
    hbm = pl.BlockSpec(memory_space=pl.ANY)
    smem = pl.BlockSpec(memory_space=pltpu.SMEM)
    fetched = pltpu.SemaphoreType.DMA((CHUNKS,))

    def call(kernel, shapes, *operands, specs=None, scratch=()):
        return pl.pallas_call(
            lambda *refs: kernel(rank_most, *refs),
            out_shape=[jax.ShapeDtypeStruct(*shape) for shape in shapes],
            in_specs=specs or [vmem] * len(operands),
            out_specs=[vmem] * len(shapes),
            scratch_shapes=scratch,
            compiler_params=pltpu.CompilerParams(vmem_limit_bytes=14 * 1024 * 1024),
        )(*operands)

    def exchange(blocks):
        return lax.all_to_all(blocks, "adapter", 0, 0, tiled=True)

    def swap(array):
        pairs = [(s, s ^ 1) for s in range(segments)]
        return lax.ppermute(array, "segment", pairs)

    info = jnp.concatenate([adapter_ids[0], adapter_ids[1], ranks[:, None]], axis=1)
    info = jnp.pad(info.astype(half), ((0, 0), (0, LANES - info.shape[1])))

    def tables(info):
        return call(table_kernel, [((rows, LANES), full)] * 2, info)

    def gather_rows(micro):
        block = jnp.concatenate([tokens[micro], info], axis=1)
        got = exchange(jnp.broadcast_to(block, (devices,) + block.shape))
        return got.reshape(rows, model_width + LANES)

    def first_layer(hidden, table):
        based, sent = call(
            first_kernel,
            [((rows, cols), full), ((devices, packed, cols), half)],
            hidden,
            base,
            maps,
            gain,
            table,
            owner.astype(jnp.int32).reshape(1),
            specs=[vmem, hbm, hbm, vmem, vmem, smem],
            scratch=[
                pltpu.VMEM((model_width, cols), half),
                pltpu.VMEM((held, model_width), half),
                fetched,
                fetched,
            ],
        )
        own = lax.dynamic_slice_in_dim(hidden, owner * cols, cols, 1)
        return call(first_after_kernel, [state], own, exchange(sent), table, based, expand)[0]

    def nothing():
        return jnp.zeros((rows, cols), half)

    def open_first(hidden):
        table, next_table = tables(hidden[:, model_width:])
        (shrink,) = call(unused_kernel, [((all_held, cols), half)])
        return first_layer(hidden, table), table, next_table, shrink

    def open_other(hidden):
        extra = jnp.pad(info, ((0, 16 - own_rows), (0, cols - LANES)))
        (sent,) = call(pack_kernel, [((devices, held + 16, cols), half)], maps, extra)
        got = exchange(sent)
        table, next_table = tables(got[:, held : held + own_rows, :LANES].reshape(rows, LANES))
        return nothing(), table, next_table, got[:, :held].reshape(all_held, cols)

    def work(h, table, weights):
        shrink, base, expand, gain, own_gain = weights
        (sent,) = call(
            before_kernel,
            [((devices, rows + packed, cols), half)],
            h,
            table,
            own_gain,
            shrink,
            specs=[vmem, vmem, vmem, hbm],
            scratch=[pltpu.VMEM((all_held, cols), half), fetched],
        )
        return call(
            after_kernel,
            [state],
            h,
            exchange(sent),
            table,
            gain,
            base,
            expand,
            specs=[vmem, vmem, vmem, vmem, hbm, vmem],
            scratch=[pltpu.VMEM((model_width, cols), half), fetched],
        )[0]

    other_base, other_expand = swap(base), swap(expand)
    lender = segments // 2
    hidden = lax.cond(
        segment == 0,
        lambda: gather_rows(0),
        lambda: lax.cond(
            segment == lender,
            lambda: gather_rows(1),
            lambda: jnp.zeros((rows, model_width + LANES), half),
        ),
    )
    later = lax.ppermute(hidden, "segment", [(lender, 0)])
    h, table, next_table, shrink = lax.cond(segment == 0, open_first, open_other, hidden)
    opened = h
    h = lax.ppermute(h, "segment", [(0, 1)])
    second = lax.cond(segment == 0, lambda: first_layer(later, next_table), nothing)

    own_gain = lax.dynamic_slice_in_dim(gain, owner * cols, cols, 1)
    own = (shrink, base, expand, gain, own_gain)
    other_gain = swap(gain)
    other_own_gain = lax.dynamic_slice_in_dim(other_gain, owner * cols, cols, 1)
    other = (swap(shrink), other_base, other_expand, other_gain, other_own_gain)

    odd = lax.switch(
        jnp.minimum(segment, 2),
        (lambda: work(second, next_table, other), lambda: work(h, table, own), nothing),
    )
    even = second
    h = odd
    for p in range(1, planes):
        h = lax.ppermute(h, "segment", [(2 * p - 1, 2 * p + 1), (2 * p - 2, 2 * p)])

        def core_0():
            first = work(h, next_table, own)
            return first, work(first, next_table, other)

        def core_1():
            first = work(h, table, other)
            return first, work(first, table, own)

        first, h = lax.switch(
            jnp.where(plane == p, core, 2), (core_0, core_1, lambda: (nothing(), nothing()))
        )
        even, odd = jnp.where(plane == p, first, even), jnp.where(plane == p, h, odd)

    swapped = swap(jnp.where(core == 0, odd, even))
    first = jnp.where(segment == 0, opened, jnp.where(core == 0, swapped, odd))
    return jnp.stack([first, jnp.where(core == 0, even, swapped)])[None]


def solution(mesh):
    in_specs = (
        P(None, "adapter", None),
        P(None, "adapter", None),
        P("adapter"),
        P("segment", None),
        P("segment", None, "adapter"),
        P("segment", "adapter", None, None),
        P("segment", None, None, "adapter"),
    )
    out_specs = P("segment", None, None, "adapter")
    return jax.shard_map(
        on_device, mesh=mesh, in_specs=in_specs, out_specs=out_specs, check_vma=False
    )
```

```python
import jax
import jax.numpy as jnp
from jax import lax
from jax.experimental import pallas as pl
from jax.experimental.pallas import tpu as pltpu
from jax.sharding import PartitionSpec as P

GROUP = 4
CHUNKS = 8
LANES = 128


def lane_group(shape, rank_most):
    return lax.broadcasted_iota(jnp.int32, shape, len(shape) - 1) // rank_most


def spread(value, rank_most):
    step = rank_most
    while step < value.shape[-1]:
        value = value + pltpu.roll(value, step, 1)
        step *= 2
    return value


def fold(rank_most, wide, cols):
    packed = wide.shape[0] // GROUP
    groups = lane_group((packed, cols), rank_most)
    folded = jnp.zeros((packed, cols), jnp.float32)
    for g in range(GROUP):
        folded = jnp.where(groups == g, wide[g * packed : (g + 1) * packed], folded)
    return folded.astype(jnp.bfloat16)


def unfold(rank_most, folded):
    groups = lane_group(folded.shape, rank_most)
    return jnp.concatenate(
        [spread(jnp.where(groups == g, folded, 0.0), rank_most) for g in range(GROUP)], axis=0
    )


def scaling(rank_most, rank, shape):
    place = lax.broadcasted_iota(jnp.int32, shape, 1) % rank_most
    return jnp.where(place.astype(jnp.float32) < rank, 32.0 / rank, 0.0)


def fetches(source, target, sems, axis=0):
    size = source.shape[axis] // CHUNKS
    copies = []
    for c in range(CHUNKS):
        part = (slice(None),) * axis + (pl.ds(c * size, size),)
        copies.append(pltpu.make_async_copy(source.at[part], target.at[part], sems.at[c]))
    for copy in copies:
        copy.start()
    return copies


def inverse_rms(squares, width):
    return lax.rsqrt(jnp.sum(squares, axis=-1, keepdims=True) / width + 1e-05)


def table_kernel(rank_most, info_ref, first_ref, second_ref):
    info = info_ref[...].astype(jnp.float32)
    rows = info.shape[0]
    lane = lax.broadcasted_iota(jnp.int32, info.shape, 1)
    ranks = jnp.broadcast_to(info[:, 2:3], info.shape).astype(jnp.bfloat16)
    numbers = lax.broadcasted_iota(jnp.int32, (rows, rows), 1).astype(jnp.float32)
    for micro, ref in enumerate((first_ref, second_ref)):
        ids = info[:, micro : micro + 1]
        onehot = jnp.where(ids == numbers, 1.0, 0.0).astype(jnp.bfloat16)
        rank = jnp.dot(onehot, ranks, preferred_element_type=jnp.float32)
        ref[...] = jnp.where(lane == 0, ids, rank)


def pack_kernel(rank_most, maps_ref, info_ref, out_ref):
    held, cols = maps_ref.shape[0], out_ref.shape[2]
    for d in range(out_ref.shape[0]):
        out_ref[d, :held, :] = maps_ref[:, d * cols : (d + 1) * cols]
        out_ref[d, held:, :] = info_ref[...]


def first_kernel(
    rank_most, hidden_ref, base_hbm, maps_hbm, gain_ref, table_ref, owner_ref,
    base_out, sent_out, base_ref, maps_ref, base_sems, maps_sems,
):
    rows = hidden_ref.shape[0]
    width, cols = base_ref.shape
    held = maps_ref.shape[0]
    base_copies = fetches(base_hbm, base_ref, base_sems)
    maps_copies = fetches(maps_hbm, maps_ref, maps_sems, axis=1)
    base = jnp.zeros((rows, cols), jnp.float32)
    shrunk = jnp.zeros((rows, held), jnp.float32)
    squares = jnp.zeros((rows, cols), jnp.float32)
    steps = width // cols
    for j in range(steps):
        if j % (steps // CHUNKS) == 0:
            base_copies[j // (steps // CHUNKS)].wait()
            maps_copies[j // (steps // CHUNKS)].wait()
        part = slice(j * cols, (j + 1) * cols)
        wide = hidden_ref[:, part].astype(jnp.float32)
        squares = squares + wide * wide
        scaled = (wide * gain_ref[:, part]).astype(jnp.bfloat16)
        base = base + jnp.dot(scaled, base_ref[part, :], preferred_element_type=jnp.float32)
        shrunk = shrunk + lax.dot_general(
            scaled, maps_ref[:, part], (((1,), (1,)), ((), ())), preferred_element_type=jnp.float32
        )
    inverse = inverse_rms(squares, width)
    base_out[...] = base * inverse
    groups = lane_group((rows, held), rank_most)
    first = owner_ref[0] * (held // rank_most)
    wanted = table_ref[:, 0:1] == (first + groups).astype(jnp.float32)
    factor = scaling(rank_most, table_ref[:, 1:2], (rows, held))
    low = spread(jnp.where(wanted, shrunk * inverse * factor, 0.0), rank_most)
    folded = fold(rank_most, jnp.concatenate([low] * (cols // held), axis=1), cols)
    for d in range(sent_out.shape[0]):
        sent_out[d] = folded


def finish(rank_most, h_ref, base, low, table_ref, expand_ref, out_ref):
    rows, cols = h_ref.shape
    wanted = table_ref[:, 0:1] - lane_group((rows, cols), rank_most).astype(jnp.float32)
    added = jnp.zeros((rows, cols), jnp.float32)
    for j in range(expand_ref.shape[0] // cols):
        picked = jnp.where(wanted == j * GROUP, low, 0.0).astype(jnp.bfloat16)
        added = added + jnp.dot(
            picked, expand_ref[j * cols : (j + 1) * cols, :], preferred_element_type=jnp.float32
        )
    update = (base + added).astype(jnp.bfloat16)
    out_ref[...] = (h_ref[...].astype(jnp.float32) + update.astype(jnp.float32)).astype(
        jnp.bfloat16
    )


def first_after_kernel(rank_most, h_ref, got_ref, table_ref, base_ref, expand_ref, out_ref):
    partial = jnp.zeros(got_ref.shape[1:], jnp.float32)
    for j in range(got_ref.shape[0]):
        partial = partial + got_ref[j].astype(jnp.float32)
    low = unfold(rank_most, partial)
    finish(rank_most, h_ref, base_ref[...], low, table_ref, expand_ref, out_ref)


def before_kernel(rank_most, h_ref, table_ref, gain_ref, shrink_hbm, out_ref, shrink_ref, sems):
    rows, cols = h_ref.shape
    copies = fetches(shrink_hbm, shrink_ref, sems)
    h = h_ref[...]
    scaled = (h.astype(jnp.float32) * gain_ref[...]).astype(jnp.bfloat16)
    wanted = table_ref[:, 0:1] - lane_group((rows, cols), rank_most).astype(jnp.float32)
    total = jnp.zeros((rows, cols), jnp.float32)
    steps = shrink_ref.shape[0] // cols
    for j in range(steps):
        if j % (steps // CHUNKS) == 0:
            copies[j // (steps // CHUNKS)].wait()
        part = lax.dot_general(
            scaled,
            shrink_ref[j * cols : (j + 1) * cols, :],
            (((1,), (1,)), ((), ())),
            preferred_element_type=jnp.float32,
        )
        total = total + jnp.where(wanted == j * GROUP, part, 0.0)
    folded = fold(rank_most, spread(total, rank_most), cols)
    for d in range(out_ref.shape[0]):
        out_ref[d, :rows, :] = h
        out_ref[d, rows:, :] = folded


def after_kernel(
    rank_most, h_ref, got_ref, table_ref, gain_ref, base_hbm, expand_hbm,
    out_ref, base_ref, expand_ref, base_sems, expand_sems,
):
    rows, cols = h_ref.shape
    copies = fetches(base_hbm, base_ref, base_sems)
    expand_copies = fetches(expand_hbm, expand_ref, expand_sems)
    sources = got_ref.shape[0]
    base = jnp.zeros((rows, cols), jnp.float32)
    squares = jnp.zeros((rows, cols), jnp.float32)
    partial = jnp.zeros((rows // GROUP, cols), jnp.float32)
    for j in range(sources):
        if j % (sources // CHUNKS) == 0:
            copies[j // (sources // CHUNKS)].wait()
        part = slice(j * cols, (j + 1) * cols)
        wide = got_ref[j, :rows, :].astype(jnp.float32)
        squares = squares + wide * wide
        scaled = (wide * gain_ref[:, part]).astype(jnp.bfloat16)
        base = base + jnp.dot(scaled, base_ref[part, :], preferred_element_type=jnp.float32)
        partial = partial + got_ref[j, rows:, :].astype(jnp.float32)
    inverse = inverse_rms(squares, sources * cols)
    factor = scaling(rank_most, table_ref[:, 1:2], (rows, cols))
    low = unfold(rank_most, partial) * inverse * factor
    for copy in expand_copies:
        copy.wait()
    finish(rank_most, h_ref, base * inverse, low, table_ref, expand_ref, out_ref)


def unused_kernel(rank_most, ref):
    ref[:16, :] = jnp.zeros((16, ref.shape[1]), ref.dtype)


def on_device(tokens, adapter_ids, ranks, gain, base_weight, shrink_weight, expand_weight):
    micro_count, own_rows, model_width = tokens.shape
    cols = base_weight.shape[2]
    ad_count, _, rank_most = shrink_weight.shape[1:]
    total_adapters = expand_weight.shape[1]
    devices = lax.axis_size("adapter")
    segments = lax.axis_size("segment")
    planes = segments // 2
    segment = lax.axis_index("segment")
    owner = lax.axis_index("adapter")
    plane, core = segment // 2, segment % 2
    rows = own_rows * devices
    packed = rows // GROUP
    held = ad_count * rank_most
    all_held = total_adapters * rank_most
    base = base_weight[0]
    expand = expand_weight[0].reshape(all_held, cols)
    maps = shrink_weight[0].transpose(0, 2, 1).reshape(held, model_width)

    half, full = jnp.bfloat16, jnp.float32
    state = ((rows, cols), half)
    vmem = pl.BlockSpec(memory_space=pltpu.VMEM)
    hbm = pl.BlockSpec(memory_space=pl.ANY)
    smem = pl.BlockSpec(memory_space=pltpu.SMEM)
    fetched = pltpu.SemaphoreType.DMA((CHUNKS,))

    def call(kernel, shapes, *operands, specs=None, scratch=()):
        return pl.pallas_call(
            lambda *refs: kernel(rank_most, *refs),
            out_shape=[jax.ShapeDtypeStruct(*shape) for shape in shapes],
            in_specs=specs or [vmem] * len(operands),
            out_specs=[vmem] * len(shapes),
            scratch_shapes=scratch,
            compiler_params=pltpu.CompilerParams(vmem_limit_bytes=14 * 1024 * 1024),
        )(*operands)

    def exchange(blocks):
        return lax.all_to_all(blocks, "adapter", 0, 0, tiled=True)

    def swap(array):
        pairs = [(s, s ^ 1) for s in range(segments)]
        return lax.ppermute(array, "segment", pairs)

    info = jnp.concatenate([adapter_ids[0], adapter_ids[1], ranks[:, None]], axis=1)
    info = jnp.pad(info.astype(half), ((0, 0), (0, LANES - info.shape[1])))

    def tables(info):
        return call(table_kernel, [((rows, LANES), full)] * 2, info)

    def gather_rows(micro):
        block = jnp.concatenate([tokens[micro], info], axis=1)
        got = exchange(jnp.broadcast_to(block, (devices,) + block.shape))
        return got.reshape(rows, model_width + LANES)

    def first_layer(hidden, table):
        based, sent = call(
            first_kernel,
            [((rows, cols), full), ((devices, packed, cols), half)],
            hidden,
            base,
            maps,
            gain,
            table,
            owner.astype(jnp.int32).reshape(1),
            specs=[vmem, hbm, hbm, vmem, vmem, smem],
            scratch=[
                pltpu.VMEM((model_width, cols), half),
                pltpu.VMEM((held, model_width), half),
                fetched,
                fetched,
            ],
        )
        own = lax.dynamic_slice_in_dim(hidden, owner * cols, cols, 1)
        return call(first_after_kernel, [state], own, exchange(sent), table, based, expand)[0]

    def nothing():
        return jnp.zeros((rows, cols), half)

    def open_first(hidden):
        table, next_table = tables(hidden[:, model_width:])
        (shrink,) = call(unused_kernel, [((all_held, cols), half)])
        return first_layer(hidden, table), table, next_table, shrink

    def open_other(hidden):
        extra = jnp.pad(info, ((0, 16 - own_rows), (0, cols - LANES)))
        (sent,) = call(pack_kernel, [((devices, held + 16, cols), half)], maps, extra)
        got = exchange(sent)
        table, next_table = tables(got[:, held : held + own_rows, :LANES].reshape(rows, LANES))
        return nothing(), table, next_table, got[:, :held].reshape(all_held, cols)

    def work(h, table, weights):
        shrink, base, expand, gain, own_gain = weights
        (sent,) = call(
            before_kernel,
            [((devices, rows + packed, cols), half)],
            h,
            table,
            own_gain,
            shrink,
            specs=[vmem, vmem, vmem, hbm],
            scratch=[pltpu.VMEM((all_held, cols), half), fetched],
        )
        return call(
            after_kernel,
            [state],
            h,
            exchange(sent),
            table,
            gain,
            base,
            expand,
            specs=[vmem, vmem, vmem, vmem, hbm, hbm],
            scratch=[
                pltpu.VMEM((model_width, cols), half),
                pltpu.VMEM((all_held, cols), half),
                fetched,
                fetched,
            ],
        )[0]

    lender = segments // 2

    def gathered(at, micro):
        shape = (rows, model_width + LANES)
        return lax.cond(
            segment == at, lambda: gather_rows(micro), lambda: jnp.zeros(shape, half)
        )

    lent = gathered(lender, 1)
    later = lax.ppermute(lent, "segment", [(lender, 0)])
    swap_base, swap_expand, lent = lax.optimization_barrier((base, expand, lent))
    other_base, other_expand = swap(swap_base), swap(swap_expand)
    hidden = gathered(0, 0)
    hidden, later, other_base = lax.optimization_barrier((hidden, later, other_base))
    h, table, next_table, shrink = lax.cond(segment == 0, open_first, open_other, hidden)
    opened = h
    h = lax.ppermute(h, "segment", [(0, 1)])
    h, swap_shrink, swap_gain = lax.optimization_barrier((h, shrink, gain))
    other_shrink, other_gain = swap(swap_shrink), swap(swap_gain)

    own_gain = lax.dynamic_slice_in_dim(gain, owner * cols, cols, 1)
    other_own_gain = lax.dynamic_slice_in_dim(other_gain, owner * cols, cols, 1)
    own = (shrink, base, expand, gain, own_gain)
    other = (other_shrink, other_base, other_expand, other_gain, other_own_gain)

    odd = lax.cond(segment == 1, lambda: work(h, table, own), nothing)
    second = lax.cond(segment == 0, lambda: first_layer(later, next_table), nothing)
    odd = lax.cond(segment == 0, lambda: work(second, next_table, other), lambda: odd)
    even = second
    h = odd
    for p in range(1, planes):
        h = lax.ppermute(h, "segment", [(2 * p - 1, 2 * p + 1), (2 * p - 2, 2 * p)])

        def core_0():
            first = work(h, next_table, own)
            return first, work(first, next_table, other)

        def core_1():
            first = work(h, table, other)
            return first, work(first, table, own)

        first, h = lax.switch(
            jnp.where(plane == p, core, 2), (core_0, core_1, lambda: (nothing(), nothing()))
        )
        even, odd = jnp.where(plane == p, first, even), jnp.where(plane == p, h, odd)

    swapped = swap(jnp.where(core == 0, odd, even))
    first = jnp.where(segment == 0, opened, jnp.where(core == 0, swapped, odd))
    return jnp.stack([first, jnp.where(core == 0, even, swapped)])[None]


def solution(mesh):
    in_specs = (
        P(None, "adapter", None),
        P(None, "adapter", None),
        P("adapter"),
        P("segment", None),
        P("segment", None, "adapter"),
        P("segment", "adapter", None, None),
        P("segment", None, None, "adapter"),
    )
    out_specs = P("segment", None, None, "adapter")
    return jax.shard_map(
        on_device, mesh=mesh, in_specs=in_specs, out_specs=out_specs, check_vma=False
    )
```

```python
import jax
import jax.numpy as jnp
from jax import lax
from jax.experimental import pallas as pl
from jax.experimental.pallas import tpu as pltpu
from jax.sharding import PartitionSpec as P

GROUP = 4
CHUNKS = 8
LANES = 128


def lane_group(shape, rank_most):
    return lax.broadcasted_iota(jnp.int32, shape, len(shape) - 1) // rank_most


def spread(value, rank_most):
    step = rank_most
    while step < value.shape[-1]:
        value = value + pltpu.roll(value, step, 1)
        step *= 2
    return value


def fold(rank_most, wide, cols):
    packed = wide.shape[0] // GROUP
    groups = lane_group((packed, cols), rank_most)
    folded = jnp.zeros((packed, cols), jnp.float32)
    for g in range(GROUP):
        folded = jnp.where(groups == g, wide[g * packed : (g + 1) * packed], folded)
    return folded.astype(jnp.bfloat16)


def unfold(rank_most, folded):
    groups = lane_group(folded.shape, rank_most)
    return jnp.concatenate(
        [spread(jnp.where(groups == g, folded, 0.0), rank_most) for g in range(GROUP)], axis=0
    )


def scaling(rank_most, rank, shape):
    place = lax.broadcasted_iota(jnp.int32, shape, 1) % rank_most
    return jnp.where(place.astype(jnp.float32) < rank, 32.0 / rank, 0.0)


def fetches(sources, target, sems, axis=0, choice=None):
    size = target.shape[axis] // CHUNKS
    parts = [(slice(None),) * axis + (pl.ds(c * size, size),) for c in range(CHUNKS)]
    every = [
        [
            pltpu.make_async_copy(source.at[part], target.at[part], sems.at[c])
            for c, part in enumerate(parts)
        ]
        for source in sources
    ]

    def start(copies):
        for copy in copies:
            copy.start()

    if choice is None:
        start(every[0])
    else:
        for number, copies in enumerate(every):
            pl.when(choice == number)(lambda copies=copies: start(copies))
    return every[0]


def inverse_rms(squares, width):
    return lax.rsqrt(jnp.sum(squares, axis=-1, keepdims=True) / width + 1e-05)


def table_kernel(rank_most, info_ref, first_ref, second_ref):
    info = info_ref[...].astype(jnp.float32)
    rows = info.shape[0]
    lane = lax.broadcasted_iota(jnp.int32, info.shape, 1)
    ranks = jnp.broadcast_to(info[:, 2:3], info.shape).astype(jnp.bfloat16)
    numbers = lax.broadcasted_iota(jnp.int32, (rows, rows), 1).astype(jnp.float32)
    for micro, ref in enumerate((first_ref, second_ref)):
        ids = info[:, micro : micro + 1]
        onehot = jnp.where(ids == numbers, 1.0, 0.0).astype(jnp.bfloat16)
        rank = jnp.dot(onehot, ranks, preferred_element_type=jnp.float32)
        ref[...] = jnp.where(lane == 0, ids, rank)


def pack_kernel(rank_most, maps_ref, info_ref, out_ref):
    held, cols = maps_ref.shape[0], out_ref.shape[2]
    for d in range(out_ref.shape[0]):
        out_ref[d, :held, :] = maps_ref[:, d * cols : (d + 1) * cols]
        out_ref[d, held:, :] = info_ref[...]


def first_kernel(
    rank_most, hidden_ref, base_hbm, maps_hbm, gain_ref, table_ref, owner_ref,
    base_out, sent_out, base_ref, maps_ref, base_sems, maps_sems,
):
    rows = hidden_ref.shape[0]
    width, cols = base_ref.shape
    held = maps_ref.shape[0]
    base_copies = fetches([base_hbm], base_ref, base_sems)
    maps_copies = fetches([maps_hbm], maps_ref, maps_sems, axis=1)
    base = jnp.zeros((rows, cols), jnp.float32)
    shrunk = jnp.zeros((rows, held), jnp.float32)
    squares = jnp.zeros((rows, cols), jnp.float32)
    steps = width // cols
    for j in range(steps):
        if j % (steps // CHUNKS) == 0:
            base_copies[j // (steps // CHUNKS)].wait()
            maps_copies[j // (steps // CHUNKS)].wait()
        part = slice(j * cols, (j + 1) * cols)
        wide = hidden_ref[:, part].astype(jnp.float32)
        squares = squares + wide * wide
        scaled = (wide * gain_ref[:, part]).astype(jnp.bfloat16)
        base = base + jnp.dot(scaled, base_ref[part, :], preferred_element_type=jnp.float32)
        shrunk = shrunk + lax.dot_general(
            scaled, maps_ref[:, part], (((1,), (1,)), ((), ())), preferred_element_type=jnp.float32
        )
    inverse = inverse_rms(squares, width)
    base_out[...] = base * inverse
    groups = lane_group((rows, held), rank_most)
    first = owner_ref[0] * (held // rank_most)
    wanted = table_ref[:, 0:1] == (first + groups).astype(jnp.float32)
    factor = scaling(rank_most, table_ref[:, 1:2], (rows, held))
    low = spread(jnp.where(wanted, shrunk * inverse * factor, 0.0), rank_most)
    folded = fold(rank_most, jnp.concatenate([low] * (cols // held), axis=1), cols)
    for d in range(sent_out.shape[0]):
        sent_out[d] = folded


def finish(rank_most, h_ref, base, low, table_ref, expand_ref, out_ref):
    rows, cols = h_ref.shape
    wanted = table_ref[:, 0:1] - lane_group((rows, cols), rank_most).astype(jnp.float32)
    added = jnp.zeros((rows, cols), jnp.float32)
    for j in range(expand_ref.shape[0] // cols):
        picked = jnp.where(wanted == j * GROUP, low, 0.0).astype(jnp.bfloat16)
        added = added + jnp.dot(
            picked, expand_ref[j * cols : (j + 1) * cols, :], preferred_element_type=jnp.float32
        )
    update = (base + added).astype(jnp.bfloat16)
    out_ref[...] = (h_ref[...].astype(jnp.float32) + update.astype(jnp.float32)).astype(
        jnp.bfloat16
    )


def first_after_kernel(rank_most, h_ref, got_ref, table_ref, base_ref, expand_ref, out_ref):
    partial = jnp.zeros(got_ref.shape[1:], jnp.float32)
    for j in range(got_ref.shape[0]):
        partial = partial + got_ref[j].astype(jnp.float32)
    low = unfold(rank_most, partial)
    finish(rank_most, h_ref, base_ref[...], low, table_ref, expand_ref, out_ref)


def before_kernel(
    rank_most, choice_ref, h_ref, table_ref, gain_ref, own_hbm, other_hbm, out_ref, shrink_ref, sems
):
    rows, cols = h_ref.shape
    copies = fetches([own_hbm, other_hbm], shrink_ref, sems, choice=choice_ref[0])
    h = h_ref[...]
    scaled = (h.astype(jnp.float32) * gain_ref[...]).astype(jnp.bfloat16)
    wanted = table_ref[:, 0:1] - lane_group((rows, cols), rank_most).astype(jnp.float32)
    total = jnp.zeros((rows, cols), jnp.float32)
    steps = shrink_ref.shape[0] // cols
    for j in range(steps):
        if j % (steps // CHUNKS) == 0:
            copies[j // (steps // CHUNKS)].wait()
        part = lax.dot_general(
            scaled,
            shrink_ref[j * cols : (j + 1) * cols, :],
            (((1,), (1,)), ((), ())),
            preferred_element_type=jnp.float32,
        )
        total = total + jnp.where(wanted == j * GROUP, part, 0.0)
    folded = fold(rank_most, spread(total, rank_most), cols)
    for d in range(out_ref.shape[0]):
        out_ref[d, :rows, :] = h
        out_ref[d, rows:, :] = folded


def after_kernel(
    rank_most, choice_ref, h_ref, got_ref, table_ref, gain_ref, own_base, other_base, own_expand, other_expand,
    out_ref, base_ref, expand_ref, base_sems, expand_sems,
):
    rows, cols = h_ref.shape
    choice = choice_ref[0]
    copies = fetches([own_base, other_base], base_ref, base_sems, choice=choice)
    expand_copies = fetches([own_expand, other_expand], expand_ref, expand_sems, choice=choice)
    sources = got_ref.shape[0]
    base = jnp.zeros((rows, cols), jnp.float32)
    squares = jnp.zeros((rows, cols), jnp.float32)
    partial = jnp.zeros((rows // GROUP, cols), jnp.float32)
    for j in range(sources):
        if j % (sources // CHUNKS) == 0:
            copies[j // (sources // CHUNKS)].wait()
        part = slice(j * cols, (j + 1) * cols)
        wide = got_ref[j, :rows, :].astype(jnp.float32)
        squares = squares + wide * wide
        scaled = (wide * gain_ref[:, part]).astype(jnp.bfloat16)
        base = base + jnp.dot(scaled, base_ref[part, :], preferred_element_type=jnp.float32)
        partial = partial + got_ref[j, rows:, :].astype(jnp.float32)
    inverse = inverse_rms(squares, sources * cols)
    factor = scaling(rank_most, table_ref[:, 1:2], (rows, cols))
    low = unfold(rank_most, partial) * inverse * factor
    for copy in expand_copies:
        copy.wait()
    finish(rank_most, h_ref, base * inverse, low, table_ref, expand_ref, out_ref)


def unused_kernel(rank_most, ref):
    ref[:16, :] = jnp.zeros((16, ref.shape[1]), ref.dtype)


def on_device(tokens, adapter_ids, ranks, gain, base_weight, shrink_weight, expand_weight):
    micro_count, own_rows, model_width = tokens.shape
    cols = base_weight.shape[2]
    ad_count, _, rank_most = shrink_weight.shape[1:]
    total_adapters = expand_weight.shape[1]
    devices = lax.axis_size("adapter")
    segments = lax.axis_size("segment")
    planes = segments // 2
    segment = lax.axis_index("segment")
    owner = lax.axis_index("adapter")
    plane, core = segment // 2, segment % 2
    rows = own_rows * devices
    packed = rows // GROUP
    held = ad_count * rank_most
    all_held = total_adapters * rank_most
    base = base_weight[0]
    expand = expand_weight[0].reshape(all_held, cols)
    maps = shrink_weight[0].transpose(0, 2, 1).reshape(held, model_width)

    half, full = jnp.bfloat16, jnp.float32
    state = ((rows, cols), half)
    vmem = pl.BlockSpec(memory_space=pltpu.VMEM)
    hbm = pl.BlockSpec(memory_space=pl.ANY)
    smem = pl.BlockSpec(memory_space=pltpu.SMEM)
    fetched = pltpu.SemaphoreType.DMA((CHUNKS,))

    def call(kernel, shapes, *operands, specs=None, scratch=()):
        return pl.pallas_call(
            lambda *refs: kernel(rank_most, *refs),
            out_shape=[jax.ShapeDtypeStruct(*shape) for shape in shapes],
            in_specs=specs or [vmem] * len(operands),
            out_specs=[vmem] * len(shapes),
            scratch_shapes=scratch,
            compiler_params=pltpu.CompilerParams(vmem_limit_bytes=14 * 1024 * 1024),
        )(*operands)

    def exchange(blocks):
        return lax.all_to_all(blocks, "adapter", 0, 0, tiled=True)

    def swap(array):
        pairs = [(s, s ^ 1) for s in range(segments)]
        return lax.ppermute(array, "segment", pairs)

    info = jnp.concatenate([adapter_ids[0], adapter_ids[1], ranks[:, None]], axis=1)
    info = jnp.pad(info.astype(half), ((0, 0), (0, LANES - info.shape[1])))

    def tables(info):
        return call(table_kernel, [((rows, LANES), full)] * 2, info)

    def gather_rows(micro, start, width):
        block = lax.dynamic_slice_in_dim(tokens[micro], start, width, 1)
        block = jnp.concatenate([block, info], axis=1)
        got = exchange(jnp.broadcast_to(block, (devices,) + block.shape))
        return got.reshape(rows, width + LANES)

    def first_layer(hidden, table):
        based, sent = call(
            first_kernel,
            [((rows, cols), full), ((devices, packed, cols), half)],
            hidden,
            base,
            maps,
            gain,
            table,
            owner.astype(jnp.int32).reshape(1),
            specs=[vmem, hbm, hbm, vmem, vmem, smem],
            scratch=[
                pltpu.VMEM((model_width, cols), half),
                pltpu.VMEM((held, model_width), half),
                fetched,
                fetched,
            ],
        )
        own = lax.dynamic_slice_in_dim(hidden, owner * cols, cols, 1)
        return call(first_after_kernel, [state], own, exchange(sent), table, based, expand)[0]

    def nothing():
        return jnp.zeros((rows, cols), half)

    def open_first(hidden):
        table, next_table = tables(hidden[:, model_width:])
        (shrink,) = call(unused_kernel, [((all_held, cols), half)])
        return first_layer(hidden, table), table, next_table, shrink

    def open_other(hidden):
        extra = jnp.pad(info, ((0, 16 - own_rows), (0, cols - LANES)))
        (sent,) = call(pack_kernel, [((devices, held + 16, cols), half)], maps, extra)
        got = exchange(sent)
        table, next_table = tables(got[:, held : held + own_rows, :LANES].reshape(rows, LANES))
        return nothing(), table, next_table, got[:, :held].reshape(all_held, cols)

    def work(h, parity, table, weights):
        (shrink, base, expand), (other_shrink, other_base, other_expand), gains, own_gains = weights
        choice = ((core + parity) % 2).astype(jnp.int32).reshape(1)
        (sent,) = call(
            before_kernel,
            [((devices, rows + packed, cols), half)],
            choice,
            h,
            table,
            own_gains[parity],
            shrink,
            other_shrink,
            specs=[smem, vmem, vmem, vmem, hbm, hbm],
            scratch=[pltpu.VMEM((all_held, cols), half), fetched],
        )
        return call(
            after_kernel,
            [state],
            choice,
            h,
            exchange(sent),
            table,
            gains[parity],
            base,
            other_base,
            expand,
            other_expand,
            specs=[smem, vmem, vmem, vmem, vmem, hbm, hbm, hbm, hbm],
            scratch=[
                pltpu.VMEM((model_width, cols), half),
                pltpu.VMEM((all_held, cols), half),
                fetched,
                fetched,
            ],
        )[0]

    width = model_width // 2
    lenders = (segments - 4, segments - 2)
    lent = lax.cond(
        (segment == lenders[0]) | (segment == lenders[1]),
        lambda: gather_rows(1, jnp.where(segment == lenders[0], 0, width), width),
        lambda: jnp.zeros((rows, width + LANES), half),
    )
    halves = [lax.ppermute(lent, "segment", [(lender, 0)]) for lender in lenders]
    swap_base, swap_expand, lent = lax.optimization_barrier((base, expand, lent))
    other_base, other_expand = swap(swap_base), swap(swap_expand)
    hidden = lax.cond(
        segment == 0,
        lambda: gather_rows(0, 0, model_width),
        lambda: jnp.zeros((rows, model_width + LANES), half),
    )
    hidden, halves, other_base, other_expand = lax.optimization_barrier(
        (hidden, halves, other_base, other_expand)
    )
    h, table, next_table, shrink = lax.cond(segment == 0, open_first, open_other, hidden)
    opened = h
    h = lax.ppermute(h, "segment", [(0, 1)])
    h, swap_shrink, swap_gain = lax.optimization_barrier((h, shrink, gain))
    other_shrink, other_gain = swap(swap_shrink), swap(swap_gain)

    def second_first():
        later = jnp.concatenate([halves[0][:, :width], halves[1]], axis=1)
        return first_layer(later, next_table)

    second = lax.cond(segment == 0, second_first, nothing)
    others = other_shrink, other_base, other_expand
    gains = (jnp.where(core == 0, gain, other_gain), jnp.where(core == 0, other_gain, gain))
    own_gains = [lax.dynamic_slice_in_dim(row, owner * cols, cols, 1) for row in gains]
    weights = (shrink, base, expand), others, gains, own_gains

    table = jnp.where(core == 0, next_table, table)
    h = jnp.where(core == 0, second, h)
    odd = lax.cond(plane == 0, lambda: work(h, 1, table, weights), nothing)
    to_next = [(s, s + 2) for s in range(segments - 2)]

    def next_plane(p, carry):
        h, even, odd = carry
        h = lax.ppermute(h, "segment", to_next)

        def both():
            first = work(h, 0, table, weights)
            return first, work(first, 1, table, weights)

        first, h = lax.cond(plane == p, both, lambda: (nothing(), nothing()))
        return h, jnp.where(plane == p, first, even), jnp.where(plane == p, h, odd)

    _, even, odd = lax.fori_loop(1, planes, next_plane, (odd, second, odd))

    swapped = swap(jnp.where(core == 0, odd, even))
    first = jnp.where(segment == 0, opened, jnp.where(core == 0, swapped, odd))
    return jnp.stack([first, jnp.where(core == 0, even, swapped)])[None]


def solution(mesh):
    in_specs = (
        P(None, "adapter", None),
        P(None, "adapter", None),
        P("adapter"),
        P("segment", None),
        P("segment", None, "adapter"),
        P("segment", "adapter", None, None),
        P("segment", None, None, "adapter"),
    )
    out_specs = P("segment", None, None, "adapter")
    return jax.shard_map(
        on_device, mesh=mesh, in_specs=in_specs, out_specs=out_specs, check_vma=False
    )
```

```python
import jax
import jax.numpy as jnp
from jax import lax
from jax.experimental import pallas as pl
from jax.experimental.pallas import tpu as pltpu
from jax.sharding import PartitionSpec as P

GROUP = 4
CHUNKS = 8
LANES = 128


def lane_group(shape, rank_most):
    return lax.broadcasted_iota(jnp.int32, shape, len(shape) - 1) // rank_most


def spread(value, rank_most):
    step = rank_most
    while step < value.shape[-1]:
        value = value + pltpu.roll(value, step, 1)
        step *= 2
    return value


def fold(rank_most, wide, cols):
    packed = wide.shape[0] // GROUP
    groups = lane_group((packed, cols), rank_most)
    folded = jnp.zeros((packed, cols), jnp.float32)
    for g in range(GROUP):
        folded = jnp.where(groups == g, wide[g * packed : (g + 1) * packed], folded)
    return folded.astype(jnp.bfloat16)


def unfold(rank_most, folded):
    groups = lane_group(folded.shape, rank_most)
    return jnp.concatenate(
        [spread(jnp.where(groups == g, folded, 0.0), rank_most) for g in range(GROUP)], axis=0
    )


def scaling(rank_most, rank, shape):
    place = lax.broadcasted_iota(jnp.int32, shape, 1) % rank_most
    return jnp.where(place.astype(jnp.float32) < rank, 32.0 / rank, 0.0)


def fetches(source, target, sems, axis=0):
    size = source.shape[axis] // CHUNKS
    copies = []
    for c in range(CHUNKS):
        part = (slice(None),) * axis + (pl.ds(c * size, size),)
        copies.append(pltpu.make_async_copy(source.at[part], target.at[part], sems.at[c]))
    for copy in copies:
        copy.start()
    return copies


def inverse_rms(squares, width):
    return lax.rsqrt(jnp.sum(squares, axis=-1, keepdims=True) / width + 1e-05)


def table_kernel(rank_most, info_ref, table_ref):
    info = info_ref[...].astype(jnp.float32)
    rows = info.shape[0]
    lane = lax.broadcasted_iota(jnp.int32, info.shape, 1)
    ranks = jnp.broadcast_to(info[:, 2:3], info.shape).astype(jnp.bfloat16)
    numbers = lax.broadcasted_iota(jnp.int32, (rows, rows), 1).astype(jnp.float32)
    table = jnp.zeros(info.shape, jnp.float32)
    for micro in range(2):
        ids = info[:, micro : micro + 1]
        onehot = jnp.where(ids == numbers, 1.0, 0.0).astype(jnp.bfloat16)
        rank = jnp.dot(onehot, ranks, preferred_element_type=jnp.float32)
        table = jnp.where(lane == 2 * micro, ids, table)
        table = jnp.where(lane == 2 * micro + 1, rank, table)
    table_ref[...] = table


def ids_and_rank(table_ref, micro_ref):
    table = table_ref[...]
    first = micro_ref[0] == 0
    return (
        jnp.where(first, table[:, 0:1], table[:, 2:3]),
        jnp.where(first, table[:, 1:2], table[:, 3:4]),
    )


def first_kernel(
    rank_most, hidden_ref, base_hbm, maps_hbm, gain_ref, table_ref, micro_ref, owner_ref, order_hbm,
    base_out, sent_out, base_ref, maps_ref, base_sems, maps_sems,
):
    rows = hidden_ref.shape[0]
    width, cols = base_ref.shape
    held = maps_ref.shape[0]
    base_copies = fetches(base_hbm, base_ref, base_sems)
    maps_copies = fetches(maps_hbm, maps_ref, maps_sems, axis=1)
    base = jnp.zeros((rows, cols), jnp.float32)
    shrunk = jnp.zeros((rows, held), jnp.float32)
    squares = jnp.zeros((rows, cols), jnp.float32)
    steps = width // cols
    for j in range(steps):
        if j % (steps // CHUNKS) == 0:
            base_copies[j // (steps // CHUNKS)].wait()
            maps_copies[j // (steps // CHUNKS)].wait()
        part = slice(j * cols, (j + 1) * cols)
        wide = hidden_ref[:, part].astype(jnp.float32)
        squares = squares + wide * wide
        scaled = (wide * gain_ref[:, part]).astype(jnp.bfloat16)
        base = base + jnp.dot(scaled, base_ref[part, :], preferred_element_type=jnp.float32)
        shrunk = shrunk + lax.dot_general(
            scaled, maps_ref[:, part], (((1,), (1,)), ((), ())), preferred_element_type=jnp.float32
        )
    inverse = inverse_rms(squares, width)
    base_out[...] = base * inverse
    groups = lane_group((rows, held), rank_most)
    first = owner_ref[0] * (held // rank_most)
    ids, rank = ids_and_rank(table_ref, micro_ref)
    wanted = ids == (first + groups).astype(jnp.float32)
    factor = scaling(rank_most, rank, (rows, held))
    low = spread(jnp.where(wanted, shrunk * inverse * factor, 0.0), rank_most)
    sent_out[...] = fold(rank_most, jnp.concatenate([low] * (cols // held), axis=1), cols)


def finish(rank_most, h_ref, base, low, ids, expand_ref, out_ref):
    rows, cols = h_ref.shape
    wanted = ids - lane_group((rows, cols), rank_most).astype(jnp.float32)
    added = jnp.zeros((rows, cols), jnp.float32)
    for j in range(expand_ref.shape[0] // cols):
        picked = jnp.where(wanted == j * GROUP, low, 0.0).astype(jnp.bfloat16)
        added = added + jnp.dot(
            picked, expand_ref[j * cols : (j + 1) * cols, :], preferred_element_type=jnp.float32
        )
    update = (base + added).astype(jnp.bfloat16)
    out_ref[...] = (h_ref[...].astype(jnp.float32) + update.astype(jnp.float32)).astype(
        jnp.bfloat16
    )


def first_after_kernel(
    rank_most, h_ref, got_ref, table_ref, micro_ref, base_ref, expand_ref, out_ref
):
    partial = jnp.zeros(got_ref.shape[1:], jnp.float32)
    for j in range(got_ref.shape[0]):
        partial = partial + got_ref[j].astype(jnp.float32)
    low = unfold(rank_most, partial)
    ids, _ = ids_and_rank(table_ref, micro_ref)
    finish(rank_most, h_ref, base_ref[...], low, ids, expand_ref, out_ref)


def before_kernel(
    rank_most, h_ref, table_ref, micro_ref, shrink_hbm, out_ref, shrink_ref, sems
):
    rows, cols = h_ref.shape
    copies = fetches(shrink_hbm, shrink_ref, sems)
    h = h_ref[...]
    ids, _ = ids_and_rank(table_ref, micro_ref)
    wanted = ids - lane_group((rows, cols), rank_most).astype(jnp.float32)
    total = jnp.zeros((rows, cols), jnp.float32)
    steps = shrink_ref.shape[0] // cols
    for j in range(steps):
        if j % (steps // CHUNKS) == 0:
            copies[j // (steps // CHUNKS)].wait()
        part = lax.dot_general(
            h,
            shrink_ref[j * cols : (j + 1) * cols, :],
            (((1,), (1,)), ((), ())),
            preferred_element_type=jnp.float32,
        )
        total = total + jnp.where(wanted == j * GROUP, part, 0.0)
    out_ref[:rows, :] = h
    out_ref[rows:, :] = fold(rank_most, spread(total, rank_most), cols)


def after_kernel(
    rank_most, h_ref, got_ref, table_ref, micro_ref, base_hbm, expand_ref, out_ref, base_ref, sems
):
    rows, cols = h_ref.shape
    copies = fetches(base_hbm, base_ref, sems)
    sources = got_ref.shape[0]
    base = jnp.zeros((rows, cols), jnp.float32)
    squares = jnp.zeros((rows, cols), jnp.float32)
    partial = jnp.zeros((rows // GROUP, cols), jnp.float32)
    for j in range(sources):
        if j % (sources // CHUNKS) == 0:
            copies[j // (sources // CHUNKS)].wait()
        block = got_ref[j, :rows, :]
        base = base + jnp.dot(
            block, base_ref[j * cols : (j + 1) * cols, :], preferred_element_type=jnp.float32
        )
        wide = block.astype(jnp.float32)
        squares = squares + wide * wide
        partial = partial + got_ref[j, rows:, :].astype(jnp.float32)
    inverse = inverse_rms(squares, sources * cols)
    ids, rank = ids_and_rank(table_ref, micro_ref)
    low = unfold(rank_most, partial) * inverse * scaling(rank_most, rank, (rows, cols))
    finish(rank_most, h_ref, base * inverse, low, ids, expand_ref, out_ref)


def unused_kernel(rank_most, *refs):
    for ref in refs:
        ref[:16, :] = jnp.zeros((16, ref.shape[1]), ref.dtype)


def on_device(tokens, adapter_ids, ranks, gain, base_weight, shrink_weight, expand_weight):
    micro_count, own_rows, model_width = tokens.shape
    cols = base_weight.shape[2]
    ad_count, _, rank_most = shrink_weight.shape[1:]
    total_adapters = expand_weight.shape[1]
    devices = lax.axis_size("adapter")
    segments = lax.axis_size("segment")
    segment = lax.axis_index("segment")
    owner = lax.axis_index("adapter")
    rows = own_rows * devices
    packed = rows // GROUP
    held = ad_count * rank_most
    all_held = total_adapters * rank_most
    gain_row = gain[0]
    expand = expand_weight[0].reshape(all_held, cols)
    maps = shrink_weight[0].transpose(0, 2, 1).reshape(held, model_width)

    half, full = jnp.bfloat16, jnp.float32
    state = ((rows, cols), half)
    vmem = pl.BlockSpec(memory_space=pltpu.VMEM)
    hbm = pl.BlockSpec(memory_space=pl.ANY)
    smem = pl.BlockSpec(memory_space=pltpu.SMEM)
    fetched = pltpu.SemaphoreType.DMA((CHUNKS,))

    def call(kernel, shapes, *operands, specs=None, scratch=()):
        return pl.pallas_call(
            lambda *refs: kernel(rank_most, *refs),
            out_shape=[jax.ShapeDtypeStruct(*shape) for shape in shapes],
            in_specs=specs or [vmem] * len(operands),
            out_specs=[vmem] * len(shapes),
            scratch_shapes=scratch,
            compiler_params=pltpu.CompilerParams(vmem_limit_bytes=14 * 1024 * 1024),
        )(*operands)

    def exchange(blocks):
        return lax.all_to_all(blocks, "adapter", 0, 0, tiled=True)

    def gather(block):
        return exchange(jnp.broadcast_to(block, (devices,) + block.shape))

    info = jnp.concatenate([adapter_ids[0], adapter_ids[1], ranks[:, None]], axis=1)
    info = jnp.pad(info.astype(half), ((0, 0), (0, LANES - info.shape[1])))

    def tables(info):
        return call(table_kernel, [((rows, LANES), full)], info)[0]

    def number(value):
        return jnp.asarray(value, jnp.int32).reshape(1)

    def gather_rows(micro):
        block = jnp.concatenate([tokens[micro], info], axis=1)
        return gather(block).reshape(rows, model_width + LANES)

    def first_layer(hidden, table, micro, order):
        base, sent = call(
            first_kernel,
            [((rows, cols), full), ((packed, cols), half)],
            hidden,
            base_weight[0],
            maps,
            gain,
            table,
            micro,
            number(owner),
            order,
            specs=[vmem, hbm, hbm, vmem, vmem, smem, smem, hbm],
            scratch=[
                pltpu.VMEM((model_width, cols), half),
                pltpu.VMEM((held, model_width), half),
                fetched,
                fetched,
            ],
        )
        own = lax.dynamic_slice_in_dim(hidden, owner * cols, cols, 1)
        return call(
            first_after_kernel,
            [state],
            own,
            gather(sent),
            table,
            micro,
            base,
            expand,
            specs=[vmem, vmem, vmem, smem, vmem, vmem],
        )[0]

    def open_first(hidden):
        table = tables(hidden[:, model_width:])
        h = first_layer(hidden, table, number(0), hidden)
        shrink, base = call(
            unused_kernel, [((all_held, cols), half), ((model_width, cols), half)]
        )
        return h, table, shrink, base

    def open_other(hidden):
        by_dest = shrink_weight[0].reshape(ad_count, devices, cols, rank_most)
        by_dest = by_dest.transpose(1, 0, 3, 2).reshape(devices, held, cols)
        extra = jnp.pad(info, ((0, 16 - own_rows), (0, cols - LANES)))
        extra = jnp.broadcast_to(extra, (devices, 16, cols))
        got = exchange(jnp.concatenate([by_dest, extra], axis=1))
        base = (base_weight[0].astype(full) * gain_row[:, None]).astype(half)
        table = tables(got[:, held : held + own_rows, :LANES].reshape(rows, LANES))
        shrink = got[:, :held].reshape(all_held, cols)
        own_gain = lax.dynamic_slice_in_dim(gain_row, owner * cols, cols, 0)
        shrink = (shrink.astype(full) * own_gain[None, :]).astype(half)
        return jnp.zeros((rows, cols), half), table, shrink, base

    block_shape = (devices, rows + packed, cols)

    def spread_out(h, table, micro, shrink):
        (sent,) = call(
            before_kernel,
            [((rows + packed, cols), half)],
            h,
            table,
            micro,
            shrink,
            specs=[vmem, vmem, smem, hbm],
            scratch=[pltpu.VMEM((all_held, cols), half), fetched],
        )
        return gather(sent)

    def project(h, got, table, micro, base):
        return call(
            after_kernel,
            [state],
            h,
            got,
            table,
            micro,
            base,
            expand,
            specs=[vmem, vmem, vmem, smem, hbm, vmem],
            scratch=[pltpu.VMEM((model_width, cols), half), fetched],
        )[0]

    def nothing():
        return jnp.zeros((rows, cols), half)

    hidden = lax.cond(
        segment == 0,
        lambda: gather_rows(0),
        lambda: lax.cond(
            segment == 2,
            lambda: gather_rows(1),
            lambda: jnp.zeros((rows, model_width + LANES), half),
        ),
    )
    later = lax.ppermute(hidden, "segment", [(2, 0)])
    h, table, shrink, base = lax.cond(segment == 0, open_first, open_other, hidden)
    outs = [h, h]
    for stage in range(1, segments + 1):
        pairs = [(s, s + 1) for s in (stage - 1, stage - 2) if 0 <= s < segments - 1]
        h = lax.ppermute(h, "segment", pairs)
        leads, trails = segment == stage, segment == stage - 1
        now = number(jnp.where(leads, 0, 1))
        if stage == 1:
            got = lax.cond(
                leads,
                lambda: spread_out(h, table, now, shrink),
                lambda: jnp.zeros(block_shape, half),
            )
            over = lax.ppermute(got[0, :16, :LANES], "segment", [(1, 0)])
            branch = jnp.where(trails, 2, jnp.where(leads, 1, 0))
            h = lax.switch(
                branch,
                (nothing, lambda: project(h, got, table, now, base), lambda: first_layer(later, table, now, over)),
            )
        else:
            h = lax.cond(
                leads | trails,
                lambda: project(h, spread_out(h, table, now, shrink), table, now, base),
                nothing,
            )
        outs = [jnp.where(leads, h, outs[0]), jnp.where(trails, h, outs[1])]
    return jnp.stack(outs)[None]


def solution(mesh):
    in_specs = (
        P(None, "adapter", None),
        P(None, "adapter", None),
        P("adapter"),
        P("segment", None),
        P("segment", None, "adapter"),
        P("segment", "adapter", None, None),
        P("segment", None, None, "adapter"),
    )
    out_specs = P("segment", None, None, "adapter")
    return jax.shard_map(
        on_device, mesh=mesh, in_specs=in_specs, out_specs=out_specs, check_vma=False
    )
```

```python
import jax
import jax.numpy as jnp
from jax import lax
from jax.experimental import pallas as pl
from jax.experimental.pallas import tpu as pltpu
from jax.sharding import PartitionSpec as P

GROUP = 4
CHUNKS = 8
LANES = 128


def lane_group(shape, rank_most):
    return lax.broadcasted_iota(jnp.int32, shape, len(shape) - 1) // rank_most


def spread(value, rank_most):
    step = rank_most
    while step < value.shape[-1]:
        value = value + pltpu.roll(value, step, 1)
        step *= 2
    return value


def fold(rank_most, wide, cols):
    packed = wide.shape[0] // GROUP
    groups = lane_group((packed, cols), rank_most)
    folded = jnp.zeros((packed, cols), jnp.float32)
    for g in range(GROUP):
        folded = jnp.where(groups == g, wide[g * packed : (g + 1) * packed], folded)
    return folded.astype(jnp.bfloat16)


def unfold(rank_most, folded):
    groups = lane_group(folded.shape, rank_most)
    return jnp.concatenate(
        [spread(jnp.where(groups == g, folded, 0.0), rank_most) for g in range(GROUP)], axis=0
    )


def scaling(rank_most, rank, shape):
    place = lax.broadcasted_iota(jnp.int32, shape, 1) % rank_most
    return jnp.where(place.astype(jnp.float32) < rank, 32.0 / rank, 0.0)


def fetches(source, target, sems, axis=0):
    size = source.shape[axis] // CHUNKS
    copies = []
    for c in range(CHUNKS):
        part = (slice(None),) * axis + (pl.ds(c * size, size),)
        copies.append(pltpu.make_async_copy(source.at[part], target.at[part], sems.at[c]))
    for copy in copies:
        copy.start()
    return copies


def inverse_rms(squares, width):
    return lax.rsqrt(jnp.sum(squares, axis=-1, keepdims=True) / width + 1e-05)


def table_kernel(rank_most, info_ref, first_ref, second_ref):
    info = info_ref[...].astype(jnp.float32)
    rows = info.shape[0]
    lane = lax.broadcasted_iota(jnp.int32, info.shape, 1)
    ranks = jnp.broadcast_to(info[:, 2:3], info.shape).astype(jnp.bfloat16)
    numbers = lax.broadcasted_iota(jnp.int32, (rows, rows), 1).astype(jnp.float32)
    for micro, ref in enumerate((first_ref, second_ref)):
        ids = info[:, micro : micro + 1]
        onehot = jnp.where(ids == numbers, 1.0, 0.0).astype(jnp.bfloat16)
        rank = jnp.dot(onehot, ranks, preferred_element_type=jnp.float32)
        ref[...] = jnp.where(lane == 0, ids, rank)


def ids_and_rank(table_ref):
    return table_ref[:, 0:1], table_ref[:, 1:2]


def first_kernel(
    rank_most, hidden_ref, base_hbm, maps_hbm, gain_ref, table_ref, owner_ref, order_hbm,
    base_out, sent_out, base_ref, maps_ref, base_sems, maps_sems,
):
    rows = hidden_ref.shape[0]
    width, cols = base_ref.shape
    held = maps_ref.shape[0]
    base_copies = fetches(base_hbm, base_ref, base_sems)
    maps_copies = fetches(maps_hbm, maps_ref, maps_sems, axis=1)
    base = jnp.zeros((rows, cols), jnp.float32)
    shrunk = jnp.zeros((rows, held), jnp.float32)
    squares = jnp.zeros((rows, cols), jnp.float32)
    steps = width // cols
    for j in range(steps):
        if j % (steps // CHUNKS) == 0:
            base_copies[j // (steps // CHUNKS)].wait()
            maps_copies[j // (steps // CHUNKS)].wait()
        part = slice(j * cols, (j + 1) * cols)
        wide = hidden_ref[:, part].astype(jnp.float32)
        squares = squares + wide * wide
        scaled = (wide * gain_ref[:, part]).astype(jnp.bfloat16)
        base = base + jnp.dot(scaled, base_ref[part, :], preferred_element_type=jnp.float32)
        shrunk = shrunk + lax.dot_general(
            scaled, maps_ref[:, part], (((1,), (1,)), ((), ())), preferred_element_type=jnp.float32
        )
    inverse = inverse_rms(squares, width)
    base_out[...] = base * inverse
    groups = lane_group((rows, held), rank_most)
    first = owner_ref[0] * (held // rank_most)
    ids, rank = ids_and_rank(table_ref)
    wanted = ids == (first + groups).astype(jnp.float32)
    factor = scaling(rank_most, rank, (rows, held))
    low = spread(jnp.where(wanted, shrunk * inverse * factor, 0.0), rank_most)
    sent_out[...] = fold(rank_most, jnp.concatenate([low] * (cols // held), axis=1), cols)


def finish(rank_most, h_ref, base, low, ids, expand_ref, out_ref):
    rows, cols = h_ref.shape
    wanted = ids - lane_group((rows, cols), rank_most).astype(jnp.float32)
    added = jnp.zeros((rows, cols), jnp.float32)
    for j in range(expand_ref.shape[0] // cols):
        picked = jnp.where(wanted == j * GROUP, low, 0.0).astype(jnp.bfloat16)
        added = added + jnp.dot(
            picked, expand_ref[j * cols : (j + 1) * cols, :], preferred_element_type=jnp.float32
        )
    update = (base + added).astype(jnp.bfloat16)
    out_ref[...] = (h_ref[...].astype(jnp.float32) + update.astype(jnp.float32)).astype(
        jnp.bfloat16
    )


def first_after_kernel(
    rank_most, h_ref, got_ref, table_ref, base_ref, expand_ref, out_ref
):
    partial = jnp.zeros(got_ref.shape[1:], jnp.float32)
    for j in range(got_ref.shape[0]):
        partial = partial + got_ref[j].astype(jnp.float32)
    low = unfold(rank_most, partial)
    ids, _ = ids_and_rank(table_ref)
    finish(rank_most, h_ref, base_ref[...], low, ids, expand_ref, out_ref)


def before_kernel(
    rank_most, h_ref, table_ref, shrink_hbm, out_ref, shrink_ref, sems
):
    rows, cols = h_ref.shape
    copies = fetches(shrink_hbm, shrink_ref, sems)
    h = h_ref[...]
    ids, _ = ids_and_rank(table_ref)
    wanted = ids - lane_group((rows, cols), rank_most).astype(jnp.float32)
    total = jnp.zeros((rows, cols), jnp.float32)
    steps = shrink_ref.shape[0] // cols
    for j in range(steps):
        if j % (steps // CHUNKS) == 0:
            copies[j // (steps // CHUNKS)].wait()
        part = lax.dot_general(
            h,
            shrink_ref[j * cols : (j + 1) * cols, :],
            (((1,), (1,)), ((), ())),
            preferred_element_type=jnp.float32,
        )
        total = total + jnp.where(wanted == j * GROUP, part, 0.0)
    out_ref[:rows, :] = h
    out_ref[rows:, :] = fold(rank_most, spread(total, rank_most), cols)


def after_kernel(
    rank_most, h_ref, got_ref, table_ref, base_hbm, expand_ref, out_ref, base_ref, sems
):
    rows, cols = h_ref.shape
    copies = fetches(base_hbm, base_ref, sems)
    sources = got_ref.shape[0]
    base = jnp.zeros((rows, cols), jnp.float32)
    squares = jnp.zeros((rows, cols), jnp.float32)
    partial = jnp.zeros((rows // GROUP, cols), jnp.float32)
    for j in range(sources):
        if j % (sources // CHUNKS) == 0:
            copies[j // (sources // CHUNKS)].wait()
        block = got_ref[j, :rows, :]
        base = base + jnp.dot(
            block, base_ref[j * cols : (j + 1) * cols, :], preferred_element_type=jnp.float32
        )
        wide = block.astype(jnp.float32)
        squares = squares + wide * wide
        partial = partial + got_ref[j, rows:, :].astype(jnp.float32)
    inverse = inverse_rms(squares, sources * cols)
    ids, rank = ids_and_rank(table_ref)
    low = unfold(rank_most, partial) * inverse * scaling(rank_most, rank, (rows, cols))
    finish(rank_most, h_ref, base * inverse, low, ids, expand_ref, out_ref)


def unused_kernel(rank_most, *refs):
    for ref in refs:
        ref[:16, :] = jnp.zeros((16, ref.shape[1]), ref.dtype)


def on_device(tokens, adapter_ids, ranks, gain, base_weight, shrink_weight, expand_weight):
    micro_count, own_rows, model_width = tokens.shape
    cols = base_weight.shape[2]
    ad_count, _, rank_most = shrink_weight.shape[1:]
    total_adapters = expand_weight.shape[1]
    devices = lax.axis_size("adapter")
    segments = lax.axis_size("segment")
    segment = lax.axis_index("segment")
    owner = lax.axis_index("adapter")
    rows = own_rows * devices
    packed = rows // GROUP
    held = ad_count * rank_most
    all_held = total_adapters * rank_most
    gain_row = gain[0]
    expand = expand_weight[0].reshape(all_held, cols)
    maps = shrink_weight[0].transpose(0, 2, 1).reshape(held, model_width)

    half, full = jnp.bfloat16, jnp.float32
    state = ((rows, cols), half)
    vmem = pl.BlockSpec(memory_space=pltpu.VMEM)
    hbm = pl.BlockSpec(memory_space=pl.ANY)
    smem = pl.BlockSpec(memory_space=pltpu.SMEM)
    fetched = pltpu.SemaphoreType.DMA((CHUNKS,))

    def call(kernel, shapes, *operands, specs=None, scratch=()):
        return pl.pallas_call(
            lambda *refs: kernel(rank_most, *refs),
            out_shape=[jax.ShapeDtypeStruct(*shape) for shape in shapes],
            in_specs=specs or [vmem] * len(operands),
            out_specs=[vmem] * len(shapes),
            scratch_shapes=scratch,
            compiler_params=pltpu.CompilerParams(vmem_limit_bytes=14 * 1024 * 1024),
        )(*operands)

    def exchange(blocks):
        return lax.all_to_all(blocks, "adapter", 0, 0, tiled=True)

    def gather(block):
        return exchange(jnp.broadcast_to(block, (devices,) + block.shape))

    info = jnp.concatenate([adapter_ids[0], adapter_ids[1], ranks[:, None]], axis=1)
    info = jnp.pad(info.astype(half), ((0, 0), (0, LANES - info.shape[1])))

    def tables(info):
        return call(table_kernel, [((rows, LANES), full)] * 2, info)

    def number(value):
        return jnp.asarray(value, jnp.int32).reshape(1)

    def gather_rows(micro):
        block = jnp.concatenate([tokens[micro], info], axis=1)
        return gather(block).reshape(rows, model_width + LANES)

    def first_layer(hidden, table, order):
        base, sent = call(
            first_kernel,
            [((rows, cols), full), ((packed, cols), half)],
            hidden,
            base_weight[0],
            maps,
            gain,
            table,
            number(owner),
            order,
            specs=[vmem, hbm, hbm, vmem, vmem, smem, hbm],
            scratch=[
                pltpu.VMEM((model_width, cols), half),
                pltpu.VMEM((held, model_width), half),
                fetched,
                fetched,
            ],
        )
        own = lax.dynamic_slice_in_dim(hidden, owner * cols, cols, 1)
        return call(
            first_after_kernel,
            [state],
            own,
            gather(sent),
            table,
            base,
            expand,
        )[0]

    def open_first(hidden):
        table, next_table = tables(hidden[:, model_width:])
        h = first_layer(hidden, table, hidden)
        shrink, base = call(
            unused_kernel, [((all_held, cols), half), ((model_width, cols), half)]
        )
        return h, table, next_table, shrink, base

    def open_other(hidden):
        by_dest = shrink_weight[0].reshape(ad_count, devices, cols, rank_most)
        by_dest = by_dest.transpose(1, 0, 3, 2).reshape(devices, held, cols)
        extra = jnp.pad(info, ((0, 16 - own_rows), (0, cols - LANES)))
        extra = jnp.broadcast_to(extra, (devices, 16, cols))
        got = exchange(jnp.concatenate([by_dest, extra], axis=1))
        base = (base_weight[0].astype(full) * gain_row[:, None]).astype(half)
        table, next_table = tables(got[:, held : held + own_rows, :LANES].reshape(rows, LANES))
        shrink = got[:, :held].reshape(all_held, cols)
        own_gain = lax.dynamic_slice_in_dim(gain_row, owner * cols, cols, 0)
        shrink = (shrink.astype(full) * own_gain[None, :]).astype(half)
        return jnp.zeros((rows, cols), half), table, next_table, shrink, base

    block_shape = (devices, rows + packed, cols)

    def spread_out(h, table, shrink):
        (sent,) = call(
            before_kernel,
            [((rows + packed, cols), half)],
            h,
            table,
            shrink,
            specs=[vmem, vmem, hbm],
            scratch=[pltpu.VMEM((all_held, cols), half), fetched],
        )
        return gather(sent)

    def project(h, got, table, base):
        return call(
            after_kernel,
            [state],
            h,
            got,
            table,
            base,
            expand,
            specs=[vmem, vmem, vmem, hbm, vmem],
            scratch=[pltpu.VMEM((model_width, cols), half), fetched],
        )[0]

    def nothing():
        return jnp.zeros((rows, cols), half)

    hidden = lax.cond(
        segment == 0,
        lambda: gather_rows(0),
        lambda: lax.cond(
            segment == 2,
            lambda: gather_rows(1),
            lambda: jnp.zeros((rows, model_width + LANES), half),
        ),
    )
    later = lax.ppermute(hidden, "segment", [(2, 0)])
    h, table, next_table, shrink, base = lax.cond(segment == 0, open_first, open_other, hidden)
    outs = [h, h]
    for stage in range(1, segments + 1):
        pairs = [(s, s + 1) for s in (stage - 1, stage - 2) if 0 <= s < segments - 1]
        h = lax.ppermute(h, "segment", pairs)
        leads, trails = segment == stage, segment == stage - 1
        now = lax.optimization_barrier(jnp.where(leads, table, next_table))
        if stage == 1:
            got = lax.cond(
                leads,
                lambda: spread_out(h, now, shrink),
                lambda: jnp.zeros(block_shape, half),
            )
            over = lax.ppermute(got[0, :16, :LANES], "segment", [(1, 0)])
            branch = jnp.where(trails, 2, jnp.where(leads, 1, 0))
            h = lax.switch(
                branch,
                (nothing, lambda: project(h, got, now, base), lambda: first_layer(later, now, over)),
            )
        else:
            h = lax.cond(
                leads | trails,
                lambda: project(h, spread_out(h, now, shrink), now, base),
                nothing,
            )
        outs = [jnp.where(leads, h, outs[0]), jnp.where(trails, h, outs[1])]
    return jnp.stack(outs)[None]


def solution(mesh):
    in_specs = (
        P(None, "adapter", None),
        P(None, "adapter", None),
        P("adapter"),
        P("segment", None),
        P("segment", None, "adapter"),
        P("segment", "adapter", None, None),
        P("segment", None, None, "adapter"),
    )
    out_specs = P("segment", None, None, "adapter")
    return jax.shard_map(
        on_device, mesh=mesh, in_specs=in_specs, out_specs=out_specs, check_vma=False
    )
```

```python
import jax
import jax.numpy as jnp
from jax import lax
from jax.experimental import pallas as pl
from jax.experimental.pallas import tpu as pltpu
from jax.sharding import PartitionSpec as P

GROUP = 4
CHUNKS = 8
LANES = 128


def lane_group(shape, rank_most):
    return lax.broadcasted_iota(jnp.int32, shape, len(shape) - 1) // rank_most


def spread(value, rank_most):
    step = rank_most
    while step < value.shape[-1]:
        value = value + pltpu.roll(value, step, 1)
        step *= 2
    return value


def fold(rank_most, wide, cols):
    packed = wide.shape[0] // GROUP
    groups = lane_group((packed, cols), rank_most)
    folded = jnp.zeros((packed, cols), jnp.float32)
    for g in range(GROUP):
        folded = jnp.where(groups == g, wide[g * packed : (g + 1) * packed], folded)
    return folded.astype(jnp.bfloat16)


def unfold(rank_most, folded):
    groups = lane_group(folded.shape, rank_most)
    return jnp.concatenate(
        [spread(jnp.where(groups == g, folded, 0.0), rank_most) for g in range(GROUP)], axis=0
    )


def scaling(rank_most, rank, shape):
    place = lax.broadcasted_iota(jnp.int32, shape, 1) % rank_most
    return jnp.where(place.astype(jnp.float32) < rank, 32.0 / rank, 0.0)


def fetches(source, target, sems, axis=0):
    pieces = sems.shape[0]
    size = source.shape[axis] // pieces
    copies = []
    for c in range(pieces):
        part = (slice(None),) * axis + (pl.ds(c * size, size),)
        copies.append(pltpu.make_async_copy(source.at[part], target.at[part], sems.at[c]))
    for copy in copies:
        copy.start()
    return copies


def inverse_rms(squares, width):
    return lax.rsqrt(jnp.sum(squares, axis=-1, keepdims=True) / width + 1e-05)


def table_kernel(rank_most, info_ref, first_ref, second_ref):
    info = info_ref[...].astype(jnp.float32)
    rows = info.shape[0]
    lane = lax.broadcasted_iota(jnp.int32, info.shape, 1)
    ranks = jnp.broadcast_to(info[:, 2:3], info.shape).astype(jnp.bfloat16)
    numbers = lax.broadcasted_iota(jnp.int32, (rows, rows), 1).astype(jnp.float32)
    for micro, ref in enumerate((first_ref, second_ref)):
        ids = info[:, micro : micro + 1]
        onehot = jnp.where(ids == numbers, 1.0, 0.0).astype(jnp.bfloat16)
        rank = jnp.dot(onehot, ranks, preferred_element_type=jnp.float32)
        ref[...] = jnp.where(lane == 0, ids, rank)


def ids_and_rank(table_ref):
    return table_ref[:, 0:1], table_ref[:, 1:2]


def first_kernel(
    rank_most, hidden_ref, base_hbm, maps_hbm, gain_ref, table_ref, owner_ref, order_hbm,
    base_out, sent_out, base_ref, maps_ref, base_sems, maps_sems,
):
    rows = hidden_ref.shape[0]
    width, cols = base_ref.shape
    held = maps_ref.shape[0]
    base_copies = fetches(base_hbm, base_ref, base_sems)
    maps_copies = fetches(maps_hbm, maps_ref, maps_sems, axis=1)
    base = jnp.zeros((rows, cols), jnp.float32)
    shrunk = jnp.zeros((rows, held), jnp.float32)
    squares = jnp.zeros((rows, cols), jnp.float32)
    steps = width // cols
    for j in range(steps):
        if j % (steps // CHUNKS) == 0:
            base_copies[j // (steps // CHUNKS)].wait()
            maps_copies[j // (steps // CHUNKS)].wait()
        part = slice(j * cols, (j + 1) * cols)
        wide = hidden_ref[:, part].astype(jnp.float32)
        squares = squares + wide * wide
        scaled = (wide * gain_ref[:, part]).astype(jnp.bfloat16)
        base = base + jnp.dot(scaled, base_ref[part, :], preferred_element_type=jnp.float32)
        shrunk = shrunk + lax.dot_general(
            scaled, maps_ref[:, part], (((1,), (1,)), ((), ())), preferred_element_type=jnp.float32
        )
    inverse = inverse_rms(squares, width)
    base_out[...] = base * inverse
    groups = lane_group((rows, held), rank_most)
    first = owner_ref[0] * (held // rank_most)
    ids, rank = ids_and_rank(table_ref)
    wanted = ids == (first + groups).astype(jnp.float32)
    factor = scaling(rank_most, rank, (rows, held))
    low = spread(jnp.where(wanted, shrunk * inverse * factor, 0.0), rank_most)
    sent_out[...] = fold(rank_most, jnp.concatenate([low] * (cols // held), axis=1), cols)


def finish(rank_most, h_ref, base, low, ids, expand_ref, out_ref, start=0):
    rows, cols = h_ref.shape
    wanted = ids - lane_group((rows, cols), rank_most).astype(jnp.float32)
    added = jnp.zeros((rows, cols), jnp.float32)
    for j in range((expand_ref.shape[0] - start) // cols):
        picked = jnp.where(wanted == j * GROUP, low, 0.0).astype(jnp.bfloat16)
        part = slice(start + j * cols, start + (j + 1) * cols)
        added = added + jnp.dot(picked, expand_ref[part, :], preferred_element_type=jnp.float32)
    update = (base + added).astype(jnp.bfloat16)
    out_ref[...] = (h_ref[...].astype(jnp.float32) + update.astype(jnp.float32)).astype(
        jnp.bfloat16
    )


def first_after_kernel(
    rank_most, h_ref, got_ref, table_ref, base_ref, expand_ref, out_ref
):
    partial = jnp.zeros(got_ref.shape[1:], jnp.float32)
    for j in range(got_ref.shape[0]):
        partial = partial + got_ref[j].astype(jnp.float32)
    low = unfold(rank_most, partial)
    ids, _ = ids_and_rank(table_ref)
    finish(rank_most, h_ref, base_ref[...], low, ids, expand_ref, out_ref)


def before_kernel(rank_most, h_ref, table_ref, shrink_ref, out_ref):
    rows, cols = h_ref.shape
    h = h_ref[...]
    ids, _ = ids_and_rank(table_ref)
    wanted = ids - lane_group((rows, cols), rank_most).astype(jnp.float32)
    total = jnp.zeros((rows, cols), jnp.float32)
    for j in range(shrink_ref.shape[0] // cols):
        part = lax.dot_general(
            h,
            shrink_ref[j * cols : (j + 1) * cols, :],
            (((1,), (1,)), ((), ())),
            preferred_element_type=jnp.float32,
        )
        total = total + jnp.where(wanted == j * GROUP, part, 0.0)
    out_ref[:rows, :] = h
    out_ref[rows:, :] = fold(rank_most, spread(total, rank_most), cols)


def after_kernel(
    rank_most, h_ref, got_ref, table_ref, wide_hbm, out_ref, wide_ref, sems
):
    rows, cols = h_ref.shape
    copies = fetches(wide_hbm, wide_ref, sems)
    sources = got_ref.shape[0]
    base = jnp.zeros((rows, cols), jnp.float32)
    squares = jnp.zeros((rows, cols), jnp.float32)
    partial = jnp.zeros((rows // GROUP, cols), jnp.float32)
    for j in range(sources):
        if j % (sources // CHUNKS) == 0:
            copies[j // (sources // CHUNKS)].wait()
        block = got_ref[j, :rows, :]
        base = base + jnp.dot(
            block, wide_ref[j * cols : (j + 1) * cols, :], preferred_element_type=jnp.float32
        )
        wide = block.astype(jnp.float32)
        squares = squares + wide * wide
        partial = partial + got_ref[j, rows:, :].astype(jnp.float32)
    inverse = inverse_rms(squares, sources * cols)
    ids, rank = ids_and_rank(table_ref)
    low = unfold(rank_most, partial) * inverse * scaling(rank_most, rank, (rows, cols))
    for copy in copies[CHUNKS:]:
        copy.wait()
    finish(rank_most, h_ref, base * inverse, low, ids, wide_ref, out_ref, sources * cols)


def unused_kernel(rank_most, *refs):
    for ref in refs:
        ref[:16, :] = jnp.zeros((16, ref.shape[1]), ref.dtype)


def on_device(tokens, adapter_ids, ranks, gain, base_weight, shrink_weight, expand_weight):
    micro_count, own_rows, model_width = tokens.shape
    cols = base_weight.shape[2]
    ad_count, _, rank_most = shrink_weight.shape[1:]
    total_adapters = expand_weight.shape[1]
    devices = lax.axis_size("adapter")
    segments = lax.axis_size("segment")
    segment = lax.axis_index("segment")
    owner = lax.axis_index("adapter")
    rows = own_rows * devices
    packed = rows // GROUP
    held = ad_count * rank_most
    all_held = total_adapters * rank_most
    wide_rows = model_width + all_held
    gain_row = gain[0]
    expand = expand_weight[0].reshape(all_held, cols)
    maps = shrink_weight[0].transpose(0, 2, 1).reshape(held, model_width)

    half, full = jnp.bfloat16, jnp.float32
    state = ((rows, cols), half)
    vmem = pl.BlockSpec(memory_space=pltpu.VMEM)
    hbm = pl.BlockSpec(memory_space=pl.ANY)
    smem = pl.BlockSpec(memory_space=pltpu.SMEM)
    fetched = pltpu.SemaphoreType.DMA((CHUNKS,))

    def call(kernel, shapes, *operands, specs=None, scratch=()):
        return pl.pallas_call(
            lambda *refs: kernel(rank_most, *refs),
            out_shape=[jax.ShapeDtypeStruct(*shape) for shape in shapes],
            in_specs=specs or [vmem] * len(operands),
            out_specs=[vmem] * len(shapes),
            scratch_shapes=scratch,
            compiler_params=pltpu.CompilerParams(vmem_limit_bytes=14 * 1024 * 1024),
        )(*operands)

    def exchange(blocks):
        return lax.all_to_all(blocks, "adapter", 0, 0, tiled=True)

    def gather(block):
        return exchange(jnp.broadcast_to(block, (devices,) + block.shape))

    info = jnp.concatenate([adapter_ids[0], adapter_ids[1], ranks[:, None]], axis=1)
    info = jnp.pad(info.astype(half), ((0, 0), (0, LANES - info.shape[1])))

    def tables(info):
        return call(table_kernel, [((rows, LANES), full)] * 2, info)

    def number(value):
        return jnp.asarray(value, jnp.int32).reshape(1)

    def gather_rows(micro):
        block = jnp.concatenate([tokens[micro], info], axis=1)
        return gather(block).reshape(rows, model_width + LANES)

    def first_layer(hidden, table, order):
        base, sent = call(
            first_kernel,
            [((rows, cols), full), ((packed, cols), half)],
            hidden,
            base_weight[0],
            maps,
            gain,
            table,
            number(owner),
            order,
            specs=[vmem, hbm, hbm, vmem, vmem, smem, hbm],
            scratch=[
                pltpu.VMEM((model_width, cols), half),
                pltpu.VMEM((held, model_width), half),
                fetched,
                fetched,
            ],
        )
        own = lax.dynamic_slice_in_dim(hidden, owner * cols, cols, 1)
        return call(
            first_after_kernel,
            [state],
            own,
            gather(sent),
            table,
            base,
            expand,
        )[0]

    def open_first(hidden):
        table, next_table = tables(hidden[:, model_width:])
        h = first_layer(hidden, table, hidden)
        shrink, wide = call(
            unused_kernel, [((all_held, cols), half), ((wide_rows, cols), half)]
        )
        return h, table, next_table, shrink, wide

    def open_other(hidden):
        by_dest = shrink_weight[0].reshape(ad_count, devices, cols, rank_most)
        by_dest = by_dest.transpose(1, 0, 3, 2).reshape(devices, held, cols)
        extra = jnp.pad(info, ((0, 16 - own_rows), (0, cols - LANES)))
        extra = jnp.broadcast_to(extra, (devices, 16, cols))
        got = exchange(jnp.concatenate([by_dest, extra], axis=1))
        base = (base_weight[0].astype(full) * gain_row[:, None]).astype(half)
        wide = jnp.concatenate([base, expand], axis=0)
        table, next_table = tables(got[:, held : held + own_rows, :LANES].reshape(rows, LANES))
        shrink = got[:, :held].reshape(all_held, cols)
        own_gain = lax.dynamic_slice_in_dim(gain_row, owner * cols, cols, 0)
        shrink = (shrink.astype(full) * own_gain[None, :]).astype(half)
        return jnp.zeros((rows, cols), half), table, next_table, shrink, wide

    block_shape = (devices, rows + packed, cols)

    def spread_out(h, table, shrink):
        (sent,) = call(
            before_kernel,
            [((rows + packed, cols), half)],
            h,
            table,
            shrink,
        )
        return gather(sent)

    def project(h, got, table, wide):
        return call(
            after_kernel,
            [state],
            h,
            got,
            table,
            wide,
            specs=[vmem, vmem, vmem, hbm],
            scratch=[
                pltpu.VMEM((wide_rows, cols), half),
                pltpu.SemaphoreType.DMA((wide_rows * CHUNKS // model_width,)),
            ],
        )[0]

    def nothing():
        return jnp.zeros((rows, cols), half)

    hidden = lax.cond(
        segment == 0,
        lambda: gather_rows(0),
        lambda: lax.cond(
            segment == 2,
            lambda: gather_rows(1),
            lambda: jnp.zeros((rows, model_width + LANES), half),
        ),
    )
    later = lax.ppermute(hidden, "segment", [(2, 0)])
    h, table, next_table, shrink, wide = lax.cond(segment == 0, open_first, open_other, hidden)
    outs = [h, h]
    for stage in range(1, segments + 1):
        pairs = [(s, s + 1) for s in (stage - 1, stage - 2) if 0 <= s < segments - 1]
        h = lax.ppermute(h, "segment", pairs)
        leads, trails = segment == stage, segment == stage - 1
        now = lax.optimization_barrier(jnp.where(leads, table, next_table))
        if stage == 1:
            got = lax.cond(
                leads,
                lambda: spread_out(h, now, shrink),
                lambda: jnp.zeros(block_shape, half),
            )
            over = lax.ppermute(got[0, :16, :LANES], "segment", [(1, 0)])
            branch = jnp.where(trails, 2, jnp.where(leads, 1, 0))
            h = lax.switch(
                branch,
                (nothing, lambda: project(h, got, now, wide), lambda: first_layer(later, now, over)),
            )
        else:
            h = lax.cond(
                leads | trails,
                lambda: project(h, spread_out(h, now, shrink), now, wide),
                nothing,
            )
        outs = [jnp.where(leads, h, outs[0]), jnp.where(trails, h, outs[1])]
    return jnp.stack(outs)[None]


def solution(mesh):
    in_specs = (
        P(None, "adapter", None),
        P(None, "adapter", None),
        P("adapter"),
        P("segment", None),
        P("segment", None, "adapter"),
        P("segment", "adapter", None, None),
        P("segment", None, None, "adapter"),
    )
    out_specs = P("segment", None, None, "adapter")
    return jax.shard_map(
        on_device, mesh=mesh, in_specs=in_specs, out_specs=out_specs, check_vma=False
    )
```

```python
import jax
import jax.numpy as jnp
from jax import lax
from jax.experimental import pallas as pl
from jax.experimental.pallas import tpu as pltpu
from jax.sharding import PartitionSpec as P

GROUP = 4
CHUNKS = 8
LANES = 128


def lane_group(shape, rank_most):
    return lax.broadcasted_iota(jnp.int32, shape, len(shape) - 1) // rank_most


def spread(value, rank_most):
    step = rank_most
    while step < value.shape[-1]:
        value = value + pltpu.roll(value, step, 1)
        step *= 2
    return value


def fold(rank_most, wide, cols):
    packed = wide.shape[0] // GROUP
    groups = lane_group((packed, cols), rank_most)
    folded = jnp.zeros((packed, cols), jnp.float32)
    for g in range(GROUP):
        folded = jnp.where(groups == g, wide[g * packed : (g + 1) * packed], folded)
    return folded.astype(jnp.bfloat16)


def unfold(rank_most, folded):
    groups = lane_group(folded.shape, rank_most)
    return jnp.concatenate(
        [spread(jnp.where(groups == g, folded, 0.0), rank_most) for g in range(GROUP)], axis=0
    )


def scaling(rank_most, rank, shape):
    place = lax.broadcasted_iota(jnp.int32, shape, 1) % rank_most
    return jnp.where(place.astype(jnp.float32) < rank, 32.0 / rank, 0.0)


def fetches(source, target, sems, axis=0):
    pieces = sems.shape[0]
    size = source.shape[axis] // pieces
    copies = []
    for c in range(pieces):
        part = (slice(None),) * axis + (pl.ds(c * size, size),)
        copies.append(pltpu.make_async_copy(source.at[part], target.at[part], sems.at[c]))
    for copy in copies:
        copy.start()
    return copies


def inverse_rms(squares, width):
    return lax.rsqrt(jnp.sum(squares, axis=-1, keepdims=True) / width + 1e-05)


def table_kernel(rank_most, info_ref, first_ref, second_ref):
    info = info_ref[...].astype(jnp.float32)
    rows = info.shape[0]
    lane = lax.broadcasted_iota(jnp.int32, info.shape, 1)
    ranks = jnp.broadcast_to(info[:, 2:3], info.shape).astype(jnp.bfloat16)
    numbers = lax.broadcasted_iota(jnp.int32, (rows, rows), 1).astype(jnp.float32)
    for micro, ref in enumerate((first_ref, second_ref)):
        ids = info[:, micro : micro + 1]
        onehot = jnp.where(ids == numbers, 1.0, 0.0).astype(jnp.bfloat16)
        rank = jnp.dot(onehot, ranks, preferred_element_type=jnp.float32)
        ref[...] = jnp.where(lane == 0, ids, rank)


def ids_and_rank(table_ref):
    return table_ref[:, 0:1], table_ref[:, 1:2]


def first_kernel(
    rank_most, hidden_ref, base_hbm, maps_hbm, gain_ref, table_ref, owner_ref,
    base_out, low_out, base_ref, maps_ref, base_sems, maps_sems,
):
    rows = hidden_ref.shape[0]
    width, cols = base_ref.shape
    held = maps_ref.shape[0]
    base_copies = fetches(base_hbm, base_ref, base_sems)
    maps_copies = fetches(maps_hbm, maps_ref, maps_sems, axis=1)
    base = jnp.zeros((rows, cols), jnp.float32)
    shrunk = jnp.zeros((rows, held), jnp.float32)
    squares = jnp.zeros((rows, cols), jnp.float32)
    steps = width // cols
    for j in range(steps):
        if j % (steps // CHUNKS) == 0:
            base_copies[j // (steps // CHUNKS)].wait()
            maps_copies[j // (steps // CHUNKS)].wait()
        part = slice(j * cols, (j + 1) * cols)
        wide = hidden_ref[:, part].astype(jnp.float32)
        squares = squares + wide * wide
        scaled = (wide * gain_ref[:, part]).astype(jnp.bfloat16)
        base = base + jnp.dot(scaled, base_ref[part, :], preferred_element_type=jnp.float32)
        shrunk = shrunk + lax.dot_general(
            scaled, maps_ref[:, part], (((1,), (1,)), ((), ())), preferred_element_type=jnp.float32
        )
    inverse = inverse_rms(squares, width)
    base_out[...] = base * inverse
    groups = lane_group((rows, held), rank_most)
    first = owner_ref[0] * (held // rank_most)
    ids, rank = ids_and_rank(table_ref)
    wanted = ids == (first + groups).astype(jnp.float32)
    factor = scaling(rank_most, rank, (rows, held))
    low_out[...] = spread(jnp.where(wanted, shrunk * inverse * factor, 0.0), rank_most)


def fold_kernel(rank_most, low_ref, order_hbm, out_ref):
    cols = out_ref.shape[1]
    low = jnp.concatenate([low_ref[...]] * (cols // low_ref.shape[1]), axis=1)
    out_ref[...] = fold(rank_most, low, cols)


def finish(rank_most, h_ref, base, low, ids, expand_ref, out_ref, start=0):
    rows, cols = h_ref.shape
    wanted = ids - lane_group((rows, cols), rank_most).astype(jnp.float32)
    added = jnp.zeros((rows, cols), jnp.float32)
    for j in range((expand_ref.shape[0] - start) // cols):
        picked = jnp.where(wanted == j * GROUP, low, 0.0).astype(jnp.bfloat16)
        part = slice(start + j * cols, start + (j + 1) * cols)
        added = added + jnp.dot(picked, expand_ref[part, :], preferred_element_type=jnp.float32)
    update = (base + added).astype(jnp.bfloat16)
    out_ref[...] = (h_ref[...].astype(jnp.float32) + update.astype(jnp.float32)).astype(
        jnp.bfloat16
    )


def first_after_kernel(
    rank_most, h_ref, got_ref, table_ref, base_ref, expand_hbm, out_ref, expand_ref, sems
):
    copies = fetches(expand_hbm, expand_ref, sems)
    partial = jnp.zeros(got_ref.shape[1:], jnp.float32)
    for j in range(got_ref.shape[0]):
        partial = partial + got_ref[j].astype(jnp.float32)
    low = unfold(rank_most, partial)
    ids, _ = ids_and_rank(table_ref)
    for copy in copies:
        copy.wait()
    finish(rank_most, h_ref, base_ref[...], low, ids, expand_ref, out_ref)


def before_kernel(rank_most, h_ref, table_ref, shrink_ref, out_ref):
    rows, cols = h_ref.shape
    h = h_ref[...]
    ids, _ = ids_and_rank(table_ref)
    wanted = ids - lane_group((rows, cols), rank_most).astype(jnp.float32)
    total = jnp.zeros((rows, cols), jnp.float32)
    for j in range(shrink_ref.shape[0] // cols):
        part = lax.dot_general(
            h,
            shrink_ref[j * cols : (j + 1) * cols, :],
            (((1,), (1,)), ((), ())),
            preferred_element_type=jnp.float32,
        )
        total = total + jnp.where(wanted == j * GROUP, part, 0.0)
    out_ref[:rows, :] = h
    out_ref[rows:, :] = fold(rank_most, spread(total, rank_most), cols)


def after_kernel(
    rank_most, h_ref, got_ref, table_ref, wide_hbm, out_ref, wide_ref, sems
):
    rows, cols = h_ref.shape
    copies = fetches(wide_hbm, wide_ref, sems)
    sources = got_ref.shape[0]
    base = jnp.zeros((rows, cols), jnp.float32)
    squares = jnp.zeros((rows, cols), jnp.float32)
    partial = jnp.zeros((rows // GROUP, cols), jnp.float32)
    for j in range(sources):
        if j % (sources // CHUNKS) == 0:
            copies[j // (sources // CHUNKS)].wait()
        block = got_ref[j, :rows, :]
        base = base + jnp.dot(
            block, wide_ref[j * cols : (j + 1) * cols, :], preferred_element_type=jnp.float32
        )
        wide = block.astype(jnp.float32)
        squares = squares + wide * wide
        partial = partial + got_ref[j, rows:, :].astype(jnp.float32)
    inverse = inverse_rms(squares, sources * cols)
    ids, rank = ids_and_rank(table_ref)
    low = unfold(rank_most, partial) * inverse * scaling(rank_most, rank, (rows, cols))
    for copy in copies[CHUNKS:]:
        copy.wait()
    finish(rank_most, h_ref, base * inverse, low, ids, wide_ref, out_ref, sources * cols)


def unused_kernel(rank_most, *refs):
    for ref in refs:
        ref[:16, :] = jnp.zeros((16, ref.shape[1]), ref.dtype)


def on_device(tokens, adapter_ids, ranks, gain, base_weight, shrink_weight, expand_weight):
    micro_count, own_rows, model_width = tokens.shape
    cols = base_weight.shape[2]
    ad_count, _, rank_most = shrink_weight.shape[1:]
    total_adapters = expand_weight.shape[1]
    devices = lax.axis_size("adapter")
    segments = lax.axis_size("segment")
    segment = lax.axis_index("segment")
    owner = lax.axis_index("adapter")
    rows = own_rows * devices
    packed = rows // GROUP
    held = ad_count * rank_most
    all_held = total_adapters * rank_most
    wide_rows = model_width + all_held
    gain_row = gain[0]
    expand = expand_weight[0].reshape(all_held, cols)
    maps = shrink_weight[0].transpose(0, 2, 1).reshape(held, model_width)

    half, full = jnp.bfloat16, jnp.float32
    state = ((rows, cols), half)
    vmem = pl.BlockSpec(memory_space=pltpu.VMEM)
    hbm = pl.BlockSpec(memory_space=pl.ANY)
    smem = pl.BlockSpec(memory_space=pltpu.SMEM)
    fetched = pltpu.SemaphoreType.DMA((CHUNKS,))

    def call(kernel, shapes, *operands, specs=None, scratch=()):
        return pl.pallas_call(
            lambda *refs: kernel(rank_most, *refs),
            out_shape=[jax.ShapeDtypeStruct(*shape) for shape in shapes],
            in_specs=specs or [vmem] * len(operands),
            out_specs=[vmem] * len(shapes),
            scratch_shapes=scratch,
            compiler_params=pltpu.CompilerParams(vmem_limit_bytes=14 * 1024 * 1024),
        )(*operands)

    def exchange(blocks):
        return lax.all_to_all(blocks, "adapter", 0, 0, tiled=True)

    def gather(block):
        return exchange(jnp.broadcast_to(block, (devices,) + block.shape))

    info = jnp.concatenate([adapter_ids[0], adapter_ids[1], ranks[:, None]], axis=1)
    info = jnp.pad(info.astype(half), ((0, 0), (0, LANES - info.shape[1])))

    def tables(info):
        return call(table_kernel, [((rows, LANES), full)] * 2, info)

    def number(value):
        return jnp.asarray(value, jnp.int32).reshape(1)

    def gather_rows(micro):
        block = jnp.concatenate([tokens[micro], info], axis=1)
        return gather(block).reshape(rows, model_width + LANES)

    first_shapes = [((rows, cols), full), ((rows, held), full)]

    def first_part(hidden, table):
        return call(
            first_kernel,
            first_shapes,
            hidden,
            base_weight[0],
            maps,
            gain,
            table,
            number(owner),
            specs=[vmem, hbm, hbm, vmem, vmem, smem],
            scratch=[
                pltpu.VMEM((model_width, cols), half),
                pltpu.VMEM((held, model_width), half),
                fetched,
                fetched,
            ],
        )

    def first_rest(hidden, table, base, low, order):
        (sent,) = call(fold_kernel, [((packed, cols), half)], low, order, specs=[vmem, hbm])
        own = lax.dynamic_slice_in_dim(hidden, owner * cols, cols, 1)
        return call(
            first_after_kernel,
            [state],
            own,
            gather(sent),
            table,
            base,
            expand,
            specs=[vmem, vmem, vmem, vmem, hbm],
            scratch=[pltpu.VMEM((all_held, cols), half), fetched],
        )[0]

    def open_first(hidden):
        table, next_table = tables(hidden[:, model_width:])
        h = first_rest(hidden, table, *first_part(hidden, table), hidden)
        shrink, wide = call(
            unused_kernel, [((all_held, cols), half), ((wide_rows, cols), half)]
        )
        return h, table, next_table, shrink, wide

    def open_other(hidden):
        by_dest = shrink_weight[0].reshape(ad_count, devices, cols, rank_most)
        by_dest = by_dest.transpose(1, 0, 3, 2).reshape(devices, held, cols)
        base = (base_weight[0].astype(full) * gain_row[:, None]).astype(half)
        base, head = lax.optimization_barrier((base, info))
        extra = jnp.pad(head, ((0, 16 - own_rows), (0, cols - LANES)))
        extra = jnp.broadcast_to(extra, (devices, 16, cols))
        got = exchange(jnp.concatenate([by_dest, extra], axis=1))
        wide = jnp.concatenate([base, expand], axis=0)
        table, next_table = tables(got[:, held : held + own_rows, :LANES].reshape(rows, LANES))
        shrink = got[:, :held].reshape(all_held, cols)
        own_gain = lax.dynamic_slice_in_dim(gain_row, owner * cols, cols, 0)
        shrink = (shrink.astype(full) * own_gain[None, :]).astype(half)
        return jnp.zeros((rows, cols), half), table, next_table, shrink, wide

    block_shape = (devices, rows + packed, cols)

    def spread_out(h, table, shrink):
        (sent,) = call(
            before_kernel,
            [((rows + packed, cols), half)],
            h,
            table,
            shrink,
        )
        return gather(sent)

    def project(h, got, table, wide):
        return call(
            after_kernel,
            [state],
            h,
            got,
            table,
            wide,
            specs=[vmem, vmem, vmem, hbm],
            scratch=[
                pltpu.VMEM((wide_rows, cols), half),
                pltpu.SemaphoreType.DMA((wide_rows * CHUNKS // model_width,)),
            ],
        )[0]

    def nothing():
        return jnp.zeros((rows, cols), half)

    hidden = lax.cond(
        segment == 0,
        lambda: gather_rows(0),
        lambda: lax.cond(
            segment == 2,
            lambda: gather_rows(1),
            lambda: jnp.zeros((rows, model_width + LANES), half),
        ),
    )
    later = lax.ppermute(hidden, "segment", [(2, 0)])
    h, table, next_table, shrink, wide = lax.cond(segment == 0, open_first, open_other, hidden)
    outs = [h, h]
    for stage in range(1, segments + 1):
        pairs = [(s, s + 1) for s in (stage - 1, stage - 2) if 0 <= s < segments - 1]
        h = lax.ppermute(h, "segment", pairs)
        leads, trails = segment == stage, segment == stage - 1
        now = lax.optimization_barrier(jnp.where(leads, table, next_table))
        if stage == 1:
            branch = jnp.where(trails, 2, jnp.where(leads, 1, 0))

            def zeros(*shapes):
                return [jnp.zeros(*shape) for shape in shapes]

            block = (block_shape, half)
            got, first_base, low = lax.switch(
                branch,
                (
                    lambda: zeros(block, *first_shapes),
                    lambda: [spread_out(h, now, shrink), *zeros(*first_shapes)],
                    lambda: [*zeros(block), *first_part(later, now)],
                ),
            )
            over = lax.ppermute(got[0, :16, :LANES], "segment", [(1, 0)])
            h = lax.switch(
                branch,
                (
                    nothing,
                    lambda: project(h, got, now, wide),
                    lambda: first_rest(later, now, first_base, low, over),
                ),
            )
        else:
            h = lax.cond(
                leads | trails,
                lambda: project(h, spread_out(h, now, shrink), now, wide),
                nothing,
            )
        outs = [jnp.where(leads, h, outs[0]), jnp.where(trails, h, outs[1])]
    return jnp.stack(outs)[None]


def solution(mesh):
    in_specs = (
        P(None, "adapter", None),
        P(None, "adapter", None),
        P("adapter"),
        P("segment", None),
        P("segment", None, "adapter"),
        P("segment", "adapter", None, None),
        P("segment", None, None, "adapter"),
    )
    out_specs = P("segment", None, None, "adapter")
    return jax.shard_map(
        on_device, mesh=mesh, in_specs=in_specs, out_specs=out_specs, check_vma=False
    )
```

```python
import jax
import jax.numpy as jnp
from jax import lax
from jax.experimental import pallas as pl
from jax.experimental.pallas import tpu as pltpu
from jax.sharding import PartitionSpec as P

GROUP = 4
CHUNKS = 4
LANES = 128


def lane_group(shape, rank_most):
    return lax.broadcasted_iota(jnp.int32, shape, len(shape) - 1) // rank_most


def spread(value, rank_most):
    step = rank_most
    while step < value.shape[-1]:
        value = value + pltpu.roll(value, step, 1)
        step *= 2
    return value


def fold(rank_most, wide, cols):
    packed = wide.shape[0] // GROUP
    groups = lane_group((packed, cols), rank_most)
    folded = jnp.zeros((packed, cols), jnp.float32)
    for g in range(GROUP):
        folded = jnp.where(groups == g, wide[g * packed : (g + 1) * packed], folded)
    return folded.astype(jnp.bfloat16)


def unfold(rank_most, folded):
    groups = lane_group(folded.shape, rank_most)
    return jnp.concatenate(
        [spread(jnp.where(groups == g, folded, 0.0), rank_most) for g in range(GROUP)], axis=0
    )


def scaling(rank_most, rank, shape):
    place = lax.broadcasted_iota(jnp.int32, shape, 1) % rank_most
    return jnp.where(place.astype(jnp.float32) < rank, 32.0 / rank, 0.0)


def fetches(source, target, sems, axis=0):
    pieces = sems.shape[0]
    size = source.shape[axis] // pieces
    copies = []
    for c in range(pieces):
        part = (slice(None),) * axis + (pl.ds(c * size, size),)
        copies.append(pltpu.make_async_copy(source.at[part], target.at[part], sems.at[c]))
    for copy in copies:
        copy.start()
    return copies


def inverse_rms(squares, width):
    return lax.rsqrt(jnp.sum(squares, axis=-1, keepdims=True) / width + 1e-05)


def table_kernel(rank_most, info_ref, first_ref, second_ref):
    info = info_ref[...].astype(jnp.float32)
    rows = info.shape[0]
    lane = lax.broadcasted_iota(jnp.int32, info.shape, 1)
    ranks = jnp.broadcast_to(info[:, 2:3], info.shape).astype(jnp.bfloat16)
    numbers = lax.broadcasted_iota(jnp.int32, (rows, rows), 1).astype(jnp.float32)
    for micro, ref in enumerate((first_ref, second_ref)):
        ids = info[:, micro : micro + 1]
        onehot = jnp.where(ids == numbers, 1.0, 0.0).astype(jnp.bfloat16)
        rank = jnp.dot(onehot, ranks, preferred_element_type=jnp.float32)
        ref[...] = jnp.where(lane == 0, ids, rank)


def ids_and_rank(table_ref):
    return table_ref[:, 0:1], table_ref[:, 1:2]


def first_kernel(
    rank_most, hidden_ref, base_hbm, maps_hbm, gain_ref, table_ref, owner_ref, order_hbm,
    base_out, sent_out, base_ref, maps_ref, base_sems, maps_sems,
):
    rows = hidden_ref.shape[0]
    width, cols = base_ref.shape
    held = maps_ref.shape[0]
    base_copies = fetches(base_hbm, base_ref, base_sems)
    maps_copies = fetches(maps_hbm, maps_ref, maps_sems, axis=1)
    base = jnp.zeros((rows, cols), jnp.float32)
    shrunk = jnp.zeros((rows, held), jnp.float32)
    squares = jnp.zeros((rows, cols), jnp.float32)
    steps = width // cols
    for j in range(steps):
        if j % (steps // CHUNKS) == 0:
            base_copies[j // (steps // CHUNKS)].wait()
            maps_copies[j // (steps // CHUNKS)].wait()
        part = slice(j * cols, (j + 1) * cols)
        wide = hidden_ref[:, part].astype(jnp.float32)
        squares = squares + wide * wide
        scaled = (wide * gain_ref[:, part]).astype(jnp.bfloat16)
        base = base + jnp.dot(scaled, base_ref[part, :], preferred_element_type=jnp.float32)
        shrunk = shrunk + lax.dot_general(
            scaled, maps_ref[:, part], (((1,), (1,)), ((), ())), preferred_element_type=jnp.float32
        )
    inverse = inverse_rms(squares, width)
    base_out[...] = base * inverse
    groups = lane_group((rows, held), rank_most)
    first = owner_ref[0] * (held // rank_most)
    ids, rank = ids_and_rank(table_ref)
    wanted = ids == (first + groups).astype(jnp.float32)
    factor = scaling(rank_most, rank, (rows, held))
    low = spread(jnp.where(wanted, shrunk * inverse * factor, 0.0), rank_most)
    sent_out[...] = fold(rank_most, jnp.concatenate([low] * (cols // held), axis=1), cols)


def finish(rank_most, h_ref, base, low, ids, expand_ref, out_ref, start=0):
    rows, cols = h_ref.shape
    wanted = ids - lane_group((rows, cols), rank_most).astype(jnp.float32)
    added = jnp.zeros((rows, cols), jnp.float32)
    for j in range((expand_ref.shape[0] - start) // cols):
        picked = jnp.where(wanted == j * GROUP, low, 0.0).astype(jnp.bfloat16)
        part = slice(start + j * cols, start + (j + 1) * cols)
        added = added + jnp.dot(picked, expand_ref[part, :], preferred_element_type=jnp.float32)
    update = (base + added).astype(jnp.bfloat16)
    out_ref[...] = (h_ref[...].astype(jnp.float32) + update.astype(jnp.float32)).astype(
        jnp.bfloat16
    )


def first_after_kernel(
    rank_most, h_ref, got_ref, table_ref, base_ref, expand_ref, out_ref
):
    partial = jnp.zeros(got_ref.shape[1:], jnp.float32)
    for j in range(got_ref.shape[0]):
        partial = partial + got_ref[j].astype(jnp.float32)
    low = unfold(rank_most, partial)
    ids, _ = ids_and_rank(table_ref)
    finish(rank_most, h_ref, base_ref[...], low, ids, expand_ref, out_ref)


def before_kernel(rank_most, h_ref, table_ref, shrink_ref, out_ref):
    rows, cols = h_ref.shape
    h = h_ref[...]
    ids, _ = ids_and_rank(table_ref)
    wanted = ids - lane_group((rows, cols), rank_most).astype(jnp.float32)
    total = jnp.zeros((rows, cols), jnp.float32)
    for j in range(shrink_ref.shape[0] // cols):
        part = lax.dot_general(
            h,
            shrink_ref[j * cols : (j + 1) * cols, :],
            (((1,), (1,)), ((), ())),
            preferred_element_type=jnp.float32,
        )
        total = total + jnp.where(wanted == j * GROUP, part, 0.0)
    out_ref[:rows, :] = h
    out_ref[rows:, :] = fold(rank_most, spread(total, rank_most), cols)


def after_kernel(
    rank_most, h_ref, got_ref, table_ref, wide_hbm, out_ref, wide_ref, sems
):
    rows, cols = h_ref.shape
    copies = fetches(wide_hbm, wide_ref, sems)
    sources = got_ref.shape[0]
    base = jnp.zeros((rows, cols), jnp.float32)
    squares = jnp.zeros((rows, cols), jnp.float32)
    partial = jnp.zeros((rows // GROUP, cols), jnp.float32)
    for j in range(sources):
        if j % (sources // CHUNKS) == 0:
            copies[j // (sources // CHUNKS)].wait()
        block = got_ref[j, :rows, :]
        base = base + jnp.dot(
            block, wide_ref[j * cols : (j + 1) * cols, :], preferred_element_type=jnp.float32
        )
        wide = block.astype(jnp.float32)
        squares = squares + wide * wide
        partial = partial + got_ref[j, rows:, :].astype(jnp.float32)
    inverse = inverse_rms(squares, sources * cols)
    ids, rank = ids_and_rank(table_ref)
    low = unfold(rank_most, partial) * inverse * scaling(rank_most, rank, (rows, cols))
    for copy in copies[CHUNKS:]:
        copy.wait()
    finish(rank_most, h_ref, base * inverse, low, ids, wide_ref, out_ref, sources * cols)


def unused_kernel(rank_most, *refs):
    for ref in refs:
        ref[:16, :] = jnp.zeros((16, ref.shape[1]), ref.dtype)


def on_device(tokens, adapter_ids, ranks, gain, base_weight, shrink_weight, expand_weight):
    micro_count, own_rows, model_width = tokens.shape
    cols = base_weight.shape[2]
    ad_count, _, rank_most = shrink_weight.shape[1:]
    total_adapters = expand_weight.shape[1]
    devices = lax.axis_size("adapter")
    segments = lax.axis_size("segment")
    segment = lax.axis_index("segment")
    owner = lax.axis_index("adapter")
    rows = own_rows * devices
    packed = rows // GROUP
    held = ad_count * rank_most
    all_held = total_adapters * rank_most
    wide_rows = model_width + all_held
    gain_row = gain[0]
    expand = expand_weight[0].reshape(all_held, cols)
    maps = shrink_weight[0].transpose(0, 2, 1).reshape(held, model_width)

    half, full = jnp.bfloat16, jnp.float32
    state = ((rows, cols), half)
    vmem = pl.BlockSpec(memory_space=pltpu.VMEM)
    hbm = pl.BlockSpec(memory_space=pl.ANY)
    smem = pl.BlockSpec(memory_space=pltpu.SMEM)
    fetched = pltpu.SemaphoreType.DMA((CHUNKS,))

    def call(kernel, shapes, *operands, specs=None, scratch=()):
        return pl.pallas_call(
            lambda *refs: kernel(rank_most, *refs),
            out_shape=[jax.ShapeDtypeStruct(*shape) for shape in shapes],
            in_specs=specs or [vmem] * len(operands),
            out_specs=[vmem] * len(shapes),
            scratch_shapes=scratch,
            compiler_params=pltpu.CompilerParams(vmem_limit_bytes=14 * 1024 * 1024),
        )(*operands)

    def exchange(blocks):
        return lax.all_to_all(blocks, "adapter", 0, 0, tiled=True)

    def gather(block):
        return exchange(jnp.broadcast_to(block, (devices,) + block.shape))

    info = jnp.concatenate([adapter_ids[0], adapter_ids[1], ranks[:, None]], axis=1)
    info = jnp.pad(info.astype(half), ((0, 0), (0, LANES - info.shape[1])))

    def tables(info):
        return call(table_kernel, [((rows, LANES), full)] * 2, info)

    def number(value):
        return jnp.asarray(value, jnp.int32).reshape(1)

    def gather_rows(micro):
        block = jnp.concatenate([tokens[micro], info], axis=1)
        return gather(block).reshape(rows, model_width + LANES)

    def first_layer(hidden, table, order):
        base, sent = call(
            first_kernel,
            [((rows, cols), full), ((packed, cols), half)],
            hidden,
            base_weight[0],
            maps,
            gain,
            table,
            number(owner),
            order,
            specs=[vmem, hbm, hbm, vmem, vmem, smem, hbm],
            scratch=[
                pltpu.VMEM((model_width, cols), half),
                pltpu.VMEM((held, model_width), half),
                fetched,
                fetched,
            ],
        )
        own = lax.dynamic_slice_in_dim(hidden, owner * cols, cols, 1)
        return call(
            first_after_kernel,
            [state],
            own,
            gather(sent),
            table,
            base,
            expand,
        )[0]

    def open_first(hidden):
        table, next_table = tables(hidden[:, model_width:])
        h = first_layer(hidden, table, hidden)
        shrink, wide = call(
            unused_kernel, [((all_held, cols), half), ((wide_rows, cols), half)]
        )
        return h, table, next_table, shrink, wide

    def open_other(hidden):
        by_dest = shrink_weight[0].reshape(ad_count, devices, cols, rank_most)
        by_dest = by_dest.transpose(1, 0, 3, 2).reshape(devices, held, cols)
        base = (base_weight[0].astype(full) * gain_row[:, None]).astype(half)
        base, head = lax.optimization_barrier((base, info))
        extra = jnp.pad(head, ((0, 16 - own_rows), (0, cols - LANES)))
        extra = jnp.broadcast_to(extra, (devices, 16, cols))
        got = exchange(jnp.concatenate([by_dest, extra], axis=1))
        wide = jnp.concatenate([base, expand], axis=0)
        table, next_table = tables(got[:, held : held + own_rows, :LANES].reshape(rows, LANES))
        shrink = got[:, :held].reshape(all_held, cols)
        own_gain = lax.dynamic_slice_in_dim(gain_row, owner * cols, cols, 0)
        shrink = (shrink.astype(full) * own_gain[None, :]).astype(half)
        return jnp.zeros((rows, cols), half), table, next_table, shrink, wide

    block_shape = (devices, rows + packed, cols)

    def spread_out(h, table, shrink):
        (sent,) = call(
            before_kernel,
            [((rows + packed, cols), half)],
            h,
            table,
            shrink,
        )
        return gather(sent)

    def project(h, got, table, wide):
        return call(
            after_kernel,
            [state],
            h,
            got,
            table,
            wide,
            specs=[vmem, vmem, vmem, hbm],
            scratch=[
                pltpu.VMEM((wide_rows, cols), half),
                pltpu.SemaphoreType.DMA((wide_rows * CHUNKS // model_width,)),
            ],
        )[0]

    def nothing():
        return jnp.zeros((rows, cols), half)

    hidden = lax.cond(
        segment == 0,
        lambda: gather_rows(0),
        lambda: lax.cond(
            segment == 2,
            lambda: gather_rows(1),
            lambda: jnp.zeros((rows, model_width + LANES), half),
        ),
    )
    later = lax.ppermute(hidden, "segment", [(2, 0)])
    h, table, next_table, shrink, wide = lax.cond(segment == 0, open_first, open_other, hidden)
    outs = [h, h]
    for stage in range(1, segments + 1):
        pairs = [(s, s + 1) for s in (stage - 1, stage - 2) if 0 <= s < segments - 1]
        h = lax.ppermute(h, "segment", pairs)
        leads, trails = segment == stage, segment == stage - 1
        now = lax.optimization_barrier(jnp.where(leads, table, next_table))
        if stage == 1:
            got = lax.cond(
                leads,
                lambda: spread_out(h, now, shrink),
                lambda: jnp.zeros(block_shape, half),
            )
            over = lax.ppermute(got[0, :16, :LANES], "segment", [(1, 0)])
            branch = jnp.where(trails, 2, jnp.where(leads, 1, 0))
            h = lax.switch(
                branch,
                (nothing, lambda: project(h, got, now, wide), lambda: first_layer(later, now, over)),
            )
        else:
            h = lax.cond(
                leads | trails,
                lambda: project(h, spread_out(h, now, shrink), now, wide),
                nothing,
            )
        outs = [jnp.where(leads, h, outs[0]), jnp.where(trails, h, outs[1])]
    return jnp.stack(outs)[None]


def solution(mesh):
    in_specs = (
        P(None, "adapter", None),
        P(None, "adapter", None),
        P("adapter"),
        P("segment", None),
        P("segment", None, "adapter"),
        P("segment", "adapter", None, None),
        P("segment", None, None, "adapter"),
    )
    out_specs = P("segment", None, None, "adapter")
    return jax.shard_map(
        on_device, mesh=mesh, in_specs=in_specs, out_specs=out_specs, check_vma=False
    )
```

```python
import jax
import jax.numpy as jnp
from jax import lax
from jax.experimental import pallas as pl
from jax.experimental.pallas import tpu as pltpu
from jax.sharding import PartitionSpec as P

GROUP = 4
CHUNKS = 4
LANES = 128


def lane_group(shape, rank_most):
    return lax.broadcasted_iota(jnp.int32, shape, len(shape) - 1) // rank_most


def spread(value, rank_most):
    step = rank_most
    while step < value.shape[-1]:
        value = value + pltpu.roll(value, step, 1)
        step *= 2
    return value


def fold(rank_most, wide, cols):
    packed = wide.shape[0] // GROUP
    groups = lane_group((packed, cols), rank_most)
    folded = jnp.zeros((packed, cols), jnp.float32)
    for g in range(GROUP):
        folded = jnp.where(groups == g, wide[g * packed : (g + 1) * packed], folded)
    return folded.astype(jnp.bfloat16)


def unfold(rank_most, folded):
    groups = lane_group(folded.shape, rank_most)
    return jnp.concatenate(
        [spread(jnp.where(groups == g, folded, 0.0), rank_most) for g in range(GROUP)], axis=0
    )


def scaling(rank_most, rank, shape):
    place = lax.broadcasted_iota(jnp.int32, shape, 1) % rank_most
    return jnp.where(place.astype(jnp.float32) < rank, 32.0 / rank, 0.0)


def fetches(source, target, sems, axis=0):
    pieces = sems.shape[0]
    size = source.shape[axis] // pieces
    copies = []
    for c in range(pieces):
        part = (slice(None),) * axis + (pl.ds(c * size, size),)
        copies.append(pltpu.make_async_copy(source.at[part], target.at[part], sems.at[c]))
    for copy in copies:
        copy.start()
    return copies


def inverse_rms(squares, width):
    return lax.rsqrt(jnp.sum(squares, axis=-1, keepdims=True) / width + 1e-05)


def table_kernel(rank_most, info_ref, first_ref, second_ref):
    info = info_ref[...].astype(jnp.float32)
    rows = info.shape[0]
    lane = lax.broadcasted_iota(jnp.int32, info.shape, 1)
    ranks = jnp.broadcast_to(info[:, 2:3], info.shape).astype(jnp.bfloat16)
    numbers = lax.broadcasted_iota(jnp.int32, (rows, rows), 1).astype(jnp.float32)
    for micro, ref in enumerate((first_ref, second_ref)):
        ids = info[:, micro : micro + 1]
        onehot = jnp.where(ids == numbers, 1.0, 0.0).astype(jnp.bfloat16)
        rank = jnp.dot(onehot, ranks, preferred_element_type=jnp.float32)
        ref[...] = jnp.where(lane == 0, ids, rank)


def ids_and_rank(table_ref):
    return table_ref[:, 0:1], table_ref[:, 1:2]


def first_kernel(
    rank_most, hidden_ref, base_hbm, maps_hbm, gain_ref, table_ref, owner_ref, order_hbm,
    base_out, sent_out, base_ref, maps_ref, base_sems, maps_sems,
):
    rows = hidden_ref.shape[0]
    width, cols = base_ref.shape
    held = maps_ref.shape[0]
    base_copies = fetches(base_hbm, base_ref, base_sems)
    maps_copies = fetches(maps_hbm, maps_ref, maps_sems, axis=1)
    base = jnp.zeros((rows, cols), jnp.float32)
    shrunk = jnp.zeros((rows, held), jnp.float32)
    squares = jnp.zeros((rows, cols), jnp.float32)
    steps = width // cols
    for j in range(steps):
        if j % (steps // CHUNKS) == 0:
            base_copies[j // (steps // CHUNKS)].wait()
            maps_copies[j // (steps // CHUNKS)].wait()
        part = slice(j * cols, (j + 1) * cols)
        wide = hidden_ref[:, part].astype(jnp.float32)
        squares = squares + wide * wide
        scaled = (wide * gain_ref[:, part]).astype(jnp.bfloat16)
        base = base + jnp.dot(scaled, base_ref[part, :], preferred_element_type=jnp.float32)
        shrunk = shrunk + lax.dot_general(
            scaled, maps_ref[:, part], (((1,), (1,)), ((), ())), preferred_element_type=jnp.float32
        )
    inverse = inverse_rms(squares, width)
    base_out[...] = base * inverse
    groups = lane_group((rows, held), rank_most)
    first = owner_ref[0] * (held // rank_most)
    ids, rank = ids_and_rank(table_ref)
    wanted = ids == (first + groups).astype(jnp.float32)
    factor = scaling(rank_most, rank, (rows, held))
    low = spread(jnp.where(wanted, shrunk * inverse * factor, 0.0), rank_most)
    sent_out[...] = fold(rank_most, jnp.concatenate([low] * (cols // held), axis=1), cols)


def finish(rank_most, h_ref, base, low, ids, expand_ref, out_ref, start=0):
    rows, cols = h_ref.shape
    wanted = ids - lane_group((rows, cols), rank_most).astype(jnp.float32)
    added = jnp.zeros((rows, cols), jnp.float32)
    for j in range((expand_ref.shape[0] - start) // cols):
        picked = jnp.where(wanted == j * GROUP, low, 0.0).astype(jnp.bfloat16)
        part = slice(start + j * cols, start + (j + 1) * cols)
        added = added + jnp.dot(picked, expand_ref[part, :], preferred_element_type=jnp.float32)
    update = (base + added).astype(jnp.bfloat16)
    out_ref[...] = (h_ref[...].astype(jnp.float32) + update.astype(jnp.float32)).astype(
        jnp.bfloat16
    )


def first_after_kernel(
    rank_most, h_ref, got_ref, table_ref, base_ref, expand_ref, out_ref
):
    partial = jnp.zeros(got_ref.shape[1:], jnp.float32)
    for j in range(got_ref.shape[0]):
        partial = partial + got_ref[j].astype(jnp.float32)
    low = unfold(rank_most, partial)
    ids, _ = ids_and_rank(table_ref)
    finish(rank_most, h_ref, base_ref[...], low, ids, expand_ref, out_ref)


def before_kernel(rank_most, h_ref, table_ref, shrink_ref, out_ref):
    rows, cols = h_ref.shape
    h = h_ref[...]
    ids, _ = ids_and_rank(table_ref)
    wanted = ids - lane_group((rows, cols), rank_most).astype(jnp.float32)
    total = jnp.zeros((rows, cols), jnp.float32)
    for j in range(shrink_ref.shape[0] // cols):
        part = lax.dot_general(
            h,
            shrink_ref[j * cols : (j + 1) * cols, :],
            (((1,), (1,)), ((), ())),
            preferred_element_type=jnp.float32,
        )
        total = total + jnp.where(wanted == j * GROUP, part, 0.0)
    out_ref[:rows, :] = h
    out_ref[rows:, :] = fold(rank_most, spread(total, rank_most), cols)


def after_kernel(
    rank_most, h_ref, got_ref, table_ref, wide_hbm, out_ref, wide_ref, sems
):
    rows, cols = h_ref.shape
    copies = fetches(wide_hbm, wide_ref, sems)
    sources = got_ref.shape[0]
    base = jnp.zeros((rows, cols), jnp.float32)
    squares = jnp.zeros((rows, cols), jnp.float32)
    partial = jnp.zeros((rows // GROUP, cols), jnp.float32)
    for j in range(sources):
        if j % (sources // CHUNKS) == 0:
            copies[j // (sources // CHUNKS)].wait()
        block = got_ref[j, :rows, :]
        base = base + jnp.dot(
            block, wide_ref[j * cols : (j + 1) * cols, :], preferred_element_type=jnp.float32
        )
        wide = block.astype(jnp.float32)
        squares = squares + wide * wide
        partial = partial + got_ref[j, rows:, :].astype(jnp.float32)
    inverse = inverse_rms(squares, sources * cols)
    ids, rank = ids_and_rank(table_ref)
    low = unfold(rank_most, partial) * inverse * scaling(rank_most, rank, (rows, cols))
    for copy in copies[CHUNKS:]:
        copy.wait()
    finish(rank_most, h_ref, base * inverse, low, ids, wide_ref, out_ref, sources * cols)


def unused_kernel(rank_most, *refs):
    for ref in refs:
        ref[:16, :] = jnp.zeros((16, ref.shape[1]), ref.dtype)


def on_device(tokens, adapter_ids, ranks, gain, base_weight, shrink_weight, expand_weight):
    micro_count, own_rows, model_width = tokens.shape
    cols = base_weight.shape[2]
    ad_count, _, rank_most = shrink_weight.shape[1:]
    total_adapters = expand_weight.shape[1]
    devices = lax.axis_size("adapter")
    segments = lax.axis_size("segment")
    segment = lax.axis_index("segment")
    owner = lax.axis_index("adapter")
    rows = own_rows * devices
    packed = rows // GROUP
    held = ad_count * rank_most
    all_held = total_adapters * rank_most
    wide_rows = model_width + all_held
    width = model_width // 2
    gain_row = gain[0]
    expand = expand_weight[0].reshape(all_held, cols)
    maps = shrink_weight[0].transpose(0, 2, 1).reshape(held, model_width)

    half, full = jnp.bfloat16, jnp.float32
    state = ((rows, cols), half)
    vmem = pl.BlockSpec(memory_space=pltpu.VMEM)
    hbm = pl.BlockSpec(memory_space=pl.ANY)
    smem = pl.BlockSpec(memory_space=pltpu.SMEM)
    fetched = pltpu.SemaphoreType.DMA((CHUNKS,))

    def call(kernel, shapes, *operands, specs=None, scratch=()):
        return pl.pallas_call(
            lambda *refs: kernel(rank_most, *refs),
            out_shape=[jax.ShapeDtypeStruct(*shape) for shape in shapes],
            in_specs=specs or [vmem] * len(operands),
            out_specs=[vmem] * len(shapes),
            scratch_shapes=scratch,
            compiler_params=pltpu.CompilerParams(vmem_limit_bytes=14 * 1024 * 1024),
        )(*operands)

    def exchange(blocks):
        return lax.all_to_all(blocks, "adapter", 0, 0, tiled=True)

    def gather(block):
        return exchange(jnp.broadcast_to(block, (devices,) + block.shape))

    info = jnp.concatenate([adapter_ids[0], adapter_ids[1], ranks[:, None]], axis=1)
    info = jnp.pad(info.astype(half), ((0, 0), (0, LANES - info.shape[1])))

    def tables(info):
        return call(table_kernel, [((rows, LANES), full)] * 2, info)

    def number(value):
        return jnp.asarray(value, jnp.int32).reshape(1)

    def gather_rows(micro, start, width):
        block = lax.dynamic_slice_in_dim(tokens[micro], start, width, 1)
        block = jnp.concatenate([block, info], axis=1)
        return gather(block).reshape(rows, width + LANES)

    def first_layer(hidden, table, order):
        base, sent = call(
            first_kernel,
            [((rows, cols), full), ((packed, cols), half)],
            hidden,
            base_weight[0],
            maps,
            gain,
            table,
            number(owner),
            order,
            specs=[vmem, hbm, hbm, vmem, vmem, smem, hbm],
            scratch=[
                pltpu.VMEM((model_width, cols), half),
                pltpu.VMEM((held, model_width), half),
                fetched,
                fetched,
            ],
        )
        own = lax.dynamic_slice_in_dim(hidden, owner * cols, cols, 1)
        return call(
            first_after_kernel,
            [state],
            own,
            gather(sent),
            table,
            base,
            expand,
        )[0]

    def open_first(head, rest):
        table, next_table = tables(head[:, width:])
        hidden = jnp.concatenate([head[:, :width], rest[:, :width]], axis=1)
        h = first_layer(hidden, table, hidden)
        shrink, wide = call(
            unused_kernel, [((all_held, cols), half), ((wide_rows, cols), half)]
        )
        return h, table, next_table, shrink, wide

    def open_other(head, rest):
        by_dest = shrink_weight[0].reshape(ad_count, devices, cols, rank_most)
        by_dest = by_dest.transpose(1, 0, 3, 2).reshape(devices, held, cols)
        base = (base_weight[0].astype(full) * gain_row[:, None]).astype(half)
        base, head = lax.optimization_barrier((base, info))
        extra = jnp.pad(head, ((0, 16 - own_rows), (0, cols - LANES)))
        extra = jnp.broadcast_to(extra, (devices, 16, cols))
        got = exchange(jnp.concatenate([by_dest, extra], axis=1))
        wide = jnp.concatenate([base, expand], axis=0)
        table, next_table = tables(got[:, held : held + own_rows, :LANES].reshape(rows, LANES))
        shrink = got[:, :held].reshape(all_held, cols)
        own_gain = lax.dynamic_slice_in_dim(gain_row, owner * cols, cols, 0)
        shrink = (shrink.astype(full) * own_gain[None, :]).astype(half)
        return jnp.zeros((rows, cols), half), table, next_table, shrink, wide

    block_shape = (devices, rows + packed, cols)

    def spread_out(h, table, shrink):
        (sent,) = call(
            before_kernel,
            [((rows + packed, cols), half)],
            h,
            table,
            shrink,
        )
        return gather(sent)

    def project(h, got, table, wide):
        return call(
            after_kernel,
            [state],
            h,
            got,
            table,
            wide,
            specs=[vmem, vmem, vmem, hbm],
            scratch=[
                pltpu.VMEM((wide_rows, cols), half),
                pltpu.SemaphoreType.DMA((wide_rows * CHUNKS // model_width,)),
            ],
        )[0]

    def nothing():
        return jnp.zeros((rows, cols), half)

    def no_rows(width):
        return jnp.zeros((rows, width + LANES), half)

    sides, beyond = (2, segments - 2), segments // 2
    side = lax.cond(
        (segment == sides[0]) | (segment == sides[1]),
        lambda: gather_rows(0, jnp.where(segment == sides[0], 0, width), width),
        lambda: no_rows(width),
    )
    head, rest = [lax.ppermute(side, "segment", [(s, 0)]) for s in sides]
    lent = lax.cond(
        segment == beyond, lambda: gather_rows(1, 0, model_width), lambda: no_rows(model_width)
    )
    later = lax.ppermute(lent, "segment", [(beyond, 0)])
    h, table, next_table, shrink, wide = lax.cond(
        segment == 0, open_first, open_other, head, rest
    )
    outs = [h, h]
    for stage in range(1, segments + 1):
        pairs = [(s, s + 1) for s in (stage - 1, stage - 2) if 0 <= s < segments - 1]
        h = lax.ppermute(h, "segment", pairs)
        leads, trails = segment == stage, segment == stage - 1
        now = lax.optimization_barrier(jnp.where(leads, table, next_table))
        if stage == 1:
            got = lax.cond(
                leads,
                lambda: spread_out(h, now, shrink),
                lambda: jnp.zeros(block_shape, half),
            )
            over = lax.ppermute(got[0, :16, :LANES], "segment", [(1, 0)])
            branch = jnp.where(trails, 2, jnp.where(leads, 1, 0))
            h = lax.switch(
                branch,
                (nothing, lambda: project(h, got, now, wide), lambda: first_layer(later, now, over)),
            )
        else:
            h = lax.cond(
                leads | trails,
                lambda: project(h, spread_out(h, now, shrink), now, wide),
                nothing,
            )
        outs = [jnp.where(leads, h, outs[0]), jnp.where(trails, h, outs[1])]
    return jnp.stack(outs)[None]


def solution(mesh):
    in_specs = (
        P(None, "adapter", None),
        P(None, "adapter", None),
        P("adapter"),
        P("segment", None),
        P("segment", None, "adapter"),
        P("segment", "adapter", None, None),
        P("segment", None, None, "adapter"),
    )
    out_specs = P("segment", None, None, "adapter")
    return jax.shard_map(
        on_device, mesh=mesh, in_specs=in_specs, out_specs=out_specs, check_vma=False
    )
```

```python
import jax
import jax.numpy as jnp
from jax import lax
from jax.experimental import pallas as pl
from jax.experimental.pallas import tpu as pltpu
from jax.sharding import PartitionSpec as P

GROUP = 4
CHUNKS = 8
LANES = 128


def lane_group(shape, rank_most):
    return lax.broadcasted_iota(jnp.int32, shape, len(shape) - 1) // rank_most


def spread(value, rank_most):
    step = rank_most
    while step < value.shape[-1]:
        value = value + pltpu.roll(value, step, 1)
        step *= 2
    return value


def fold(rank_most, wide, cols):
    packed = wide.shape[0] // GROUP
    groups = lane_group((packed, cols), rank_most)
    folded = jnp.zeros((packed, cols), jnp.float32)
    for g in range(GROUP):
        folded = jnp.where(groups == g, wide[g * packed : (g + 1) * packed], folded)
    return folded.astype(jnp.bfloat16)


def unfold(rank_most, folded):
    groups = lane_group(folded.shape, rank_most)
    return jnp.concatenate(
        [spread(jnp.where(groups == g, folded, 0.0), rank_most) for g in range(GROUP)], axis=0
    )


def scaling(rank_most, rank, shape):
    place = lax.broadcasted_iota(jnp.int32, shape, 1) % rank_most
    return jnp.where(place.astype(jnp.float32) < rank, 32.0 / rank, 0.0)


def fetches(source, target, sems, axis=0):
    pieces = sems.shape[0]
    size = source.shape[axis] // pieces
    copies = []
    for c in range(pieces):
        part = (slice(None),) * axis + (pl.ds(c * size, size),)
        copies.append(pltpu.make_async_copy(source.at[part], target.at[part], sems.at[c]))
    for copy in copies:
        copy.start()
    return copies


def inverse_rms(squares, width):
    return lax.rsqrt(jnp.sum(squares, axis=-1, keepdims=True) / width + 1e-05)


def table_kernel(rank_most, info_ref, first_ref, second_ref):
    info = info_ref[...].astype(jnp.float32)
    rows = info.shape[0]
    lane = lax.broadcasted_iota(jnp.int32, info.shape, 1)
    ranks = jnp.broadcast_to(info[:, 2:3], info.shape).astype(jnp.bfloat16)
    numbers = lax.broadcasted_iota(jnp.int32, (rows, rows), 1).astype(jnp.float32)
    for micro, ref in enumerate((first_ref, second_ref)):
        ids = info[:, micro : micro + 1]
        onehot = jnp.where(ids == numbers, 1.0, 0.0).astype(jnp.bfloat16)
        rank = jnp.dot(onehot, ranks, preferred_element_type=jnp.float32)
        ref[...] = jnp.where(lane == 0, ids, rank)


def ids_and_rank(table_ref):
    return table_ref[:, 0:1], table_ref[:, 1:2]


def first_kernel(
    rank_most, hidden_ref, base_hbm, maps_hbm, gain_ref, table_ref, owner_ref, order_hbm,
    base_out, sent_out, base_ref, maps_ref, base_sems, maps_sems,
):
    rows = hidden_ref.shape[0]
    width, cols = base_ref.shape
    held = maps_ref.shape[0]
    base_copies = fetches(base_hbm, base_ref, base_sems)
    maps_copies = fetches(maps_hbm, maps_ref, maps_sems, axis=1)
    base = jnp.zeros((rows, cols), jnp.float32)
    shrunk = jnp.zeros((rows, held), jnp.float32)
    squares = jnp.zeros((rows, cols), jnp.float32)
    steps = width // cols
    for j in range(steps):
        if j % (steps // CHUNKS) == 0:
            base_copies[j // (steps // CHUNKS)].wait()
            maps_copies[j // (steps // CHUNKS)].wait()
        part = slice(j * cols, (j + 1) * cols)
        wide = hidden_ref[:, part].astype(jnp.float32)
        squares = squares + wide * wide
        scaled = (wide * gain_ref[:, part]).astype(jnp.bfloat16)
        base = base + jnp.dot(scaled, base_ref[part, :], preferred_element_type=jnp.float32)
        shrunk = shrunk + lax.dot_general(
            scaled, maps_ref[:, part], (((1,), (1,)), ((), ())), preferred_element_type=jnp.float32
        )
    inverse = inverse_rms(squares, width)
    base_out[...] = base * inverse
    groups = lane_group((rows, held), rank_most)
    first = owner_ref[0] * (held // rank_most)
    ids, rank = ids_and_rank(table_ref)
    wanted = ids == (first + groups).astype(jnp.float32)
    factor = scaling(rank_most, rank, (rows, held))
    low = spread(jnp.where(wanted, shrunk * inverse * factor, 0.0), rank_most)
    sent_out[...] = fold(rank_most, jnp.concatenate([low] * (cols // held), axis=1), cols)


def finish(rank_most, h_ref, base, low, ids, expand_ref, out_ref, start=0):
    rows, cols = h_ref.shape
    wanted = ids - lane_group((rows, cols), rank_most).astype(jnp.float32)
    added = jnp.zeros((rows, cols), jnp.float32)
    for j in range((expand_ref.shape[0] - start) // cols):
        picked = jnp.where(wanted == j * GROUP, low, 0.0).astype(jnp.bfloat16)
        part = slice(start + j * cols, start + (j + 1) * cols)
        added = added + jnp.dot(picked, expand_ref[part, :], preferred_element_type=jnp.float32)
    update = (base + added).astype(jnp.bfloat16)
    out_ref[...] = (h_ref[...].astype(jnp.float32) + update.astype(jnp.float32)).astype(
        jnp.bfloat16
    )


def first_after_kernel(
    rank_most, h_ref, got_ref, table_ref, base_ref, expand_ref, out_ref
):
    partial = jnp.zeros(got_ref.shape[1:], jnp.float32)
    for j in range(got_ref.shape[0]):
        partial = partial + got_ref[j].astype(jnp.float32)
    low = unfold(rank_most, partial)
    ids, _ = ids_and_rank(table_ref)
    finish(rank_most, h_ref, base_ref[...], low, ids, expand_ref, out_ref)


def before_kernel(rank_most, h_ref, table_ref, shrink_ref, out_ref):
    rows, cols = h_ref.shape
    h = h_ref[...]
    ids, _ = ids_and_rank(table_ref)
    wanted = ids - lane_group((rows, cols), rank_most).astype(jnp.float32)
    total = jnp.zeros((rows, cols), jnp.float32)
    for j in range(shrink_ref.shape[0] // cols):
        part = lax.dot_general(
            h,
            shrink_ref[j * cols : (j + 1) * cols, :],
            (((1,), (1,)), ((), ())),
            preferred_element_type=jnp.float32,
        )
        total = total + jnp.where(wanted == j * GROUP, part, 0.0)
    out_ref[:rows, :] = h
    out_ref[rows:, :] = fold(rank_most, spread(total, rank_most), cols)


def after_kernel(
    rank_most, h_ref, got_ref, table_ref, wide_hbm, out_ref, wide_ref, sems
):
    rows, cols = h_ref.shape
    copies = fetches(wide_hbm, wide_ref, sems)
    sources = got_ref.shape[0]
    base = jnp.zeros((rows, cols), jnp.float32)
    squares = jnp.zeros((rows, cols), jnp.float32)
    partial = jnp.zeros((rows // GROUP, cols), jnp.float32)
    for j in range(sources):
        if j % (sources // CHUNKS) == 0:
            copies[j // (sources // CHUNKS)].wait()
        block = got_ref[j, :rows, :]
        base = base + jnp.dot(
            block, wide_ref[j * cols : (j + 1) * cols, :], preferred_element_type=jnp.float32
        )
        wide = block.astype(jnp.float32)
        squares = squares + wide * wide
        partial = partial + got_ref[j, rows:, :].astype(jnp.float32)
    inverse = inverse_rms(squares, sources * cols)
    ids, rank = ids_and_rank(table_ref)
    low = unfold(rank_most, partial) * inverse * scaling(rank_most, rank, (rows, cols))
    for copy in copies[CHUNKS:]:
        copy.wait()
    finish(rank_most, h_ref, base * inverse, low, ids, wide_ref, out_ref, sources * cols)


def unused_kernel(rank_most, *refs):
    for ref in refs:
        ref[:16, :] = jnp.zeros((16, ref.shape[1]), ref.dtype)


def on_device(tokens, adapter_ids, ranks, gain, base_weight, shrink_weight, expand_weight):
    micro_count, own_rows, model_width = tokens.shape
    cols = base_weight.shape[2]
    ad_count, _, rank_most = shrink_weight.shape[1:]
    total_adapters = expand_weight.shape[1]
    devices = lax.axis_size("adapter")
    segments = lax.axis_size("segment")
    segment = lax.axis_index("segment")
    owner = lax.axis_index("adapter")
    rows = own_rows * devices
    packed = rows // GROUP
    held = ad_count * rank_most
    all_held = total_adapters * rank_most
    wide_rows = model_width + all_held
    gain_row = gain[0]
    expand = expand_weight[0].reshape(all_held, cols)
    maps = shrink_weight[0].transpose(0, 2, 1).reshape(held, model_width)

    half, full = jnp.bfloat16, jnp.float32
    state = ((rows, cols), half)
    vmem = pl.BlockSpec(memory_space=pltpu.VMEM)
    hbm = pl.BlockSpec(memory_space=pl.ANY)
    smem = pl.BlockSpec(memory_space=pltpu.SMEM)
    fetched = pltpu.SemaphoreType.DMA((CHUNKS,))

    def call(kernel, shapes, *operands, specs=None, scratch=()):
        return pl.pallas_call(
            lambda *refs: kernel(rank_most, *refs),
            out_shape=[jax.ShapeDtypeStruct(*shape) for shape in shapes],
            in_specs=specs or [vmem] * len(operands),
            out_specs=[vmem] * len(shapes),
            scratch_shapes=scratch,
            compiler_params=pltpu.CompilerParams(vmem_limit_bytes=14 * 1024 * 1024),
        )(*operands)

    def exchange(blocks):
        return lax.all_to_all(blocks, "adapter", 0, 0, tiled=True)

    def gather(block):
        return exchange(jnp.broadcast_to(block, (devices,) + block.shape))

    info = jnp.concatenate([adapter_ids[0], adapter_ids[1], ranks[:, None]], axis=1)
    info = jnp.pad(info.astype(half), ((0, 0), (0, LANES - info.shape[1])))

    def tables(info):
        return call(table_kernel, [((rows, LANES), full)] * 2, info)

    def number(value):
        return jnp.asarray(value, jnp.int32).reshape(1)

    def gather_rows(micro):
        block = jnp.concatenate([tokens[micro], info], axis=1)
        return gather(block).reshape(rows, model_width + LANES)

    def first_layer(hidden, table, order):
        base, sent = call(
            first_kernel,
            [((rows, cols), full), ((packed, cols), half)],
            hidden,
            base_weight[0],
            maps,
            gain,
            table,
            number(owner),
            order,
            specs=[vmem, hbm, hbm, vmem, vmem, smem, hbm],
            scratch=[
                pltpu.VMEM((model_width, cols), half),
                pltpu.VMEM((held, model_width), half),
                fetched,
                fetched,
            ],
        )
        own = lax.dynamic_slice_in_dim(hidden, owner * cols, cols, 1)
        return call(
            first_after_kernel,
            [state],
            own,
            gather(sent),
            table,
            base,
            expand,
        )[0]

    def unused():
        return call(unused_kernel, [((all_held, cols), half), ((wide_rows, cols), half)])

    def nothing():
        return jnp.zeros((rows, cols), half)

    def second_gather(h):
        return gather(h).transpose(1, 0, 2).reshape(rows, model_width)

    def open_first(hidden):
        table, next_table = tables(hidden[:, model_width:])
        h = first_layer(hidden, table, hidden)
        shrink, wide = unused()
        return h, table, next_table, shrink, wide

    def open_second(hidden):
        table, next_table = tables(gather(info).reshape(rows, LANES))
        shrink, wide = unused()
        return nothing(), table, next_table, shrink, wide

    def open_other(hidden):
        by_dest = shrink_weight[0].reshape(ad_count, devices, cols, rank_most)
        by_dest = by_dest.transpose(1, 0, 3, 2).reshape(devices, held, cols)
        extra = jnp.pad(info, ((0, 16 - own_rows), (0, cols - LANES)))
        extra = jnp.broadcast_to(extra, (devices, 16, cols))
        got = exchange(jnp.concatenate([by_dest, extra], axis=1))
        base = (base_weight[0].astype(full) * gain_row[:, None]).astype(half)
        wide = jnp.concatenate([base, expand], axis=0)
        table, next_table = tables(got[:, held : held + own_rows, :LANES].reshape(rows, LANES))
        shrink = got[:, :held].reshape(all_held, cols)
        own_gain = lax.dynamic_slice_in_dim(gain_row, owner * cols, cols, 0)
        shrink = (shrink.astype(full) * own_gain[None, :]).astype(half)
        return jnp.zeros((rows, cols), half), table, next_table, shrink, wide

    block_shape = (devices, rows + packed, cols)

    def spread_out(h, table, shrink):
        (sent,) = call(
            before_kernel,
            [((rows + packed, cols), half)],
            h,
            table,
            shrink,
        )
        return gather(sent)

    def project(h, got, table, wide):
        return call(
            after_kernel,
            [state],
            h,
            got,
            table,
            wide,
            specs=[vmem, vmem, vmem, hbm],
            scratch=[
                pltpu.VMEM((wide_rows, cols), half),
                pltpu.SemaphoreType.DMA((wide_rows * CHUNKS // model_width,)),
            ],
        )[0]

    hidden = lax.cond(
        segment == 0,
        lambda: gather_rows(0),
        lambda: lax.cond(
            segment == 2,
            lambda: gather_rows(1),
            lambda: jnp.zeros((rows, model_width + LANES), half),
        ),
    )
    later = lax.ppermute(hidden, "segment", [(2, 0)])
    h, table, next_table, shrink, wide = lax.switch(
        jnp.minimum(segment, 2), (open_first, open_second, open_other), hidden
    )
    outs = [h, h]
    for stage in range(1, segments + 1):
        pairs = [(s, s + 1) for s in (stage - 1, stage - 2) if 0 <= s < segments - 1]
        h = lax.ppermute(h, "segment", pairs)
        leads, trails = segment == stage, segment == stage - 1
        now = lax.optimization_barrier(jnp.where(leads, table, next_table))
        if stage == 1:
            got = lax.cond(
                leads,
                lambda: second_gather(h),
                lambda: jnp.zeros((rows, model_width), half),
            )
            over = lax.ppermute(got[:16, :LANES], "segment", [(1, 0)])
            branch = jnp.where(trails, 2, jnp.where(leads, 1, 0))
            h = lax.switch(
                branch,
                (nothing, lambda: first_layer(got, now, got), lambda: first_layer(later, now, over)),
            )
        elif stage == 2:
            branch = jnp.where(trails, 2, jnp.where(leads, 1, 0))

            def again():
                gathered = second_gather(h)
                return first_layer(gathered, now, gathered)

            h = lax.switch(
                branch,
                (nothing, lambda: project(h, spread_out(h, now, shrink), now, wide), again),
            )
        else:
            h = lax.cond(
                leads | trails,
                lambda: project(h, spread_out(h, now, shrink), now, wide),
                nothing,
            )
        outs = [jnp.where(leads, h, outs[0]), jnp.where(trails, h, outs[1])]
    return jnp.stack(outs)[None]


def solution(mesh):
    in_specs = (
        P(None, "adapter", None),
        P(None, "adapter", None),
        P("adapter"),
        P("segment", None),
        P("segment", None, "adapter"),
        P("segment", "adapter", None, None),
        P("segment", None, None, "adapter"),
    )
    out_specs = P("segment", None, None, "adapter")
    return jax.shard_map(
        on_device, mesh=mesh, in_specs=in_specs, out_specs=out_specs, check_vma=False
    )
```

```python
import jax
import jax.numpy as jnp
from jax import lax
from jax.experimental import pallas as pl
from jax.experimental.pallas import tpu as pltpu
from jax.sharding import PartitionSpec as P

GROUP = 4
CHUNKS = 8
DEPTH = 3
LANES = 128


def lane_group(shape, rank_most):
    return lax.broadcasted_iota(jnp.int32, shape, len(shape) - 1) // rank_most


def spread(value, rank_most):
    step = rank_most
    while step < value.shape[-1]:
        value = value + pltpu.roll(value, step, 1)
        step *= 2
    return value


def fold(rank_most, wide, cols):
    packed = wide.shape[0] // GROUP
    groups = lane_group((packed, cols), rank_most)
    folded = jnp.zeros((packed, cols), jnp.float32)
    for g in range(GROUP):
        folded = jnp.where(groups == g, wide[g * packed : (g + 1) * packed], folded)
    return folded.astype(jnp.bfloat16)


def unfold(rank_most, folded):
    groups = lane_group(folded.shape, rank_most)
    return jnp.concatenate(
        [spread(jnp.where(groups == g, folded, 0.0), rank_most) for g in range(GROUP)], axis=0
    )


def scaling(rank_most, rank, shape):
    place = lax.broadcasted_iota(jnp.int32, shape, 1) % rank_most
    return jnp.where(place.astype(jnp.float32) < rank, 32.0 / rank, 0.0)


def fetches(source, target, sems, axis=0):
    pieces = sems.shape[0]
    size = source.shape[axis] // pieces
    copies = []
    for c in range(pieces):
        part = (slice(None),) * axis + (pl.ds(c * size, size),)
        copies.append(pltpu.make_async_copy(source.at[part], target.at[part], sems.at[c]))
    for copy in copies[:DEPTH]:
        copy.start()

    def wait(c):
        copies[c].wait()
        if c + DEPTH < pieces:
            copies[c + DEPTH].start()

    return wait


def inverse_rms(squares, width):
    return lax.rsqrt(jnp.sum(squares, axis=-1, keepdims=True) / width + 1e-05)


def table_kernel(rank_most, info_ref, first_ref, second_ref):
    info = info_ref[...].astype(jnp.float32)
    rows = info.shape[0]
    lane = lax.broadcasted_iota(jnp.int32, info.shape, 1)
    ranks = jnp.broadcast_to(info[:, 2:3], info.shape).astype(jnp.bfloat16)
    numbers = lax.broadcasted_iota(jnp.int32, (rows, rows), 1).astype(jnp.float32)
    for micro, ref in enumerate((first_ref, second_ref)):
        ids = info[:, micro : micro + 1]
        onehot = jnp.where(ids == numbers, 1.0, 0.0).astype(jnp.bfloat16)
        rank = jnp.dot(onehot, ranks, preferred_element_type=jnp.float32)
        ref[...] = jnp.where(lane == 0, ids, rank)


def ids_and_rank(table_ref):
    return table_ref[:, 0:1], table_ref[:, 1:2]


def first_kernel(
    rank_most, hidden_ref, base_hbm, maps_hbm, gain_ref, table_ref, owner_ref, order_hbm,
    base_out, sent_out, base_ref, maps_ref, base_sems, maps_sems,
):
    rows = hidden_ref.shape[0]
    width, cols = base_ref.shape
    held = maps_ref.shape[0]
    base_wait = fetches(base_hbm, base_ref, base_sems)
    maps_wait = fetches(maps_hbm, maps_ref, maps_sems, axis=1)
    base = jnp.zeros((rows, cols), jnp.float32)
    shrunk = jnp.zeros((rows, held), jnp.float32)
    squares = jnp.zeros((rows, cols), jnp.float32)
    steps = width // cols
    for j in range(steps):
        if j % (steps // CHUNKS) == 0:
            base_wait(j // (steps // CHUNKS))
            maps_wait(j // (steps // CHUNKS))
        part = slice(j * cols, (j + 1) * cols)
        wide = hidden_ref[:, part].astype(jnp.float32)
        squares = squares + wide * wide
        scaled = (wide * gain_ref[:, part]).astype(jnp.bfloat16)
        base = base + jnp.dot(scaled, base_ref[part, :], preferred_element_type=jnp.float32)
        shrunk = shrunk + lax.dot_general(
            scaled, maps_ref[:, part], (((1,), (1,)), ((), ())), preferred_element_type=jnp.float32
        )
    inverse = inverse_rms(squares, width)
    base_out[...] = base * inverse
    groups = lane_group((rows, held), rank_most)
    first = owner_ref[0] * (held // rank_most)
    ids, rank = ids_and_rank(table_ref)
    wanted = ids == (first + groups).astype(jnp.float32)
    factor = scaling(rank_most, rank, (rows, held))
    low = spread(jnp.where(wanted, shrunk * inverse * factor, 0.0), rank_most)
    sent_out[...] = fold(rank_most, jnp.concatenate([low] * (cols // held), axis=1), cols)


def finish(rank_most, h_ref, base, low, ids, expand_ref, out_ref, start=0):
    rows, cols = h_ref.shape
    wanted = ids - lane_group((rows, cols), rank_most).astype(jnp.float32)
    added = jnp.zeros((rows, cols), jnp.float32)
    for j in range((expand_ref.shape[0] - start) // cols):
        picked = jnp.where(wanted == j * GROUP, low, 0.0).astype(jnp.bfloat16)
        part = slice(start + j * cols, start + (j + 1) * cols)
        added = added + jnp.dot(picked, expand_ref[part, :], preferred_element_type=jnp.float32)
    update = (base + added).astype(jnp.bfloat16)
    out_ref[...] = (h_ref[...].astype(jnp.float32) + update.astype(jnp.float32)).astype(
        jnp.bfloat16
    )


def first_after_kernel(
    rank_most, h_ref, got_ref, table_ref, base_ref, expand_ref, out_ref
):
    partial = jnp.zeros(got_ref.shape[1:], jnp.float32)
    for j in range(got_ref.shape[0]):
        partial = partial + got_ref[j].astype(jnp.float32)
    low = unfold(rank_most, partial)
    ids, _ = ids_and_rank(table_ref)
    finish(rank_most, h_ref, base_ref[...], low, ids, expand_ref, out_ref)


def before_kernel(rank_most, h_ref, table_ref, shrink_ref, out_ref):
    rows, cols = h_ref.shape
    h = h_ref[...]
    ids, _ = ids_and_rank(table_ref)
    wanted = ids - lane_group((rows, cols), rank_most).astype(jnp.float32)
    total = jnp.zeros((rows, cols), jnp.float32)
    for j in range(shrink_ref.shape[0] // cols):
        part = lax.dot_general(
            h,
            shrink_ref[j * cols : (j + 1) * cols, :],
            (((1,), (1,)), ((), ())),
            preferred_element_type=jnp.float32,
        )
        total = total + jnp.where(wanted == j * GROUP, part, 0.0)
    out_ref[:rows, :] = h
    out_ref[rows:, :] = fold(rank_most, spread(total, rank_most), cols)


def after_kernel(
    rank_most, h_ref, got_ref, table_ref, wide_hbm, out_ref, wide_ref, sems
):
    rows, cols = h_ref.shape
    wait = fetches(wide_hbm, wide_ref, sems)
    sources = got_ref.shape[0]
    base = jnp.zeros((rows, cols), jnp.float32)
    squares = jnp.zeros((rows, cols), jnp.float32)
    partial = jnp.zeros((rows // GROUP, cols), jnp.float32)
    for j in range(sources):
        if j % (sources // CHUNKS) == 0:
            wait(j // (sources // CHUNKS))
        block = got_ref[j, :rows, :]
        base = base + jnp.dot(
            block, wide_ref[j * cols : (j + 1) * cols, :], preferred_element_type=jnp.float32
        )
        wide = block.astype(jnp.float32)
        squares = squares + wide * wide
        partial = partial + got_ref[j, rows:, :].astype(jnp.float32)
    inverse = inverse_rms(squares, sources * cols)
    ids, rank = ids_and_rank(table_ref)
    low = unfold(rank_most, partial) * inverse * scaling(rank_most, rank, (rows, cols))
    for c in range(CHUNKS, sems.shape[0]):
        wait(c)
    finish(rank_most, h_ref, base * inverse, low, ids, wide_ref, out_ref, sources * cols)


def unused_kernel(rank_most, *refs):
    for ref in refs:
        ref[:16, :] = jnp.zeros((16, ref.shape[1]), ref.dtype)


def on_device(tokens, adapter_ids, ranks, gain, base_weight, shrink_weight, expand_weight):
    micro_count, own_rows, model_width = tokens.shape
    cols = base_weight.shape[2]
    ad_count, _, rank_most = shrink_weight.shape[1:]
    total_adapters = expand_weight.shape[1]
    devices = lax.axis_size("adapter")
    segments = lax.axis_size("segment")
    segment = lax.axis_index("segment")
    owner = lax.axis_index("adapter")
    rows = own_rows * devices
    packed = rows // GROUP
    held = ad_count * rank_most
    all_held = total_adapters * rank_most
    wide_rows = model_width + all_held
    gain_row = gain[0]
    expand = expand_weight[0].reshape(all_held, cols)
    maps = shrink_weight[0].transpose(0, 2, 1).reshape(held, model_width)

    half, full = jnp.bfloat16, jnp.float32
    state = ((rows, cols), half)
    vmem = pl.BlockSpec(memory_space=pltpu.VMEM)
    hbm = pl.BlockSpec(memory_space=pl.ANY)
    smem = pl.BlockSpec(memory_space=pltpu.SMEM)
    fetched = pltpu.SemaphoreType.DMA((CHUNKS,))

    def call(kernel, shapes, *operands, specs=None, scratch=()):
        return pl.pallas_call(
            lambda *refs: kernel(rank_most, *refs),
            out_shape=[jax.ShapeDtypeStruct(*shape) for shape in shapes],
            in_specs=specs or [vmem] * len(operands),
            out_specs=[vmem] * len(shapes),
            scratch_shapes=scratch,
            compiler_params=pltpu.CompilerParams(vmem_limit_bytes=14 * 1024 * 1024),
        )(*operands)

    def exchange(blocks):
        return lax.all_to_all(blocks, "adapter", 0, 0, tiled=True)

    def gather(block):
        return exchange(jnp.broadcast_to(block, (devices,) + block.shape))

    info = jnp.concatenate([adapter_ids[0], adapter_ids[1], ranks[:, None]], axis=1)
    info = jnp.pad(info.astype(half), ((0, 0), (0, LANES - info.shape[1])))

    def tables(info):
        return call(table_kernel, [((rows, LANES), full)] * 2, info)

    def number(value):
        return jnp.asarray(value, jnp.int32).reshape(1)

    def gather_rows(micro):
        block = jnp.concatenate([tokens[micro], info], axis=1)
        return gather(block).reshape(rows, model_width + LANES)

    def first_layer(hidden, table, order):
        base, sent = call(
            first_kernel,
            [((rows, cols), full), ((packed, cols), half)],
            hidden,
            base_weight[0],
            maps,
            gain,
            table,
            number(owner),
            order,
            specs=[vmem, hbm, hbm, vmem, vmem, smem, hbm],
            scratch=[
                pltpu.VMEM((model_width, cols), half),
                pltpu.VMEM((held, model_width), half),
                fetched,
                fetched,
            ],
        )
        own = lax.dynamic_slice_in_dim(hidden, owner * cols, cols, 1)
        return call(
            first_after_kernel,
            [state],
            own,
            gather(sent),
            table,
            base,
            expand,
        )[0]

    def open_first(hidden):
        table, next_table = tables(hidden[:, model_width:])
        h = first_layer(hidden, table, hidden)
        shrink, wide = call(
            unused_kernel, [((all_held, cols), half), ((wide_rows, cols), half)]
        )
        return h, table, next_table, shrink, wide

    def open_other(hidden):
        by_dest = shrink_weight[0].reshape(ad_count, devices, cols, rank_most)
        by_dest = by_dest.transpose(1, 0, 3, 2).reshape(devices, held, cols)
        extra = jnp.pad(info, ((0, 16 - own_rows), (0, cols - LANES)))
        extra = jnp.broadcast_to(extra, (devices, 16, cols))
        got = exchange(jnp.concatenate([by_dest, extra], axis=1))
        base = (base_weight[0].astype(full) * gain_row[:, None]).astype(half)
        wide = jnp.concatenate([base, expand], axis=0)
        table, next_table = tables(got[:, held : held + own_rows, :LANES].reshape(rows, LANES))
        shrink = got[:, :held].reshape(all_held, cols)
        own_gain = lax.dynamic_slice_in_dim(gain_row, owner * cols, cols, 0)
        shrink = (shrink.astype(full) * own_gain[None, :]).astype(half)
        return jnp.zeros((rows, cols), half), table, next_table, shrink, wide

    block_shape = (devices, rows + packed, cols)

    def spread_out(h, table, shrink):
        (sent,) = call(
            before_kernel,
            [((rows + packed, cols), half)],
            h,
            table,
            shrink,
        )
        return gather(sent)

    def project(h, got, table, wide):
        return call(
            after_kernel,
            [state],
            h,
            got,
            table,
            wide,
            specs=[vmem, vmem, vmem, hbm],
            scratch=[
                pltpu.VMEM((wide_rows, cols), half),
                pltpu.SemaphoreType.DMA((wide_rows * CHUNKS // model_width,)),
            ],
        )[0]

    def nothing():
        return jnp.zeros((rows, cols), half)

    hidden = lax.cond(
        segment == 0,
        lambda: gather_rows(0),
        lambda: lax.cond(
            segment == 2,
            lambda: gather_rows(1),
            lambda: jnp.zeros((rows, model_width + LANES), half),
        ),
    )
    later = lax.ppermute(hidden, "segment", [(2, 0)])
    h, table, next_table, shrink, wide = lax.cond(segment == 0, open_first, open_other, hidden)
    outs = [h, h]
    for stage in range(1, segments + 1):
        pairs = [(s, s + 1) for s in (stage - 1, stage - 2) if 0 <= s < segments - 1]
        h = lax.ppermute(h, "segment", pairs)
        leads, trails = segment == stage, segment == stage - 1
        now = lax.optimization_barrier(jnp.where(leads, table, next_table))
        if stage == 1:
            got = lax.cond(
                leads,
                lambda: spread_out(h, now, shrink),
                lambda: jnp.zeros(block_shape, half),
            )
            over = lax.ppermute(got[0, :16, :LANES], "segment", [(1, 0)])
            branch = jnp.where(trails, 2, jnp.where(leads, 1, 0))
            h = lax.switch(
                branch,
                (nothing, lambda: project(h, got, now, wide), lambda: first_layer(later, now, over)),
            )
        else:
            h = lax.cond(
                leads | trails,
                lambda: project(h, spread_out(h, now, shrink), now, wide),
                nothing,
            )
        outs = [jnp.where(leads, h, outs[0]), jnp.where(trails, h, outs[1])]
    return jnp.stack(outs)[None]


def solution(mesh):
    in_specs = (
        P(None, "adapter", None),
        P(None, "adapter", None),
        P("adapter"),
        P("segment", None),
        P("segment", None, "adapter"),
        P("segment", "adapter", None, None),
        P("segment", None, None, "adapter"),
    )
    out_specs = P("segment", None, None, "adapter")
    return jax.shard_map(
        on_device, mesh=mesh, in_specs=in_specs, out_specs=out_specs, check_vma=False
    )
```

```python
import jax
import jax.numpy as jnp
from jax import lax
from jax.experimental import pallas as pl
from jax.experimental.pallas import tpu as pltpu
from jax.sharding import PartitionSpec as P

GROUP = 4
CHUNKS = 16
LANES = 128


def lane_group(shape, rank_most):
    return lax.broadcasted_iota(jnp.int32, shape, len(shape) - 1) // rank_most


def spread(value, rank_most):
    step = rank_most
    while step < value.shape[-1]:
        value = value + pltpu.roll(value, step, 1)
        step *= 2
    return value


def fold(rank_most, wide, cols):
    packed = wide.shape[0] // GROUP
    groups = lane_group((packed, cols), rank_most)
    folded = jnp.zeros((packed, cols), jnp.float32)
    for g in range(GROUP):
        folded = jnp.where(groups == g, wide[g * packed : (g + 1) * packed], folded)
    return folded.astype(jnp.bfloat16)


def unfold(rank_most, folded):
    groups = lane_group(folded.shape, rank_most)
    return jnp.concatenate(
        [spread(jnp.where(groups == g, folded, 0.0), rank_most) for g in range(GROUP)], axis=0
    )


def scaling(rank_most, rank, shape):
    place = lax.broadcasted_iota(jnp.int32, shape, 1) % rank_most
    return jnp.where(place.astype(jnp.float32) < rank, 32.0 / rank, 0.0)


def fetches(source, target, sems, axis=0):
    pieces = sems.shape[0]
    size = source.shape[axis] // pieces
    copies = []
    for c in range(pieces):
        part = (slice(None),) * axis + (pl.ds(c * size, size),)
        copies.append(pltpu.make_async_copy(source.at[part], target.at[part], sems.at[c]))
    for copy in copies:
        copy.start()
    return copies


def inverse_rms(squares, width):
    return lax.rsqrt(jnp.sum(squares, axis=-1, keepdims=True) / width + 1e-05)


def table_kernel(rank_most, info_ref, first_ref, second_ref):
    info = info_ref[...].astype(jnp.float32)
    rows = info.shape[0]
    lane = lax.broadcasted_iota(jnp.int32, info.shape, 1)
    ranks = jnp.broadcast_to(info[:, 2:3], info.shape).astype(jnp.bfloat16)
    numbers = lax.broadcasted_iota(jnp.int32, (rows, rows), 1).astype(jnp.float32)
    for micro, ref in enumerate((first_ref, second_ref)):
        ids = info[:, micro : micro + 1]
        onehot = jnp.where(ids == numbers, 1.0, 0.0).astype(jnp.bfloat16)
        rank = jnp.dot(onehot, ranks, preferred_element_type=jnp.float32)
        ref[...] = jnp.where(lane == 0, ids, rank)


def ids_and_rank(table_ref):
    return table_ref[:, 0:1], table_ref[:, 1:2]


def first_kernel(
    rank_most, hidden_ref, base_hbm, maps_hbm, gain_ref, table_ref, owner_ref, order_hbm,
    base_out, sent_out, base_ref, maps_ref, base_sems, maps_sems,
):
    rows = hidden_ref.shape[0]
    width, cols = base_ref.shape
    held = maps_ref.shape[0]
    base_copies = fetches(base_hbm, base_ref, base_sems)
    maps_copies = fetches(maps_hbm, maps_ref, maps_sems, axis=1)
    base = jnp.zeros((rows, cols), jnp.float32)
    shrunk = jnp.zeros((rows, held), jnp.float32)
    squares = jnp.zeros((rows, cols), jnp.float32)
    steps = width // cols
    for j in range(steps):
        if j % (steps // CHUNKS) == 0:
            base_copies[j // (steps // CHUNKS)].wait()
            maps_copies[j // (steps // CHUNKS)].wait()
        part = slice(j * cols, (j + 1) * cols)
        wide = hidden_ref[:, part].astype(jnp.float32)
        squares = squares + wide * wide
        scaled = (wide * gain_ref[:, part]).astype(jnp.bfloat16)
        base = base + jnp.dot(scaled, base_ref[part, :], preferred_element_type=jnp.float32)
        shrunk = shrunk + lax.dot_general(
            scaled, maps_ref[:, part], (((1,), (1,)), ((), ())), preferred_element_type=jnp.float32
        )
    inverse = inverse_rms(squares, width)
    base_out[...] = base * inverse
    groups = lane_group((rows, held), rank_most)
    first = owner_ref[0] * (held // rank_most)
    ids, rank = ids_and_rank(table_ref)
    wanted = ids == (first + groups).astype(jnp.float32)
    factor = scaling(rank_most, rank, (rows, held))
    low = spread(jnp.where(wanted, shrunk * inverse * factor, 0.0), rank_most)
    sent_out[...] = fold(rank_most, jnp.concatenate([low] * (cols // held), axis=1), cols)


def finish(rank_most, h_ref, base, low, ids, expand_ref, out_ref, start=0):
    rows, cols = h_ref.shape
    wanted = ids - lane_group((rows, cols), rank_most).astype(jnp.float32)
    added = jnp.zeros((rows, cols), jnp.float32)
    for j in range((expand_ref.shape[0] - start) // cols):
        picked = jnp.where(wanted == j * GROUP, low, 0.0).astype(jnp.bfloat16)
        part = slice(start + j * cols, start + (j + 1) * cols)
        added = added + jnp.dot(picked, expand_ref[part, :], preferred_element_type=jnp.float32)
    update = (base + added).astype(jnp.bfloat16)
    out_ref[...] = (h_ref[...].astype(jnp.float32) + update.astype(jnp.float32)).astype(
        jnp.bfloat16
    )


def first_after_kernel(
    rank_most, h_ref, got_ref, table_ref, base_ref, expand_ref, out_ref
):
    partial = jnp.zeros(got_ref.shape[1:], jnp.float32)
    for j in range(got_ref.shape[0]):
        partial = partial + got_ref[j].astype(jnp.float32)
    low = unfold(rank_most, partial)
    ids, _ = ids_and_rank(table_ref)
    finish(rank_most, h_ref, base_ref[...], low, ids, expand_ref, out_ref)


def before_kernel(rank_most, h_ref, table_ref, shrink_ref, out_ref):
    rows, cols = h_ref.shape
    h = h_ref[...]
    ids, _ = ids_and_rank(table_ref)
    wanted = ids - lane_group((rows, cols), rank_most).astype(jnp.float32)
    total = jnp.zeros((rows, cols), jnp.float32)
    for j in range(shrink_ref.shape[0] // cols):
        part = lax.dot_general(
            h,
            shrink_ref[j * cols : (j + 1) * cols, :],
            (((1,), (1,)), ((), ())),
            preferred_element_type=jnp.float32,
        )
        total = total + jnp.where(wanted == j * GROUP, part, 0.0)
    out_ref[:rows, :] = h
    out_ref[rows:, :] = fold(rank_most, spread(total, rank_most), cols)


def after_kernel(
    rank_most, h_ref, got_ref, table_ref, wide_hbm, out_ref, wide_ref, sems
):
    rows, cols = h_ref.shape
    copies = fetches(wide_hbm, wide_ref, sems)
    sources = got_ref.shape[0]
    base = jnp.zeros((rows, cols), jnp.float32)
    squares = jnp.zeros((rows, cols), jnp.float32)
    partial = jnp.zeros((rows // GROUP, cols), jnp.float32)
    for j in range(sources):
        if j % (sources // CHUNKS) == 0:
            copies[j // (sources // CHUNKS)].wait()
        block = got_ref[j, :rows, :]
        base = base + jnp.dot(
            block, wide_ref[j * cols : (j + 1) * cols, :], preferred_element_type=jnp.float32
        )
        wide = block.astype(jnp.float32)
        squares = squares + wide * wide
        partial = partial + got_ref[j, rows:, :].astype(jnp.float32)
    inverse = inverse_rms(squares, sources * cols)
    ids, rank = ids_and_rank(table_ref)
    low = unfold(rank_most, partial) * inverse * scaling(rank_most, rank, (rows, cols))
    for copy in copies[CHUNKS:]:
        copy.wait()
    finish(rank_most, h_ref, base * inverse, low, ids, wide_ref, out_ref, sources * cols)


def unused_kernel(rank_most, *refs):
    for ref in refs:
        ref[:16, :] = jnp.zeros((16, ref.shape[1]), ref.dtype)


def on_device(tokens, adapter_ids, ranks, gain, base_weight, shrink_weight, expand_weight):
    micro_count, own_rows, model_width = tokens.shape
    cols = base_weight.shape[2]
    ad_count, _, rank_most = shrink_weight.shape[1:]
    total_adapters = expand_weight.shape[1]
    devices = lax.axis_size("adapter")
    segments = lax.axis_size("segment")
    segment = lax.axis_index("segment")
    owner = lax.axis_index("adapter")
    rows = own_rows * devices
    packed = rows // GROUP
    held = ad_count * rank_most
    all_held = total_adapters * rank_most
    wide_rows = model_width + all_held
    gain_row = gain[0]
    expand = expand_weight[0].reshape(all_held, cols)
    maps = shrink_weight[0].transpose(0, 2, 1).reshape(held, model_width)

    half, full = jnp.bfloat16, jnp.float32
    state = ((rows, cols), half)
    vmem = pl.BlockSpec(memory_space=pltpu.VMEM)
    hbm = pl.BlockSpec(memory_space=pl.ANY)
    smem = pl.BlockSpec(memory_space=pltpu.SMEM)
    fetched = pltpu.SemaphoreType.DMA((CHUNKS,))

    def call(kernel, shapes, *operands, specs=None, scratch=()):
        return pl.pallas_call(
            lambda *refs: kernel(rank_most, *refs),
            out_shape=[jax.ShapeDtypeStruct(*shape) for shape in shapes],
            in_specs=specs or [vmem] * len(operands),
            out_specs=[vmem] * len(shapes),
            scratch_shapes=scratch,
            compiler_params=pltpu.CompilerParams(vmem_limit_bytes=14 * 1024 * 1024),
        )(*operands)

    def exchange(blocks):
        return lax.all_to_all(blocks, "adapter", 0, 0, tiled=True)

    def gather(block):
        return exchange(jnp.broadcast_to(block, (devices,) + block.shape))

    info = jnp.concatenate([adapter_ids[0], adapter_ids[1], ranks[:, None]], axis=1)
    info = jnp.pad(info.astype(half), ((0, 0), (0, LANES - info.shape[1])))

    def tables(info):
        return call(table_kernel, [((rows, LANES), full)] * 2, info)

    def number(value):
        return jnp.asarray(value, jnp.int32).reshape(1)

    def gather_rows(micro):
        block = jnp.concatenate([tokens[micro], info], axis=1)
        return gather(block).reshape(rows, model_width + LANES)

    def first_layer(hidden, table, order):
        base, sent = call(
            first_kernel,
            [((rows, cols), full), ((packed, cols), half)],
            hidden,
            base_weight[0],
            maps,
            gain,
            table,
            number(owner),
            order,
            specs=[vmem, hbm, hbm, vmem, vmem, smem, hbm],
            scratch=[
                pltpu.VMEM((model_width, cols), half),
                pltpu.VMEM((held, model_width), half),
                fetched,
                fetched,
            ],
        )
        own = lax.dynamic_slice_in_dim(hidden, owner * cols, cols, 1)
        return call(
            first_after_kernel,
            [state],
            own,
            gather(sent),
            table,
            base,
            expand,
        )[0]

    def open_first(hidden):
        table, next_table = tables(hidden[:, model_width:])
        h = first_layer(hidden, table, hidden)
        shrink, wide = call(
            unused_kernel, [((all_held, cols), half), ((wide_rows, cols), half)]
        )
        return h, table, next_table, shrink, wide

    def open_other(hidden):
        by_dest = shrink_weight[0].reshape(ad_count, devices, cols, rank_most)
        by_dest = by_dest.transpose(1, 0, 3, 2).reshape(devices, held, cols)
        extra = jnp.pad(info, ((0, 16 - own_rows), (0, cols - LANES)))
        extra = jnp.broadcast_to(extra, (devices, 16, cols))
        got = exchange(jnp.concatenate([by_dest, extra], axis=1))
        base = (base_weight[0].astype(full) * gain_row[:, None]).astype(half)
        wide = jnp.concatenate([base, expand], axis=0)
        table, next_table = tables(got[:, held : held + own_rows, :LANES].reshape(rows, LANES))
        shrink = got[:, :held].reshape(all_held, cols)
        own_gain = lax.dynamic_slice_in_dim(gain_row, owner * cols, cols, 0)
        shrink = (shrink.astype(full) * own_gain[None, :]).astype(half)
        return jnp.zeros((rows, cols), half), table, next_table, shrink, wide

    block_shape = (devices, rows + packed, cols)

    def spread_out(h, table, shrink):
        (sent,) = call(
            before_kernel,
            [((rows + packed, cols), half)],
            h,
            table,
            shrink,
        )
        return gather(sent)

    def project(h, got, table, wide):
        return call(
            after_kernel,
            [state],
            h,
            got,
            table,
            wide,
            specs=[vmem, vmem, vmem, hbm],
            scratch=[
                pltpu.VMEM((wide_rows, cols), half),
                pltpu.SemaphoreType.DMA((wide_rows * CHUNKS // model_width,)),
            ],
        )[0]

    def nothing():
        return jnp.zeros((rows, cols), half)

    hidden = lax.cond(
        segment == 0,
        lambda: gather_rows(0),
        lambda: lax.cond(
            segment == 2,
            lambda: gather_rows(1),
            lambda: jnp.zeros((rows, model_width + LANES), half),
        ),
    )
    later = lax.ppermute(hidden, "segment", [(2, 0)])
    h, table, next_table, shrink, wide = lax.cond(segment == 0, open_first, open_other, hidden)
    outs = [h, h]
    for stage in range(1, segments + 1):
        pairs = [(s, s + 1) for s in (stage - 1, stage - 2) if 0 <= s < segments - 1]
        h = lax.ppermute(h, "segment", pairs)
        leads, trails = segment == stage, segment == stage - 1
        now = lax.optimization_barrier(jnp.where(leads, table, next_table))
        if stage == 1:
            got = lax.cond(
                leads,
                lambda: spread_out(h, now, shrink),
                lambda: jnp.zeros(block_shape, half),
            )
            over = lax.ppermute(got[0, :16, :LANES], "segment", [(1, 0)])
            branch = jnp.where(trails, 2, jnp.where(leads, 1, 0))
            h = lax.switch(
                branch,
                (nothing, lambda: project(h, got, now, wide), lambda: first_layer(later, now, over)),
            )
        else:
            h = lax.cond(
                leads | trails,
                lambda: project(h, spread_out(h, now, shrink), now, wide),
                nothing,
            )
        outs = [jnp.where(leads, h, outs[0]), jnp.where(trails, h, outs[1])]
    return jnp.stack(outs)[None]


def solution(mesh):
    in_specs = (
        P(None, "adapter", None),
        P(None, "adapter", None),
        P("adapter"),
        P("segment", None),
        P("segment", None, "adapter"),
        P("segment", "adapter", None, None),
        P("segment", None, None, "adapter"),
    )
    out_specs = P("segment", None, None, "adapter")
    return jax.shard_map(
        on_device, mesh=mesh, in_specs=in_specs, out_specs=out_specs, check_vma=False
    )
```
